128 devices in a mesh: dp: 16 (over z, x), heads: 8 (over y, core).
Axes of the slice: x: 4, y: 4, z: 4, core: 2. Of those that a mesh axis runs over, the one named last changes fastest.
Arguments:
- tokens_in: bfloat16 [16384, 2048], P(('dp', 'heads')), may hold values from -6 to 6
- cotangent: bfloat16 [16384, 2048], P(('dp', 'heads')), may hold values from -7.2 to 7.2
- seg_starts: int32 [16, 4], P('dp'), may hold values from 0 to 1023, as said below
- gains: float32 [5120], replicated, may hold values from 0.47 to 2.61
- w_q_down: bfloat16 [2048, 1024], replicated, may hold values from -0.125 to 0.125
- w_key: bfloat16 [2048, 256], replicated, may hold values from -0.125 to 0.125
- w_value: bfloat16 [2048, 256], replicated, may hold values from -0.125 to 0.125
- w_q_up: bfloat16 [1024, 4096], P(None, 'heads'), may hold values from -0.1875 to 0.1875
- w_out: bfloat16 [2048, 4096], P(None, 'heads'), may hold values from -0.625 to 0.625
- w_gate: bfloat16 [2048, 5632], P(None, 'heads'), may hold values from -0.125 to 0.125
- w_up: bfloat16 [2048, 5632], P(None, 'heads'), may hold values from -0.125 to 0.125
- w_down: bfloat16 [2048, 5632], P(None, 'heads'), may hold values from -0.078125 to 0.078125
- mom_gains: float32 [5120], P(('dp', 'heads')), may hold values from -460.8 to 460.8
- mom_q_down: float32 [2048, 1024], P(('dp', 'heads')), may hold values from -368.64 to 368.64
- mom_key: float32 [2048, 256], P(('dp', 'heads')), may hold values from -829.44 to 829.44
- mom_value: float32 [2048, 256], P(('dp', 'heads')), may hold values from -921.6 to 921.6
- mom_q_up: float32 [1024, 4096], P('dp', 'heads'), may hold values from -184.32 to 184.32
- mom_out: float32 [2048, 4096], P('dp', 'heads'), may hold values from -92.16 to 92.16
- mom_gate: float32 [2048, 5632], P('dp', 'heads'), may hold values from -276.48 to 276.48
- mom_up: float32 [2048, 5632], P('dp', 'heads'), may hold values from -322.56 to 322.56
- mom_down: float32 [2048, 5632], P('dp', 'heads'), may hold values from -552.96 to 552.96
Outputs:
- layer_out: bfloat16 [16384, 2048], P(('dp', 'heads'))
- input_grad: float32 [16384, 2048], P(('dp', 'heads'))
- gains_grad: float32 [5120], P(('dp', 'heads'))
- q_down_grad: float32 [2048, 1024], P(('dp', 'heads'))
- key_w_grad: float32 [2048, 256], P(('dp', 'heads'))
- value_w_grad: float32 [2048, 256], P(('dp', 'heads'))
- q_up_grad: float32 [1024, 4096], P('dp', 'heads')
- out_w_grad: float32 [2048, 4096], P('dp', 'heads')
- gate_w_grad: float32 [2048, 5632], P('dp', 'heads')
- up_w_grad: float32 [2048, 5632], P('dp', 'heads')
- down_w_grad: float32 [2048, 5632], P('dp', 'heads')
- gains_mom: float32 [5120], P(('dp', 'heads'))
- q_down_mom: float32 [2048, 1024], P(('dp', 'heads'))
- key_w_mom: float32 [2048, 256], P(('dp', 'heads'))
- value_w_mom: float32 [2048, 256], P(('dp', 'heads'))
- q_up_mom: float32 [1024, 4096], P('dp', 'heads')
- out_w_mom: float32 [2048, 4096], P('dp', 'heads')
- gate_w_mom: float32 [2048, 5632], P('dp', 'heads')
- up_w_mom: float32 [2048, 5632], P('dp', 'heads')
- down_w_mom: float32 [2048, 5632], P('dp', 'heads')
- gains_new: float32 [5120], P(('dp', 'heads'))
- q_down_new: float32 [2048, 1024], P(('dp', 'heads'))
- key_w_new: float32 [2048, 256], P(('dp', 'heads'))
- value_w_new: float32 [2048, 256], P(('dp', 'heads'))
- q_up_new: float32 [1024, 4096], P('dp', 'heads')
- out_w_new: float32 [2048, 4096], P('dp', 'heads')
- gate_w_new: float32 [2048, 5632], P('dp', 'heads')
- up_w_new: float32 [2048, 5632], P('dp', 'heads')
- down_w_new: float32 [2048, 5632], P('dp', 'heads')
The draws below stay inside these ranges and needn't reach their ends.
Inputs may be any that keep to these rules, and one draw needn't show every extreme that they name: `seg_starts`: in each row the entries rise strictly and the first is 0.
All inputs are finite; a program needn't handle non-finite values.
Results may differ from the reference program's by a relative error of at most 0.029.
Values may be sent and summed in bfloat16 or wider, within the bound.
No kernel may reach another device: no remote copies, remote signals or barrier semaphores. Data moves between devices by JAX's collectives and lax.ppermute only.
A program may use at most 192 MiB of HBM per device.

```python
import math
import jax
import jax.numpy as jnp
from jax import lax

D = 2048
LATENT = 1024
HEADS = 16
HEAD_DIM = 256
FF = 5632
TOK_DEV = 128
NS_STEPS = 3
FF_BLOCK = 352
QDIM = 4096
ROW_LEN = 1024
ROWS = 16
TOKENS = 16384
GAINS = 5120


def row_ramp(count, low_end, high_end):
    return low_end + (high_end - low_end) * jnp.arange(count, dtype=jnp.float32) / max(count - 1, 1)


def mixed_noise(key, shape):
    normal_key = jax.random.fold_in(key, 0)
    bell_part = jax.random.truncated_normal(normal_key, -4.0, 4.0, shape, jnp.float32)
    return bell_part


def ramped_rows(key, row_count, col_count, scale, low_end, high_end):
    return scale * row_ramp(row_count, low_end, high_end)[:, None] * mixed_noise(key, (row_count, col_count))


def gain_vector(key, low_end, high_end):
    ramp_all = jnp.concatenate([row_ramp(D, low_end, high_end), row_ramp(LATENT, low_end, high_end), row_ramp(D, low_end, high_end)])
    return ramp_all * (1.0 + 0.025 * mixed_noise(key, (GAINS,)))


def draw_seg_starts(key, part):
    key = jax.random.fold_in(key, 5)
    first_key, second_key, third_key = jax.random.split(key, 3)
    first_start = jax.random.randint(first_key, (ROWS, 1), 1, TOK_DEV)
    second_start = jax.random.randint(second_key, (ROWS, 1), ROW_LEN - TOK_DEV + 1, ROW_LEN - 1)
    third_start = jax.random.randint(third_key, (ROWS, 1), second_start + 1, ROW_LEN)
    zero_start = jnp.zeros((ROWS, 1), jnp.int32)
    return jnp.concatenate([zero_start, first_start, second_start, third_start], axis=1).astype(jnp.int32)


def draw_gains(key, part):
    key = jax.random.fold_in(key, 3)
    return gain_vector(key, 0.6, 1.8)


def draw_cotangent(key, part):
    key = jax.random.fold_in(key, 7)
    return ramped_rows(key, D, TOKENS, 1.0, 0.6, 1.8).T.astype(jnp.bfloat16)


def draw_mom_gains(key, part):
    key = jax.random.fold_in(key, 11)
    return ramped_rows(key, GAINS, 1, 0.5 * TOKENS ** 0.5, 0.6, 1.8)[:, 0]


def draw_mom_q_down(key, part):
    key = jax.random.fold_in(key, 13)
    return ramped_rows(key, D, LATENT, 0.4 * TOKENS ** 0.5, 0.6, 1.8)


def draw_mom_key(key, part):
    key = jax.random.fold_in(key, 17)
    return ramped_rows(key, D, HEAD_DIM, 0.9 * TOKENS ** 0.5, 0.6, 1.8)


def draw_mom_value(key, part):
    key = jax.random.fold_in(key, 19)
    return ramped_rows(key, D, HEAD_DIM, TOKENS ** 0.5, 0.6, 1.8)


def draw_mom_q_up(key, part):
    key = jax.random.fold_in(key, 23)
    return ramped_rows(key, LATENT, QDIM, 0.2 * TOKENS ** 0.5, 0.6, 1.8)


def draw_mom_out(key, part):
    key = jax.random.fold_in(key, 29)
    return ramped_rows(key, D, QDIM, 0.1 * TOKENS ** 0.5, 0.6, 1.8)


def draw_mom_gate(key, part):
    key = jax.random.fold_in(key, 31)
    return ramped_rows(key, D, FF, 0.3 * TOKENS ** 0.5, 0.6, 1.8)


def draw_mom_up(key, part):
    key = jax.random.fold_in(key, 37)
    return ramped_rows(key, D, FF, 0.35 * TOKENS ** 0.5, 0.6, 1.8)


def draw_mom_down(key, part):
    key = jax.random.fold_in(key, 41)
    return ramped_rows(key, D, FF, 0.6 * TOKENS ** 0.5, 0.6, 1.8)


def block_scale(key, extent, cuts, low, largest):
    factor_of, own = 1.0, jax.random.fold_in(key, 6)
    for axis_at, blocks in cuts:
        draws = jnp.exp(jax.random.uniform(jax.random.fold_in(own, axis_at), (blocks,), jnp.float32, low / len(cuts), largest / len(cuts)))
        factor_of = factor_of * jnp.repeat(draws, extent[axis_at] // blocks).reshape([-1 if axis == axis_at else 1 for axis in range(len(extent))])
    return factor_of


def noise(key, extent, deviation, most, pieces=(), held_as=jnp.bfloat16):
    factor_of = block_scale(key, extent, pieces, -0.22, 0.18) if pieces else 1.0
    result = jax.random.normal(key, extent, jnp.float32) * deviation * factor_of
    return jnp.minimum(jnp.maximum(result, -most), most).astype(held_as)


def setup_inputs(seed: int = 0) -> dict:
    arg_keys = jax.random.split(jax.random.key(seed), 22)
    tokens_in = noise(arg_keys[0], (TOKENS, D), 1.0, 6.0, ((0, 128),))
    cotangent = draw_cotangent(jax.random.fold_in(arg_keys[21], 71), 0)
    seg_starts = draw_seg_starts(jax.random.fold_in(arg_keys[21], 71), 0)
    gains = draw_gains(jax.random.fold_in(arg_keys[21], 71), 0)
    w_q_down = noise(arg_keys[4], (D, LATENT), D ** -0.5, 0.125)
    w_key = noise(arg_keys[5], (D, HEAD_DIM), D ** -0.5, 0.125)
    w_value = noise(arg_keys[6], (D, HEAD_DIM), D ** -0.5, 0.125)
    w_q_up = noise(arg_keys[7], (LATENT, QDIM), LATENT ** -0.5, 0.1875, ((1, 8),))
    w_out = noise(arg_keys[8], (D, QDIM), (QDIM * 24 // ROW_LEN) ** -0.5, 0.625, ((1, 8),))
    w_gate = noise(arg_keys[9], (D, FF), D ** -0.5, 0.125, ((1, 8),))
    w_up = noise(arg_keys[10], (D, FF), D ** -0.5, 0.125, ((1, 8),))
    w_down = noise(arg_keys[11], (D, FF), FF ** -0.5, 0.078125, ((1, 8),))
    mom_gains = draw_mom_gains(jax.random.fold_in(arg_keys[21], 71), 0)
    mom_q_down = draw_mom_q_down(jax.random.fold_in(arg_keys[21], 71), 0)
    mom_key = draw_mom_key(jax.random.fold_in(arg_keys[21], 71), 0)
    mom_value = draw_mom_value(jax.random.fold_in(arg_keys[21], 71), 0)
    mom_q_up = draw_mom_q_up(jax.random.fold_in(arg_keys[21], 71), 0)
    mom_out = draw_mom_out(jax.random.fold_in(arg_keys[21], 71), 0)
    mom_gate = draw_mom_gate(jax.random.fold_in(arg_keys[21], 71), 0)
    mom_up = draw_mom_up(jax.random.fold_in(arg_keys[21], 71), 0)
    mom_down = draw_mom_down(jax.random.fold_in(arg_keys[21], 71), 0)
    return {"tokens_in": tokens_in, "cotangent": cotangent, "seg_starts": seg_starts, "gains": gains, "w_q_down": w_q_down, "w_key": w_key, "w_value": w_value, "w_q_up": w_q_up, "w_out": w_out, "w_gate": w_gate, "w_up": w_up, "w_down": w_down, "mom_gains": mom_gains, "mom_q_down": mom_q_down, "mom_key": mom_key, "mom_value": mom_value, "mom_q_up": mom_q_up, "mom_out": mom_out, "mom_gate": mom_gate, "mom_up": mom_up, "mom_down": mom_down}


@jax.custom_vjp
def low(v):
    return lax.optimization_barrier(v.astype(jnp.bfloat16)).astype(jnp.float32)

@jax.custom_vjp
def low_back(v):
    return v

def low_keep(v):
    return (low(v), None)

def low_pass(kept, grad):
    return (grad,)

def back_keep(v):
    return (v, None)

def back_low(kept, grad):
    return (low(grad),)
low.defvjp(low_keep, low_pass)
low_back.defvjp(back_keep, back_low)
highest = lax.Precision.HIGHEST
coef_first = 3.4445
coef_second = -4.775
coef_third = 2.0315
muon_rate = 0.5
gain_rate = 0.004
decay_rate = 0.5

def exact_dot(left, right):
    return jnp.dot(left, right, precision=highest, preferred_element_type=jnp.float32)

def rms_scale(values):
    return lax.rsqrt(lax.optimization_barrier(jnp.mean(values * values, axis=-1, keepdims=True)) + 1e-05)

def segment_info(starts, token_index):
    started = starts[None, :] <= token_index[:, None]
    seg_ids = lax.optimization_barrier(jnp.sum(started.astype(jnp.int32), axis=1))
    seg_begin = lax.optimization_barrier(jnp.max(jnp.where(started, starts[None, :], 0), axis=1))
    return (seg_ids, token_index - seg_begin)

def rotary_tables(positions, head_dim):
    half_dim = head_dim // 2
    frequency = jnp.exp(jnp.arange(half_dim, dtype=jnp.float32) * (-2.0 * math.log(10000.0) / head_dim))
    angles = positions.astype(jnp.float32)[:, None] * frequency[None, :]
    return (jnp.cos(angles), jnp.sin(angles))

def rotate(values, cosine, sine_part):
    half_dim = values.shape[-1] // 2
    first_half = values[..., :half_dim]
    second_half = values[..., half_dim:]
    return jnp.concatenate([first_half * cosine - second_half * sine_part, second_half * cosine + first_half * sine_part], axis=-1)

def row_forward(params, inputs, seg_ids, positions):
    gains, w_q_down, w_key, w_value, w_q_up, w_out, w_gate, w_up, w_down = params
    row_len = inputs.shape[0]
    gain_one = gains[:D]
    gain_latent = gains[D:D + LATENT]
    gain_two = gains[D + LATENT:]
    normed_one = low(inputs * rms_scale(inputs) * gain_one)
    latent_raw = low_back(exact_dot(normed_one, w_q_down))
    latent_normed = low(latent_raw * rms_scale(latent_raw) * gain_latent)
    cosine, sine_part = rotary_tables(positions, HEAD_DIM)
    keys = low(rotate(low_back(exact_dot(normed_one, w_key)), cosine, sine_part))
    values = low(low_back(exact_dot(normed_one, w_value)))
    query_pre = low_back(exact_dot(latent_normed, w_q_up)).reshape(row_len, HEADS, HEAD_DIM)
    queries = low(rotate(query_pre, cosine[:, None, :], sine_part[:, None, :]))
    block_len = min(512, row_len)
    block_count = row_len // block_len
    score_scale = HEAD_DIM ** (-0.5)
    key_at = jnp.arange(row_len, dtype=jnp.int32)

    def attend_block(query_block, block_index):
        first_row = (block_index * block_len).astype(jnp.int32)
        query_at = first_row + jnp.arange(block_len, dtype=jnp.int32)
        query_ids = lax.dynamic_slice_in_dim(seg_ids, first_row, block_len)
        allowed = (query_ids[:, None] == seg_ids[None, :]) & (key_at[None, :] <= query_at[:, None])
        scores = low_back(jnp.einsum('qhd,kd->hqk', query_block, keys, precision=highest) * score_scale)
        scores = jnp.where(allowed[None], scores, -1e+30)
        row_max = lax.optimization_barrier(jnp.max(scores, axis=-1, keepdims=True))
        exponent = jnp.exp(scores - row_max)
        attn_probs = low(exponent / lax.optimization_barrier(jnp.sum(exponent, axis=-1, keepdims=True)))
        return jnp.einsum('hqk,kd->qhd', attn_probs, values, precision=highest)
    checked = jax.checkpoint(attend_block)

    def map_block(block_args):
        return checked(block_args[0], block_args[1])
    attended = lax.map(map_block, (queries.reshape(block_count, block_len, HEADS, HEAD_DIM), jnp.arange(block_count, dtype=jnp.int32)))
    attended = low(low_back(attended.reshape(row_len, HEADS * HEAD_DIM)))
    hidden_one = inputs + low_back(exact_dot(attended, w_out.T))
    normed_two = low(hidden_one * rms_scale(hidden_one) * gain_two)
    gate = low_back(exact_dot(normed_two, w_gate))
    up_part = low_back(exact_dot(normed_two, w_up))
    middle = low(jax.nn.silu(gate) * up_part)
    return hidden_one + exact_dot(middle, w_down.T)

def orthogonalize(blocks):
    norms = jnp.sqrt(lax.optimization_barrier(jnp.sum(blocks * blocks, axis=(1, 2), keepdims=True)))
    iterate = blocks / (norms + 1e-07)
    for step_index in range(NS_STEPS):
        gram_matrix = jnp.einsum('brc,brd->bcd', iterate, iterate, precision=highest)
        first_term = jnp.einsum('brc,bcd->brd', iterate, gram_matrix, precision=highest)
        second_term = jnp.einsum('brc,bcd->brd', first_term, gram_matrix, precision=highest)
        iterate = coef_first * iterate + coef_second * first_term + coef_third * second_term
    return iterate

def split_columns(matrix, block_cols):
    row_count = matrix.shape[0]
    return matrix.reshape(row_count, matrix.shape[1] // block_cols, block_cols).transpose(1, 0, 2)

def join_columns(blocks):
    return blocks.transpose(1, 0, 2).reshape(blocks.shape[1], blocks.shape[0] * blocks.shape[2])

def muon_update(weight, momentum, block_cols):
    ortho = join_columns(orthogonalize(split_columns(momentum, block_cols)))
    return weight - muon_rate * math.sqrt(weight.shape[0] / block_cols) * ortho

def reference(tokens_in, cotangent, seg_starts, gains, w_q_down, w_key, w_value, w_q_up, w_out, w_gate, w_up, w_down, mom_gains, mom_q_down, mom_key, mom_value, mom_q_up, mom_out, mom_gate, mom_up, mom_down):
    params = (gains.astype(jnp.float32), w_q_down.astype(jnp.float32), w_key.astype(jnp.float32), w_value.astype(jnp.float32), w_q_up.astype(jnp.float32), w_out.astype(jnp.float32), w_gate.astype(jnp.float32), w_up.astype(jnp.float32), w_down.astype(jnp.float32))
    inputs_all = tokens_in.astype(jnp.float32).reshape(ROWS, ROW_LEN, D)
    back_all = cotangent.astype(jnp.float32).reshape(ROWS, ROW_LEN, D)
    token_index = jnp.arange(ROW_LEN, dtype=jnp.int32)

    def row_step(totals, row_args):
        row_inputs, row_back, row_starts = row_args
        seg_ids, positions = segment_info(row_starts, token_index)

        def forward_fn(param_tuple, inputs):
            return row_forward(param_tuple, inputs, seg_ids, positions)
        outputs, pullback = jax.vjp(forward_fn, params, row_inputs)
        param_grads, input_grads = pullback(row_back)
        totals = jax.tree.map(jnp.add, totals, param_grads)
        return (totals, (outputs.astype(jnp.bfloat16), input_grads))
    zero_grads = jax.tree.map(jnp.zeros_like, params)
    grads, (layer_rows, input_rows) = lax.scan(row_step, zero_grads, (inputs_all, back_all, seg_starts))
    gains_grad, q_down_grad, key_w_grad, value_w_grad, q_up_grad, out_w_grad, gate_w_grad, up_w_grad, down_w_grad = grads
    gains_mom = decay_rate * mom_gains + gains_grad
    q_down_mom = decay_rate * mom_q_down + q_down_grad
    key_w_mom = decay_rate * mom_key + key_w_grad
    value_w_mom = decay_rate * mom_value + value_w_grad
    q_up_mom = decay_rate * mom_q_up + q_up_grad
    out_w_mom = decay_rate * mom_out + out_w_grad
    gate_w_mom = decay_rate * mom_gate + gate_w_grad
    up_w_mom = decay_rate * mom_up + up_w_grad
    down_w_mom = decay_rate * mom_down + down_w_grad
    gains_new = params[0] - gain_rate * gains_mom
    q_down_new = muon_update(params[1], q_down_mom, LATENT)
    key_w_new = muon_update(params[2], key_w_mom, HEAD_DIM)
    value_w_new = muon_update(params[3], value_w_mom, HEAD_DIM)
    q_up_new = muon_update(params[4], q_up_mom, HEAD_DIM)
    out_w_new = muon_update(params[5], out_w_mom, HEAD_DIM)
    gate_w_new = muon_update(params[6], gate_w_mom, FF_BLOCK)
    up_w_new = muon_update(params[7], up_w_mom, FF_BLOCK)
    down_w_new = muon_update(params[8], down_w_mom, FF_BLOCK)
    layer_out = layer_rows.reshape(TOKENS, D)
    input_grad = input_rows.reshape(TOKENS, D)
    return (layer_out, input_grad, gains_grad, q_down_grad, key_w_grad, value_w_grad, q_up_grad, out_w_grad, gate_w_grad, up_w_grad, down_w_grad, gains_mom, q_down_mom, key_w_mom, value_w_mom, q_up_mom, out_w_mom, gate_w_mom, up_w_mom, down_w_mom, gains_new, q_down_new, key_w_new, value_w_new, q_up_new, out_w_new, gate_w_new, up_w_new, down_w_new)
```

```python
import math

import jax
import jax.numpy as jnp
from jax import lax
from jax.sharding import PartitionSpec as P

NS_STEPS = 3
FF_BLOCK = 352


coef_first = 3.4445
coef_second = -4.775
coef_third = 2.0315
muon_rate = 0.5
gain_rate = 0.004
decay_rate = 0.5


def matmul(left, right):
    return jnp.dot(left, right, preferred_element_type=jnp.float32)


def matmul_nt(left, right):
    return lax.dot_general(
        left, right, (((1,), (1,)), ((), ())), preferred_element_type=jnp.float32
    )


def matmul_tn(left, right):
    return lax.dot_general(
        left, right, (((0,), (0,)), ((), ())), preferred_element_type=jnp.float32
    )


def rms_scale(values):
    return lax.rsqrt(jnp.mean(values * values, axis=-1, keepdims=True) + 1e-05)


def norm_back(values, scale, gain, grad_out):
    weighted = gain * grad_out
    inner = jnp.mean(values * weighted, axis=-1, keepdims=True)
    grad_in = scale * weighted - values * (scale * scale * scale) * inner
    gain_grad = jnp.sum(grad_out * values * scale, axis=0)
    return (grad_in, gain_grad)


def segment_info(starts, token_index):
    started = starts[None, :] <= token_index[:, None]
    seg_ids = jnp.sum(started.astype(jnp.int32), axis=1)
    seg_begin = jnp.max(jnp.where(started, starts[None, :], 0), axis=1)
    return (seg_ids, token_index - seg_begin)


def rotary_tables(positions, head_dim):
    half_dim = head_dim // 2
    frequency = jnp.exp(
        jnp.arange(half_dim, dtype=jnp.float32) * (-2.0 * math.log(10000.0) / head_dim)
    )
    angles = positions.astype(jnp.float32)[:, None] * frequency[None, :]
    return (jnp.cos(angles), jnp.sin(angles))


def rotate(values, cosine, sine_part):
    half_dim = values.shape[-1] // 2
    first_half = values[..., :half_dim]
    second_half = values[..., half_dim:]
    return jnp.concatenate(
        [
            first_half * cosine - second_half * sine_part,
            second_half * cosine + first_half * sine_part,
        ],
        axis=-1,
    )


def rotate_back(grads, cosine, sine_part):
    half_dim = grads.shape[-1] // 2
    first_half = grads[..., :half_dim]
    second_half = grads[..., half_dim:]
    return jnp.concatenate(
        [
            first_half * cosine + second_half * sine_part,
            second_half * cosine - first_half * sine_part,
        ],
        axis=-1,
    )


def block_mask(row_ids, first_row, end_row):
    query_ids = row_ids[first_row:end_row]
    key_ids = row_ids[:end_row]
    query_at = jnp.arange(first_row, end_row, dtype=jnp.int32)[:, None]
    key_at = jnp.arange(end_row, dtype=jnp.int32)[None, :]
    return (query_ids[:, None] == key_ids[None, :]) & (key_at <= query_at)


def gram_of(blocks):
    low = blocks.astype(jnp.bfloat16)
    return jnp.einsum("brc,brd->bcd", low, low, preferred_element_type=jnp.float32)


def times(left, right):
    return jnp.einsum(
        "brc,bcd->brd",
        left.astype(jnp.bfloat16),
        right.astype(jnp.bfloat16),
        preferred_element_type=jnp.float32,
    )


def orthogonal(blocks, gram_sums):
    diagonal = jnp.eye(gram_sums.shape[-1], dtype=jnp.bool_)
    trace_sum = jnp.sum(jnp.where(diagonal, gram_sums, 0.0), axis=(1, 2))
    factor = 1.0 / (jnp.sqrt(trace_sum) + 1e-07)
    iterate = blocks * factor[:, None, None]
    gram = gram_sums * (factor * factor)[:, None, None]
    for step_index in range(NS_STEPS):
        first_term = times(iterate, gram)
        second_term = times(first_term, gram)
        iterate = coef_first * iterate + coef_second * first_term + coef_third * second_term
        if step_index + 1 < NS_STEPS:
            change = coef_second * gram + coef_third * times(gram, gram)
            once = times(gram, change)
            twice = times(once, change)
            gram = (coef_first * coef_first) * gram + (2.0 * coef_first) * once + twice
    return iterate


def split_columns(matrix, block_cols):
    row_count = matrix.shape[0]
    return matrix.reshape(row_count, matrix.shape[1] // block_cols, block_cols).transpose(1, 0, 2)


def join_columns(blocks):
    return blocks.transpose(1, 0, 2).reshape(blocks.shape[1], blocks.shape[0] * blocks.shape[2])


def own_rows(weight, count, rank):
    share_rows = weight.shape[0] // count
    return lax.dynamic_slice_in_dim(weight, rank * share_rows, share_rows, 0).astype(jnp.float32)


def on_device(
    tokens_in,
    cotangent,
    seg_starts,
    gains,
    w_q_down,
    w_key,
    w_value,
    w_q_up,
    w_out,
    w_gate,
    w_up,
    w_down,
    mom_gains,
    mom_q_down,
    mom_key,
    mom_value,
    mom_q_up,
    mom_out,
    mom_gate,
    mom_up,
    mom_down,
):
    heads_count = lax.axis_size("heads")
    heads_rank = lax.axis_index("heads")
    dp_count = lax.axis_size("dp")
    dp_rank = lax.axis_index("dp")
    all_rank = lax.axis_index(("dp", "heads"))
    all_count = dp_count * heads_count
    local_rows = tokens_in.shape[0]
    row_len = local_rows * heads_count
    model_width = tokens_in.shape[1]
    latent_width = w_q_down.shape[1]
    head_dim = w_key.shape[1]
    local_heads = w_q_up.shape[1] // head_dim
    score_scale = head_dim ** (-0.5)
    block_len = min(512, row_len)
    block_count = row_len // block_len
    starts = seg_starts[0]
    whole_index = jnp.arange(row_len, dtype=jnp.int32)
    own_index = heads_rank * local_rows + jnp.arange(local_rows, dtype=jnp.int32)
    gain_one = gains[:model_width]
    gain_latent = gains[model_width : model_width + latent_width]
    gain_two = gains[model_width + latent_width :]
    inputs = tokens_in.astype(jnp.float32)
    scale_one = rms_scale(inputs)
    normed_one = (inputs * scale_one * gain_one).astype(jnp.bfloat16)
    latent_raw = matmul(normed_one, w_q_down)
    scale_latent = rms_scale(latent_raw)
    latent_normed = (latent_raw * scale_latent * gain_latent).astype(jnp.bfloat16)
    own_pos = segment_info(starts, own_index)[1]
    own_cos, own_sin = rotary_tables(own_pos, head_dim)
    key_local = rotate(matmul(normed_one, w_key), own_cos, own_sin).astype(jnp.bfloat16)
    value_local = matmul(normed_one, w_value).astype(jnp.bfloat16)
    packed_rows = lax.all_gather(
        jnp.concatenate([latent_normed, key_local, value_local], axis=1), "heads", axis=0, tiled=True
    )
    latent_rows = packed_rows[:, :latent_width]
    key_rows = packed_rows[:, latent_width : latent_width + head_dim]
    value_rows = packed_rows[:, latent_width + head_dim :]
    share_rows = model_width // all_count
    normed_parts = lax.all_to_all(
        normed_one.reshape(local_rows, dp_count, heads_count, share_rows)
        .transpose(2, 0, 1, 3)
        .reshape(heads_count * local_rows, dp_count * share_rows),
        "heads",
        split_axis=0,
        concat_axis=0,
        tiled=True,
    )
    row_ids, row_pos = segment_info(starts, whole_index)
    row_cos, row_sin = rotary_tables(row_pos, head_dim)
    query_pre = matmul(latent_rows, w_q_up).reshape(row_len, local_heads, head_dim)
    query_rows = rotate(query_pre, row_cos[:, None, :], row_sin[:, None, :]).astype(jnp.bfloat16)
    attended_blocks = []
    lse_blocks = []
    for block_index in range(block_count):
        first_row = block_index * block_len
        end_row = first_row + block_len
        allowed = block_mask(row_ids, first_row, end_row)
        scores = (
            jnp.einsum(
                "qhd,kd->hqk",
                query_rows[first_row:end_row],
                key_rows[:end_row],
                preferred_element_type=jnp.float32,
            )
            * score_scale
        )
        scores = jnp.where(allowed[None], scores, -1e30)
        row_max = jnp.max(scores, axis=-1, keepdims=True)
        exponent = jnp.exp(scores - row_max)
        row_total = jnp.sum(exponent, axis=-1, keepdims=True)
        attn_probs = (exponent / row_total).astype(jnp.bfloat16)
        lse_blocks.append(row_max + jnp.log(row_total))
        attended_blocks.append(
            jnp.einsum(
                "hqk,kd->qhd", attn_probs, value_rows[:end_row], preferred_element_type=jnp.float32
            )
        )
    attended = (
        jnp.concatenate(attended_blocks, axis=0)
        .astype(jnp.bfloat16)
        .reshape(row_len, local_heads * head_dim)
    )
    attn_mixed = lax.psum_scatter(
        matmul_nt(attended, w_out).astype(jnp.bfloat16), "heads", scatter_dimension=0, tiled=True
    ).astype(jnp.float32)
    hidden_one = inputs + attn_mixed
    scale_two = rms_scale(hidden_one)
    normed_two = (hidden_one * scale_two * gain_two).astype(jnp.bfloat16)
    ffn_input = lax.all_gather(normed_two, "heads", axis=0, tiled=True)
    gate_raw = matmul(ffn_input, w_gate)
    up_raw = matmul(ffn_input, w_up)
    sigmoid_gate = jax.nn.sigmoid(gate_raw)
    activated = gate_raw * sigmoid_gate
    hidden_mid = (activated * up_raw).astype(jnp.bfloat16)
    ffn_mixed = lax.psum_scatter(
        matmul_nt(hidden_mid, w_down).astype(jnp.bfloat16), "heads", scatter_dimension=0, tiled=True
    ).astype(jnp.float32)
    layer_out = (hidden_one + ffn_mixed).astype(jnp.bfloat16)
    grad_rows = lax.all_gather(cotangent, "heads", axis=0, tiled=True)
    mid_back = matmul(grad_rows, w_down)
    down_w_part = matmul_tn(grad_rows, hidden_mid)
    gate_back = (mid_back * up_raw * sigmoid_gate * (1.0 + gate_raw * (1.0 - sigmoid_gate))).astype(
        jnp.bfloat16
    )
    up_back = (mid_back * activated).astype(jnp.bfloat16)
    gate_up_part = matmul_tn(ffn_input, jnp.concatenate([gate_back, up_back], axis=1))
    normed_two_back = lax.psum_scatter(
        (matmul_nt(gate_back, w_gate) + matmul_nt(up_back, w_up)).astype(jnp.bfloat16),
        "heads",
        scatter_dimension=0,
        tiled=True,
    ).astype(jnp.float32)
    hidden_part, gain_two_grad = norm_back(hidden_one, scale_two, gain_two, normed_two_back)
    hidden_back = cotangent.astype(jnp.float32) + hidden_part
    hidden_rows = lax.all_gather(hidden_back.astype(jnp.bfloat16), "heads", axis=0, tiled=True)
    attended_back = matmul(hidden_rows, w_out).astype(jnp.bfloat16)
    out_w_part = matmul_tn(hidden_rows, attended)
    attended_back = attended_back.reshape(row_len, local_heads, head_dim)
    key_back = jnp.zeros((row_len, head_dim), jnp.float32)
    value_back = jnp.zeros((row_len, head_dim), jnp.float32)
    query_back_blocks = []
    for block_index in range(block_count):
        first_row = block_index * block_len
        end_row = first_row + block_len
        query_block = query_rows[first_row:end_row]
        keys_seen = key_rows[:end_row]
        values_seen = value_rows[:end_row]
        back_block = attended_back[first_row:end_row]
        allowed = block_mask(row_ids, first_row, end_row)
        scores = (
            jnp.einsum("qhd,kd->hqk", query_block, keys_seen, preferred_element_type=jnp.float32)
            * score_scale
        )
        scores = jnp.where(allowed[None], scores, -1e30)
        attn_probs = jnp.exp(scores - lse_blocks[block_index])
        probs_back = jnp.einsum(
            "qhd,kd->hqk", back_block, values_seen, preferred_element_type=jnp.float32
        )
        inner = jnp.sum(attn_probs * probs_back, axis=-1, keepdims=True)
        score_back = (attn_probs * (probs_back - inner)).astype(jnp.bfloat16)
        query_back_blocks.append(
            jnp.einsum("hqk,kd->qhd", score_back, keys_seen, preferred_element_type=jnp.float32)
            * score_scale
        )
        key_back = key_back.at[:end_row].add(
            jnp.einsum("hqk,qhd->kd", score_back, query_block, preferred_element_type=jnp.float32)
            * score_scale
        )
        value_back = value_back.at[:end_row].add(
            jnp.einsum(
                "hqk,qhd->kd",
                attn_probs.astype(jnp.bfloat16),
                back_block,
                preferred_element_type=jnp.float32,
            )
        )
    query_back = jnp.concatenate(query_back_blocks, axis=0)
    query_back = (
        rotate_back(query_back, row_cos[:, None, :], row_sin[:, None, :])
        .astype(jnp.bfloat16)
        .reshape(row_len, local_heads * head_dim)
    )
    q_up_part = matmul_tn(latent_rows, query_back)
    latent_part = matmul_nt(query_back, w_q_up)
    packed_sums = lax.psum_scatter(
        jnp.concatenate([latent_part, key_back, value_back], axis=1).astype(jnp.bfloat16),
        "heads",
        scatter_dimension=0,
        tiled=True,
    ).astype(jnp.float32)
    latent_back = packed_sums[:, :latent_width]
    key_sum = packed_sums[:, latent_width : latent_width + head_dim]
    value_sum = packed_sums[:, latent_width + head_dim :]
    latent_raw_grad, gain_latent_grad = norm_back(
        latent_raw, scale_latent, gain_latent, latent_back
    )
    latent_raw_back = latent_raw_grad.astype(jnp.bfloat16)
    key_pre_back = rotate_back(key_sum, own_cos, own_sin).astype(jnp.bfloat16)
    values_low = value_sum.astype(jnp.bfloat16)
    normed_one_back = (
        matmul_nt(latent_raw_back, w_q_down)
        + matmul_nt(key_pre_back, w_key)
        + matmul_nt(values_low, w_value)
    )
    input_part, gain_one_grad = norm_back(inputs, scale_one, gain_one, normed_one_back)
    input_grad = hidden_back + input_part
    packed_back = lax.all_gather(
        jnp.concatenate([latent_raw_back, key_pre_back, values_low], axis=1),
        "heads",
        axis=0,
        tiled=True,
    )
    shared_part = matmul_tn(normed_parts, packed_back).astype(jnp.bfloat16)
    shared_grad = lax.psum_scatter(
        shared_part, "dp", scatter_dimension=0, tiled=True
    ).astype(jnp.float32)
    q_down_grad = shared_grad[:, :latent_width]
    key_w_grad = shared_grad[:, latent_width : latent_width + head_dim]
    value_w_grad = shared_grad[:, latent_width + head_dim :]
    gains_part = jnp.concatenate([gain_one_grad, gain_latent_grad, gain_two_grad])
    gains_grad = lax.psum_scatter(gains_part, ("dp", "heads"), scatter_dimension=0, tiled=True)
    ffn_sums = lax.psum_scatter(
        jnp.concatenate([gate_up_part, down_w_part], axis=1).astype(jnp.bfloat16),
        "dp",
        scatter_dimension=0,
        tiled=True,
    ).astype(jnp.float32)
    local_ff = w_gate.shape[1]
    gate_w_grad = ffn_sums[:, :local_ff]
    up_w_grad = ffn_sums[:, local_ff : 2 * local_ff]
    down_w_grad = ffn_sums[:, 2 * local_ff :]
    local_q = w_q_up.shape[1]
    head_sums = lax.psum_scatter(
        jnp.concatenate(
            [
                q_up_part.reshape(dp_count, -1, local_q),
                out_w_part.reshape(dp_count, -1, local_q),
            ],
            axis=1,
        ).astype(jnp.bfloat16),
        "dp",
        scatter_dimension=0,
        tiled=True,
    ).astype(jnp.float32)[0]
    q_up_rows = w_q_up.shape[0] // dp_count
    q_up_grad = head_sums[:q_up_rows]
    out_w_grad = head_sums[q_up_rows:]
    gains_mom = decay_rate * mom_gains + gains_grad
    q_down_mom = decay_rate * mom_q_down + q_down_grad
    key_w_mom = decay_rate * mom_key + key_w_grad
    value_w_mom = decay_rate * mom_value + value_w_grad
    q_up_mom = decay_rate * mom_q_up + q_up_grad
    out_w_mom = decay_rate * mom_out + out_w_grad
    gate_w_mom = decay_rate * mom_gate + gate_w_grad
    up_w_mom = decay_rate * mom_up + up_w_grad
    down_w_mom = decay_rate * mom_down + down_w_grad
    gains_new = own_rows(gains, all_count, all_rank) - gain_rate * gains_mom
    ffn_count = w_gate.shape[1] // FF_BLOCK
    head_blocks = (
        split_columns(q_up_mom, head_dim),
        split_columns(out_w_mom, head_dim),
        jnp.concatenate(
            [
                split_columns(gate_w_mom, FF_BLOCK),
                split_columns(up_w_mom, FF_BLOCK),
                split_columns(down_w_mom, FF_BLOCK),
            ],
            axis=0,
        ),
    )
    mom_rows = jnp.concatenate([q_down_mom, key_w_mom, value_w_mom], axis=1).astype(jnp.bfloat16)
    mom_rows = lax.all_gather(mom_rows, "dp", axis=0, tiled=True)
    mom_rows = lax.all_gather(mom_rows, "heads", axis=0, tiled=True)
    pair_rows = jnp.stack(
        [
            mom_rows[:, latent_width : latent_width + head_dim],
            mom_rows[:, latent_width + head_dim :],
        ]
    )
    shared_iter = (
        orthogonal(q_down_mom[None], gram_of(mom_rows[None, :, :latent_width])),
        orthogonal(jnp.stack([key_w_mom, value_w_mom]), gram_of(pair_rows)),
    )
    head_grams = lax.psum(
        tuple(gram_of(blocks).astype(jnp.bfloat16) for blocks in head_blocks), "dp"
    )
    head_iter = tuple(
        orthogonal(blocks, grams.astype(jnp.float32))
        for blocks, grams in zip(head_blocks, head_grams)
    )
    query_ortho, output_ortho, ffn_ortho = head_iter
    q_up_new = own_rows(w_q_up, dp_count, dp_rank) - muon_rate * math.sqrt(
        w_q_up.shape[0] / head_dim
    ) * join_columns(query_ortho)
    out_w_new = own_rows(w_out, dp_count, dp_rank) - muon_rate * math.sqrt(
        w_out.shape[0] / head_dim
    ) * join_columns(output_ortho)
    ffn_factor = muon_rate * math.sqrt(w_gate.shape[0] / FF_BLOCK)
    gate_w_new = own_rows(w_gate, dp_count, dp_rank) - ffn_factor * join_columns(
        ffn_ortho[:ffn_count]
    )
    up_w_new = own_rows(w_up, dp_count, dp_rank) - ffn_factor * join_columns(
        ffn_ortho[ffn_count : 2 * ffn_count]
    )
    down_w_new = own_rows(w_down, dp_count, dp_rank) - ffn_factor * join_columns(
        ffn_ortho[2 * ffn_count :]
    )
    q_down_new = (
        own_rows(w_q_down, all_count, all_rank)
        - muon_rate * math.sqrt(w_q_down.shape[0] / latent_width) * shared_iter[0][0]
    )
    pair_factor = muon_rate * math.sqrt(w_key.shape[0] / head_dim)
    key_w_new = own_rows(w_key, all_count, all_rank) - pair_factor * shared_iter[1][0]
    value_w_new = own_rows(w_value, all_count, all_rank) - pair_factor * shared_iter[1][1]
    return (
        layer_out,
        input_grad,
        gains_grad,
        q_down_grad,
        key_w_grad,
        value_w_grad,
        q_up_grad,
        out_w_grad,
        gate_w_grad,
        up_w_grad,
        down_w_grad,
        gains_mom,
        q_down_mom,
        key_w_mom,
        value_w_mom,
        q_up_mom,
        out_w_mom,
        gate_w_mom,
        up_w_mom,
        down_w_mom,
        gains_new,
        q_down_new,
        key_w_new,
        value_w_new,
        q_up_new,
        out_w_new,
        gate_w_new,
        up_w_new,
        down_w_new,
    )


def solution(mesh):
    placed = (
        P(("dp", "heads"), None),
        P(("dp", "heads"), None),
        P("dp", None),
        P(),
        P(),
        P(),
        P(),
        P(None, "heads"),
        P(None, "heads"),
        P(None, "heads"),
        P(None, "heads"),
        P(None, "heads"),
        P(("dp", "heads")),
        P(("dp", "heads"), None),
        P(("dp", "heads"), None),
        P(("dp", "heads"), None),
        P("dp", "heads"),
        P("dp", "heads"),
        P("dp", "heads"),
        P("dp", "heads"),
        P("dp", "heads"),
    )
    return jax.shard_map(
        on_device,
        mesh=mesh,
        in_specs=placed,
        out_specs=(
            P(("dp", "heads"), None),
            P(("dp", "heads"), None),
            P(("dp", "heads")),
            P(("dp", "heads"), None),
            P(("dp", "heads"), None),
            P(("dp", "heads"), None),
            P("dp", "heads"),
            P("dp", "heads"),
            P("dp", "heads"),
            P("dp", "heads"),
            P("dp", "heads"),
            P(("dp", "heads")),
            P(("dp", "heads"), None),
            P(("dp", "heads"), None),
            P(("dp", "heads"), None),
            P("dp", "heads"),
            P("dp", "heads"),
            P("dp", "heads"),
            P("dp", "heads"),
            P("dp", "heads"),
            P(("dp", "heads")),
            P(("dp", "heads"), None),
            P(("dp", "heads"), None),
            P(("dp", "heads"), None),
            P("dp", "heads"),
            P("dp", "heads"),
            P("dp", "heads"),
            P("dp", "heads"),
            P("dp", "heads"),
        ),
        check_vma=False,
    )
```

```python
import math

import jax
import jax.numpy as jnp
from jax import lax
from jax.experimental import pallas as pl
from jax.experimental.pallas import tpu as pltpu
from jax.sharding import PartitionSpec as P

NS_STEPS = 3
FF_BLOCK = 352
SIDE = 4
CORES = 2

coef_first = 3.4445
coef_second = -4.775
coef_third = 2.0315
muon_rate = 0.5
gain_rate = 0.004
decay_rate = 0.5
low_type = jnp.bfloat16
vmem_bytes = 28 * 1024 * 1024


def matmul(left, right):
    return jnp.dot(left, right, preferred_element_type=jnp.float32)


def matmul_nt(left, right):
    return lax.dot_general(
        left, right, (((1,), (1,)), ((), ())), preferred_element_type=jnp.float32
    )


def matmul_tn(left, right):
    return lax.dot_general(
        left, right, (((0,), (0,)), ((), ())), preferred_element_type=jnp.float32
    )


def rms_scale(values):
    return lax.rsqrt(jnp.mean(values * values, axis=-1, keepdims=True) + 1e-05)


def norm_back(values, scale, gain, grad_out):
    weighted = gain * grad_out
    inner = jnp.mean(values * weighted, axis=-1, keepdims=True)
    grad_in = scale * weighted - values * (scale * scale * scale) * inner
    gain_grad = jnp.sum(grad_out * values * scale, axis=0)
    return (grad_in, gain_grad)


def segment_info(starts, token_index):
    started = starts[None, :] <= token_index[:, None]
    seg_ids = jnp.sum(started.astype(jnp.int32), axis=1)
    seg_begin = jnp.max(jnp.where(started, starts[None, :], 0), axis=1)
    return (seg_ids, token_index - seg_begin)


def rotary_tables(positions, head_dim):
    half_dim = head_dim // 2
    frequency = jnp.exp(
        jnp.arange(half_dim, dtype=jnp.float32) * (-2.0 * math.log(10000.0) / head_dim)
    )
    angles = positions.astype(jnp.float32)[:, None] * frequency[None, :]
    return (jnp.cos(angles), jnp.sin(angles))


def rotate(values, cosine, sine_part):
    half_dim = values.shape[-1] // 2
    first_half = values[..., :half_dim]
    second_half = values[..., half_dim:]
    return jnp.concatenate(
        [
            first_half * cosine - second_half * sine_part,
            second_half * cosine + first_half * sine_part,
        ],
        axis=-1,
    )


def rotate_back(grads, cosine, sine_part):
    return rotate(grads, cosine, -sine_part)


def shift_heads(values, step, core):
    pairs = [
        (CORES * place + side, CORES * ((place + step) % SIDE) + (side ^ core))
        for place in range(SIDE)
        for side in range(CORES)
    ]
    return lax.ppermute(values, "heads", pairs)


def shift_dp(values, step_z, step_x):
    pairs = [
        (SIDE * z + x, SIDE * ((z + step_z) % SIDE) + (x + step_x) % SIDE)
        for z in range(SIDE)
        for x in range(SIDE)
    ]
    return lax.ppermute(values, "dp", pairs)


def gather_heads(own):
    ring = [own] + [shift_heads(own, -step, 0) for step in range(1, SIDE)]
    return ring + [shift_heads(piece, 0, 1) for piece in ring]


def scatter_heads(far_half, own_half):
    rows = own_half.shape[0] // SIDE
    chip_sum = own_half.astype(jnp.float32) + shift_heads(far_half, 0, 1).astype(jnp.float32)
    chip_sum = chip_sum.reshape(SIDE, rows, *own_half.shape[1:])
    total = chip_sum[0]
    for step in range(1, SIDE):
        total = total + shift_heads(chip_sum[step].astype(far_half.dtype), step, 0).astype(
            jnp.float32
        )
    return total


def scatter_dp(parts):
    place_z = lax.axis_index("dp") // SIDE
    place_x = lax.axis_index("dp") % SIDE
    kind = parts.dtype
    grid = parts.reshape(SIDE, SIDE, *parts.shape[1:])

    def pick(array, place, axis):
        return lax.dynamic_index_in_dim(array, place % SIDE, axis, keepdims=False)

    total = pick(grid, place_x, 1).astype(jnp.float32)
    for step in range(1, SIDE):
        total = total + shift_dp(pick(grid, place_x + step, 1), 0, step).astype(jnp.float32)
    column = total.astype(kind)
    total = pick(total, place_z, 0)
    for step in range(1, SIDE):
        total = total + shift_dp(pick(column, place_z + step, 0), step, 0).astype(jnp.float32)
    return total


def gather_dp(own):
    ring = jnp.concatenate([own] + [shift_dp(own, 0, step) for step in range(1, SIDE)], axis=0)
    return jnp.concatenate([ring] + [shift_dp(ring, step, 0) for step in range(1, SIDE)], axis=0)


def visible(ids_q, ids_k, first_row, rows, cols):
    query_at = first_row + lax.broadcasted_iota(jnp.int32, (rows, cols), 0)
    key_at = lax.broadcasted_iota(jnp.int32, (rows, cols), 1)
    return (ids_q == ids_k) & (key_at <= query_at)


def attend_kernel(
    slots, latent, weight, keys, values, cosine, sine, ids_q, ids_k, query_out, mixed_out, lse_out
):
    row_len, head_dim = keys.shape
    piece = row_len // (SIDE * CORES)
    block = CORES * piece
    scale = head_dim ** (-0.5)
    for index in range(SIDE):
        first = index * block
        end = first + block
        rows = slice(first, end)
        query = rotate(matmul(latent[rows, :], weight[...]), cosine[rows, :], sine[rows, :])
        query = query.astype(low_type)
        query_out[rows, :] = query
        scores = matmul_nt(query, keys[:end, :]) * scale
        allowed = visible(ids_q[rows, :], ids_k[:, :end], first, block, end)
        scores = jnp.where(allowed, scores, -1e30)
        row_max = jnp.max(scores, axis=-1, keepdims=True)
        exponent = jnp.exp(scores - row_max)
        row_total = jnp.sum(exponent, axis=-1, keepdims=True)
        probs = (exponent * (1.0 / row_total)).astype(low_type)
        lse_out[0, rows, :] = row_max + jnp.log(row_total)
        mixed = matmul(probs, values[:end, :]).astype(low_type)
        for side in range(CORES):
            place = pl.multiple_of(slots[CORES * index + side] * piece, piece)
            mixed_out[pl.ds(place, piece), :] = mixed[side * piece : (side + 1) * piece, :]


def attend(slots, latent_rows, w_q_up, key_rows, value_rows, cosine, sine, row_ids):
    row_len, head_dim = key_rows.shape
    latent_width, width = w_q_up.shape
    count = width // head_dim
    whole = lambda head, slots: (0, 0)
    column = lambda head, slots: (0, head)
    return pl.pallas_call(
        attend_kernel,
        grid_spec=pltpu.PrefetchScalarGridSpec(
            num_scalar_prefetch=1,
            grid=(count,),
            in_specs=[
                pl.BlockSpec((row_len, latent_width), whole),
                pl.BlockSpec((latent_width, head_dim), column),
                pl.BlockSpec((row_len, head_dim), whole),
                pl.BlockSpec((row_len, head_dim), whole),
                pl.BlockSpec((row_len, head_dim // 2), whole),
                pl.BlockSpec((row_len, head_dim // 2), whole),
                pl.BlockSpec((row_len, 1), whole),
                pl.BlockSpec((1, row_len), whole),
            ],
            out_specs=[
                pl.BlockSpec((row_len, head_dim), column),
                pl.BlockSpec((row_len, head_dim), column),
                pl.BlockSpec((1, row_len, 1), lambda head, slots: (head, 0, 0)),
            ],
        ),
        out_shape=[
            jax.ShapeDtypeStruct((row_len, width), low_type),
            jax.ShapeDtypeStruct((row_len, width), low_type),
            jax.ShapeDtypeStruct((count, row_len, 1), jnp.float32),
        ],
        compiler_params=pltpu.CompilerParams(vmem_limit_bytes=vmem_bytes),
        cost_estimate=pl.CostEstimate(
            flops=2 * width * row_len * (latent_width + 2 * row_len),
            bytes_accessed=8 * row_len * width,
            transcendentals=count * row_len * row_len,
        ),
        name="attend",
    )(
        slots,
        latent_rows,
        w_q_up,
        key_rows,
        value_rows,
        cosine,
        sine,
        row_ids[:, None],
        row_ids[None, :],
    )


def attend_back_kernel(
    slots,
    query_in,
    keys,
    values,
    mixed_back,
    lse,
    cosine,
    sine,
    ids_q,
    ids_k,
    query_back,
    pair_back,
    key_sum,
    value_sum,
):
    row_len, head_dim = keys.shape
    piece = row_len // (SIDE * CORES)
    block = CORES * piece
    scale = head_dim ** (-0.5)
    head = pl.program_id(0)

    @pl.when(head == 0)
    def _():
        key_sum[...] = jnp.zeros_like(key_sum)
        value_sum[...] = jnp.zeros_like(value_sum)

    for index in range(SIDE):
        first = index * block
        end = first + block
        rows = slice(first, end)
        places = [
            pl.multiple_of(slots[CORES * index + side] * piece, piece) for side in range(CORES)
        ]
        query = query_in[rows, :]
        back = jnp.concatenate([mixed_back[pl.ds(place, piece), :] for place in places], axis=0)
        scores = matmul_nt(query, keys[:end, :]) * scale
        allowed = visible(ids_q[rows, :], ids_k[:, :end], first, block, end)
        probs = jnp.where(allowed, jnp.exp(scores - lse[0, rows, :]), 0.0)
        probs_back = matmul_nt(back, values[:end, :])
        inner = jnp.sum(probs * probs_back, axis=-1, keepdims=True)
        score_back = (probs * (probs_back - inner)).astype(low_type)
        probs_low = probs.astype(low_type)
        value_sum[:end, :] += matmul_tn(probs_low, back)
        key_sum[:end, :] += matmul_tn(score_back, query) * scale
        query_grad = matmul(score_back, keys[:end, :]) * scale
        query_grad = rotate_back(query_grad, cosine[rows, :], sine[rows, :]).astype(low_type)
        for side, place in enumerate(places):
            query_back[pl.ds(place, piece), :] = query_grad[side * piece : (side + 1) * piece, :]

    @pl.when(head == pl.num_programs(0) - 1)
    def _():
        for index in range(SIDE * CORES):
            place = pl.multiple_of(slots[index] * piece, piece)
            rows = slice(index * piece, (index + 1) * piece)
            pair_back[pl.ds(place, piece), :head_dim] = key_sum[rows, :].astype(low_type)
            pair_back[pl.ds(place, piece), head_dim:] = value_sum[rows, :].astype(low_type)


def attend_back(slots, query_rows, key_rows, value_rows, mixed_back, lse, cosine, sine, row_ids):
    row_len, head_dim = key_rows.shape
    width = query_rows.shape[1]
    count = width // head_dim
    whole = lambda head, slots: (0, 0)
    column = lambda head, slots: (0, head)
    return pl.pallas_call(
        attend_back_kernel,
        grid_spec=pltpu.PrefetchScalarGridSpec(
            num_scalar_prefetch=1,
            grid=(count,),
            in_specs=[
                pl.BlockSpec((row_len, head_dim), column),
                pl.BlockSpec((row_len, head_dim), whole),
                pl.BlockSpec((row_len, head_dim), whole),
                pl.BlockSpec((row_len, head_dim), column),
                pl.BlockSpec((1, row_len, 1), lambda head, slots: (head, 0, 0)),
                pl.BlockSpec((row_len, head_dim // 2), whole),
                pl.BlockSpec((row_len, head_dim // 2), whole),
                pl.BlockSpec((row_len, 1), whole),
                pl.BlockSpec((1, row_len), whole),
            ],
            out_specs=[
                pl.BlockSpec((row_len, head_dim), column),
                pl.BlockSpec((row_len, 2 * head_dim), whole),
            ],
            scratch_shapes=[
                pltpu.VMEM((row_len, head_dim), jnp.float32),
                pltpu.VMEM((row_len, head_dim), jnp.float32),
            ],
        ),
        out_shape=[
            jax.ShapeDtypeStruct((row_len, width), low_type),
            jax.ShapeDtypeStruct((row_len, 2 * head_dim), low_type),
        ],
        compiler_params=pltpu.CompilerParams(vmem_limit_bytes=vmem_bytes),
        cost_estimate=pl.CostEstimate(
            flops=10 * width * row_len * row_len,
            bytes_accessed=8 * row_len * width,
            transcendentals=count * row_len * row_len,
        ),
        name="attend_back",
    )(
        slots,
        query_rows,
        key_rows,
        value_rows,
        mixed_back,
        lse,
        cosine,
        sine,
        row_ids[:, None],
        row_ids[None, :],
    )


def place_kernel(slots, source, target):
    target[...] = source[...]


def place_blocks(slots, rows, count):
    piece = rows.shape[0] // count
    width = rows.shape[1]
    return pl.pallas_call(
        place_kernel,
        grid_spec=pltpu.PrefetchScalarGridSpec(
            num_scalar_prefetch=1,
            grid=(count,),
            in_specs=[pl.BlockSpec((piece, width), lambda index, slots: (index, 0))],
            out_specs=pl.BlockSpec((piece, width), lambda index, slots: (slots[index], 0)),
        ),
        out_shape=jax.ShapeDtypeStruct(rows.shape, rows.dtype),
        cost_estimate=pl.CostEstimate(
            flops=0, bytes_accessed=4 * rows.shape[0] * width, transcendentals=0
        ),
        name="place_blocks",
    )(slots, rows)


def gram_of(blocks):
    low = blocks.astype(low_type)
    return jnp.einsum("brc,brd->bcd", low, low, preferred_element_type=jnp.float32)


def times(left, right):
    return jnp.einsum(
        "brc,bcd->brd",
        left.astype(low_type),
        right.astype(low_type),
        preferred_element_type=jnp.float32,
    )


def orthogonal(blocks, gram_sums):
    diagonal = jnp.eye(gram_sums.shape[-1], dtype=jnp.bool_)
    trace_sum = jnp.sum(jnp.where(diagonal, gram_sums, 0.0), axis=(1, 2))
    factor = 1.0 / (jnp.sqrt(trace_sum) + 1e-07)
    iterate = blocks * factor[:, None, None]
    gram = gram_sums * (factor * factor)[:, None, None]
    for step_index in range(NS_STEPS):
        first_term = times(iterate, gram)
        second_term = times(first_term, gram)
        iterate = coef_first * iterate + coef_second * first_term + coef_third * second_term
        if step_index + 1 < NS_STEPS:
            change = coef_second * gram + coef_third * times(gram, gram)
            once = times(gram, change)
            twice = times(once, change)
            gram = (coef_first * coef_first) * gram + (2.0 * coef_first) * once + twice
    return iterate


def split_columns(matrix, block_cols):
    row_count = matrix.shape[0]
    return matrix.reshape(row_count, matrix.shape[1] // block_cols, block_cols).transpose(1, 0, 2)


def join_columns(blocks):
    return blocks.transpose(1, 0, 2).reshape(blocks.shape[1], blocks.shape[0] * blocks.shape[2])


def own_rows(weight, count, rank):
    share_rows = weight.shape[0] // count
    return lax.dynamic_slice_in_dim(weight, rank * share_rows, share_rows, 0).astype(jnp.float32)


def on_device(
    tokens_in,
    cotangent,
    seg_starts,
    gains,
    w_q_down,
    w_key,
    w_value,
    w_q_up,
    w_out,
    w_gate,
    w_up,
    w_down,
    mom_gains,
    mom_q_down,
    mom_key,
    mom_value,
    mom_q_up,
    mom_out,
    mom_gate,
    mom_up,
    mom_down,
):
    heads_count = lax.axis_size("heads")
    heads_rank = lax.axis_index("heads")
    dp_count = lax.axis_size("dp")
    dp_rank = lax.axis_index("dp")
    all_rank = lax.axis_index(("dp", "heads"))
    all_count = dp_count * heads_count
    local_rows = tokens_in.shape[0]
    row_len = local_rows * heads_count
    half_len = row_len // 2
    model_width = tokens_in.shape[1]
    latent_width = w_q_down.shape[1]
    head_dim = w_key.shape[1]
    local_q = w_q_up.shape[1]
    local_ff = w_gate.shape[1]
    starts = seg_starts[0]
    whole_index = jnp.arange(row_len, dtype=jnp.int32)
    own_index = heads_rank * local_rows + jnp.arange(local_rows, dtype=jnp.int32)
    ranks = jnp.arange(heads_count, dtype=jnp.int32)
    far_core = (ranks % CORES) ^ (heads_rank % CORES)
    slots = SIDE * far_core + (ranks // CORES - heads_rank // CORES) % SIDE
    gain_one = gains[:model_width]
    gain_latent = gains[model_width : model_width + latent_width]
    gain_two = gains[model_width + latent_width :]
    inputs = tokens_in.astype(jnp.float32)
    scale_one = rms_scale(inputs)
    normed_one = (inputs * scale_one * gain_one).astype(low_type)
    latent_raw = matmul(normed_one, w_q_down)
    scale_latent = rms_scale(latent_raw)
    latent_normed = (latent_raw * scale_latent * gain_latent).astype(low_type)
    own_pos = segment_info(starts, own_index)[1]
    own_cos, own_sin = rotary_tables(own_pos, head_dim)
    key_local = rotate(matmul(normed_one, w_key), own_cos, own_sin).astype(low_type)
    value_local = matmul(normed_one, w_value).astype(low_type)
    packed_rows = lax.all_gather(
        jnp.concatenate([latent_normed, key_local, value_local], axis=1), "heads", axis=0, tiled=True
    )
    latent_rows = packed_rows[:, :latent_width]
    key_rows = packed_rows[:, latent_width : latent_width + head_dim]
    value_rows = packed_rows[:, latent_width + head_dim :]
    share_rows = model_width // all_count
    normed_parts = lax.all_to_all(
        normed_one.reshape(local_rows, dp_count, heads_count, share_rows)
        .transpose(2, 0, 1, 3)
        .reshape(heads_count * local_rows, dp_count * share_rows),
        "heads",
        split_axis=0,
        concat_axis=0,
        tiled=True,
    )
    normed_parts = place_blocks(slots, normed_parts, heads_count)
    grad_rows = place_blocks(
        slots, lax.all_gather(cotangent, "heads", axis=0, tiled=True), heads_count
    )
    row_ids, row_pos = segment_info(starts, whole_index)
    row_cos, row_sin = rotary_tables(row_pos, head_dim)
    query_rows, attended, lse = attend(
        slots, latent_rows, w_q_up, key_rows, value_rows, row_cos, row_sin, row_ids
    )
    attn_mixed = scatter_heads(
        matmul_nt(attended[half_len:], w_out).astype(low_type),
        matmul_nt(attended[:half_len], w_out),
    )
    hidden_one = inputs + attn_mixed
    scale_two = rms_scale(hidden_one)
    normed_two = (hidden_one * scale_two * gain_two).astype(low_type)
    ffn_input = jnp.concatenate(gather_heads(normed_two), axis=0)
    gate_raw = matmul(ffn_input, w_gate)
    up_raw = matmul(ffn_input, w_up)
    sigmoid_gate = jax.nn.sigmoid(gate_raw)
    activated = gate_raw * sigmoid_gate
    hidden_mid = (activated * up_raw).astype(low_type)
    mid_back = matmul(grad_rows, w_down)
    gate_back = (mid_back * up_raw * sigmoid_gate * (1.0 + gate_raw * (1.0 - sigmoid_gate))).astype(
        low_type
    )
    up_back = (mid_back * activated).astype(low_type)
    normed_two_back = scatter_heads(
        (matmul_nt(gate_back[half_len:], w_gate) + matmul_nt(up_back[half_len:], w_up)).astype(
            low_type
        ),
        matmul_nt(gate_back[:half_len], w_gate) + matmul_nt(up_back[:half_len], w_up),
    )
    gate_up_part = matmul_tn(ffn_input, jnp.concatenate([gate_back, up_back], axis=1))
    down_w_part = matmul_tn(grad_rows, hidden_mid)
    ffn_sums = lax.psum_scatter(
        jnp.concatenate([gate_up_part, down_w_part], axis=1).astype(low_type),
        "dp",
        scatter_dimension=0,
        tiled=True,
    ).astype(jnp.float32)
    hidden_part, gain_two_grad = norm_back(hidden_one, scale_two, gain_two, normed_two_back)
    hidden_back = cotangent.astype(jnp.float32) + hidden_part
    hidden_rows = jnp.concatenate(gather_heads(hidden_back.astype(low_type)), axis=0)
    attended_back = matmul(hidden_rows, w_out).astype(low_type)
    late_mid, _ = lax.optimization_barrier((hidden_mid, attended_back))
    ffn_mixed = scatter_heads(
        matmul_nt(late_mid[half_len:], w_down).astype(low_type),
        matmul_nt(late_mid[:half_len], w_down),
    )
    layer_out = (hidden_one + ffn_mixed).astype(low_type)
    out_w_part = matmul_tn(hidden_rows, attended)
    query_back, pair_back = attend_back(
        slots, query_rows, key_rows, value_rows, attended_back, lse, row_cos, row_sin, row_ids
    )
    packed_sums = scatter_heads(
        jnp.concatenate(
            [matmul_nt(query_back[half_len:], w_q_up).astype(low_type), pair_back[half_len:]],
            axis=1,
        ),
        jnp.concatenate(
            [matmul_nt(query_back[:half_len], w_q_up).astype(low_type), pair_back[:half_len]],
            axis=1,
        ),
    )
    latent_back = packed_sums[:, :latent_width]
    key_sum = packed_sums[:, latent_width : latent_width + head_dim]
    value_sum = packed_sums[:, latent_width + head_dim :]
    latent_raw_grad, gain_latent_grad = norm_back(
        latent_raw, scale_latent, gain_latent, latent_back
    )
    latent_raw_back = latent_raw_grad.astype(low_type)
    key_pre_back = rotate_back(key_sum, own_cos, own_sin).astype(low_type)
    values_low = value_sum.astype(low_type)
    packed_back = jnp.concatenate(
        gather_heads(jnp.concatenate([latent_raw_back, key_pre_back, values_low], axis=1)), axis=0
    )
    shared_part = matmul_tn(normed_parts, packed_back).astype(low_type)
    shared_grad = scatter_dp(shared_part.reshape(dp_count, share_rows, shared_part.shape[1]))
    q_down_grad = shared_grad[:, :latent_width]
    key_w_grad = shared_grad[:, latent_width : latent_width + head_dim]
    value_w_grad = shared_grad[:, latent_width + head_dim :]
    latent_ordered = place_blocks(slots, latent_rows, heads_count)
    q_up_part = matmul_tn(latent_ordered, query_back)
    head_sums = scatter_dp(
        jnp.concatenate(
            [
                q_up_part.astype(low_type).reshape(dp_count, -1, local_q),
                out_w_part.astype(low_type).reshape(dp_count, -1, local_q),
            ],
            axis=1,
        )
    )
    q_up_rows = w_q_up.shape[0] // dp_count
    q_up_grad = head_sums[:q_up_rows]
    out_w_grad = head_sums[q_up_rows:]
    gate_w_grad = ffn_sums[:, :local_ff]
    up_w_grad = ffn_sums[:, local_ff : 2 * local_ff]
    down_w_grad = ffn_sums[:, 2 * local_ff :]
    normed_one_back = (
        matmul_nt(latent_raw_back, w_q_down)
        + matmul_nt(key_pre_back, w_key)
        + matmul_nt(values_low, w_value)
    )
    input_part, gain_one_grad = norm_back(inputs, scale_one, gain_one, normed_one_back)
    input_grad = hidden_back + input_part
    share_gains = gains.shape[0] // all_count
    gains_part = jnp.concatenate([gain_one_grad, gain_latent_grad, gain_two_grad])
    gains_part = gains_part.reshape(dp_count, heads_count, share_gains).transpose(1, 0, 2)
    gains_part = gains_part.reshape(SIDE, CORES, dp_count * share_gains)
    own_core = heads_rank % CORES
    own_step = heads_rank // CORES

    def by_step(array, core):
        side = lax.dynamic_index_in_dim(array, core, 1, keepdims=False)
        return lax.dynamic_slice_in_dim(jnp.concatenate([side, side], axis=0), own_step, SIDE, 0)

    gains_sum = scatter_heads(by_step(gains_part, 1 - own_core), by_step(gains_part, own_core))
    gains_grad = scatter_dp(gains_sum.reshape(dp_count, 1, share_gains))[0]
    gains_mom = decay_rate * mom_gains + gains_grad
    q_down_mom = decay_rate * mom_q_down + q_down_grad
    key_w_mom = decay_rate * mom_key + key_w_grad
    value_w_mom = decay_rate * mom_value + value_w_grad
    q_up_mom = decay_rate * mom_q_up + q_up_grad
    out_w_mom = decay_rate * mom_out + out_w_grad
    gate_w_mom = decay_rate * mom_gate + gate_w_grad
    up_w_mom = decay_rate * mom_up + up_w_grad
    down_w_mom = decay_rate * mom_down + down_w_grad
    gains_new = own_rows(gains, all_count, all_rank) - gain_rate * gains_mom
    ffn_count = w_gate.shape[1] // FF_BLOCK
    ffn_blocks = jnp.concatenate(
        [
            split_columns(gate_w_mom, FF_BLOCK),
            split_columns(up_w_mom, FF_BLOCK),
            split_columns(down_w_mom, FF_BLOCK),
        ],
        axis=0,
    )
    ffn_gram = lax.psum(gram_of(ffn_blocks).astype(low_type), "dp").astype(jnp.float32)
    ffn_ortho = orthogonal(ffn_blocks, ffn_gram)
    query_blocks = split_columns(q_up_mom, head_dim)
    output_blocks = split_columns(out_w_mom, head_dim)
    head_grams = jnp.concatenate([gram_of(query_blocks), gram_of(output_blocks)], axis=0)
    gram_rows = head_dim // dp_count
    head_count = query_blocks.shape[0]
    head_grams = (
        head_grams.astype(low_type)
        .reshape(2 * head_count, dp_count, gram_rows, head_dim)
        .transpose(1, 0, 2, 3)
        .reshape(dp_count, 2 * head_count * gram_rows, head_dim)
    )
    head_grams = scatter_dp(head_grams).astype(low_type)
    place_z = dp_rank // SIDE
    place_x = dp_rank % SIDE
    head_grams = gather_dp(head_grams[None])
    head_grams = head_grams.reshape(SIDE, SIDE, 2 * head_count, gram_rows, head_dim)
    order_z = (place_z - jnp.arange(SIDE)) % SIDE
    order_x = (place_x - jnp.arange(SIDE)) % SIDE
    head_grams = jnp.concatenate(
        [lax.dynamic_index_in_dim(head_grams, order_z[z], 0) for z in range(SIDE)], axis=0
    )
    head_grams = jnp.concatenate(
        [lax.dynamic_index_in_dim(head_grams, order_x[x], 1) for x in range(SIDE)], axis=1
    )
    head_grams = head_grams.transpose(2, 0, 1, 3, 4).reshape(2 * head_count, head_dim, head_dim)
    head_grams = head_grams.astype(jnp.float32)
    query_ortho = orthogonal(query_blocks, head_grams[:head_count])
    output_ortho = orthogonal(output_blocks, head_grams[head_count:])
    mom_rows = jnp.concatenate([q_down_mom, key_w_mom, value_w_mom], axis=1).astype(low_type)
    mom_rows = gather_dp(mom_rows)
    mom_rows = jnp.concatenate(gather_heads(mom_rows), axis=0)
    pair_rows = jnp.stack(
        [
            mom_rows[:, latent_width : latent_width + head_dim],
            mom_rows[:, latent_width + head_dim :],
        ]
    )
    shared_iter = (
        orthogonal(q_down_mom[None], gram_of(mom_rows[None, :, :latent_width])),
        orthogonal(jnp.stack([key_w_mom, value_w_mom]), gram_of(pair_rows)),
    )
    q_up_new = own_rows(w_q_up, dp_count, dp_rank) - muon_rate * math.sqrt(
        w_q_up.shape[0] / head_dim
    ) * join_columns(query_ortho)
    out_w_new = own_rows(w_out, dp_count, dp_rank) - muon_rate * math.sqrt(
        w_out.shape[0] / head_dim
    ) * join_columns(output_ortho)
    ffn_factor = muon_rate * math.sqrt(w_gate.shape[0] / FF_BLOCK)
    gate_w_new = own_rows(w_gate, dp_count, dp_rank) - ffn_factor * join_columns(
        ffn_ortho[:ffn_count]
    )
    up_w_new = own_rows(w_up, dp_count, dp_rank) - ffn_factor * join_columns(
        ffn_ortho[ffn_count : 2 * ffn_count]
    )
    down_w_new = own_rows(w_down, dp_count, dp_rank) - ffn_factor * join_columns(
        ffn_ortho[2 * ffn_count :]
    )
    q_down_new = (
        own_rows(w_q_down, all_count, all_rank)
        - muon_rate * math.sqrt(w_q_down.shape[0] / latent_width) * shared_iter[0][0]
    )
    pair_factor = muon_rate * math.sqrt(w_key.shape[0] / head_dim)
    key_w_new = own_rows(w_key, all_count, all_rank) - pair_factor * shared_iter[1][0]
    value_w_new = own_rows(w_value, all_count, all_rank) - pair_factor * shared_iter[1][1]
    return (
        layer_out,
        input_grad,
        gains_grad,
        q_down_grad,
        key_w_grad,
        value_w_grad,
        q_up_grad,
        out_w_grad,
        gate_w_grad,
        up_w_grad,
        down_w_grad,
        gains_mom,
        q_down_mom,
        key_w_mom,
        value_w_mom,
        q_up_mom,
        out_w_mom,
        gate_w_mom,
        up_w_mom,
        down_w_mom,
        gains_new,
        q_down_new,
        key_w_new,
        value_w_new,
        q_up_new,
        out_w_new,
        gate_w_new,
        up_w_new,
        down_w_new,
    )


def solution(mesh):
    placed = (
        P(("dp", "heads"), None),
        P(("dp", "heads"), None),
        P("dp", None),
        P(),
        P(),
        P(),
        P(),
        P(None, "heads"),
        P(None, "heads"),
        P(None, "heads"),
        P(None, "heads"),
        P(None, "heads"),
        P(("dp", "heads")),
        P(("dp", "heads"), None),
        P(("dp", "heads"), None),
        P(("dp", "heads"), None),
        P("dp", "heads"),
        P("dp", "heads"),
        P("dp", "heads"),
        P("dp", "heads"),
        P("dp", "heads"),
    )
    return jax.shard_map(
        on_device,
        mesh=mesh,
        in_specs=placed,
        out_specs=(
            P(("dp", "heads"), None),
            P(("dp", "heads"), None),
            P(("dp", "heads")),
            P(("dp", "heads"), None),
            P(("dp", "heads"), None),
            P(("dp", "heads"), None),
            P("dp", "heads"),
            P("dp", "heads"),
            P("dp", "heads"),
            P("dp", "heads"),
            P("dp", "heads"),
            P(("dp", "heads")),
            P(("dp", "heads"), None),
            P(("dp", "heads"), None),
            P(("dp", "heads"), None),
            P("dp", "heads"),
            P("dp", "heads"),
            P("dp", "heads"),
            P("dp", "heads"),
            P("dp", "heads"),
            P(("dp", "heads")),
            P(("dp", "heads"), None),
            P(("dp", "heads"), None),
            P(("dp", "heads"), None),
            P("dp", "heads"),
            P("dp", "heads"),
            P("dp", "heads"),
            P("dp", "heads"),
            P("dp", "heads"),
        ),
        check_vma=False,
    )
```

```python
import math

import jax
import jax.numpy as jnp
from jax import lax
from jax.experimental import pallas as pl
from jax.experimental.pallas import tpu as pltpu
from jax.sharding import PartitionSpec as P

NS_STEPS = 3
FF_BLOCK = 352
SIDE = 4
CORES = 2

coef_first = 3.4445
coef_second = -4.775
coef_third = 2.0315
muon_rate = 0.5
gain_rate = 0.004
decay_rate = 0.5
low_type = jnp.bfloat16
vmem_bytes = 28 * 1024 * 1024


def matmul(left, right):
    return jnp.dot(left, right, preferred_element_type=jnp.float32)


def matmul_nt(left, right):
    return lax.dot_general(
        left, right, (((1,), (1,)), ((), ())), preferred_element_type=jnp.float32
    )


def matmul_tn(left, right):
    return lax.dot_general(
        left, right, (((0,), (0,)), ((), ())), preferred_element_type=jnp.float32
    )


def rms_scale(values):
    return lax.rsqrt(jnp.mean(values * values, axis=-1, keepdims=True) + 1e-05)


def norm_back(values, scale, gain, grad_out):
    weighted = gain * grad_out
    inner = jnp.mean(values * weighted, axis=-1, keepdims=True)
    grad_in = scale * weighted - values * (scale * scale * scale) * inner
    gain_grad = jnp.sum(grad_out * values * scale, axis=0)
    return (grad_in, gain_grad)


def segment_info(starts, token_index):
    started = starts[None, :] <= token_index[:, None]
    seg_ids = jnp.sum(started.astype(jnp.int32), axis=1)
    seg_begin = jnp.max(jnp.where(started, starts[None, :], 0), axis=1)
    return (seg_ids, token_index - seg_begin)


def rotary_tables(positions, head_dim):
    half_dim = head_dim // 2
    frequency = jnp.exp(
        jnp.arange(half_dim, dtype=jnp.float32) * (-2.0 * math.log(10000.0) / head_dim)
    )
    angles = positions.astype(jnp.float32)[:, None] * frequency[None, :]
    return (jnp.cos(angles), jnp.sin(angles))


def rotate(values, cosine, sine_part):
    half_dim = values.shape[-1] // 2
    first_half = values[..., :half_dim]
    second_half = values[..., half_dim:]
    return jnp.concatenate(
        [
            first_half * cosine - second_half * sine_part,
            second_half * cosine + first_half * sine_part,
        ],
        axis=-1,
    )


def rotate_back(grads, cosine, sine_part):
    return rotate(grads, cosine, -sine_part)


def shift_heads(values, step, core):
    pairs = [
        (CORES * place + side, CORES * ((place + step) % SIDE) + (side ^ core))
        for place in range(SIDE)
        for side in range(CORES)
    ]
    return lax.ppermute(values, "heads", pairs)


def shift_dp(values, step_z, step_x):
    pairs = [
        (SIDE * z + x, SIDE * ((z + step_z) % SIDE) + (x + step_x) % SIDE)
        for z in range(SIDE)
        for x in range(SIDE)
    ]
    return lax.ppermute(values, "dp", pairs)


def gather_heads(own):
    ring = [own] + [shift_heads(own, -step, 0) for step in range(1, SIDE)]
    return ring + [shift_heads(piece, 0, 1) for piece in ring]


def scatter_heads(far_half, own_half):
    rows = own_half.shape[0] // SIDE
    chip_sum = own_half.astype(jnp.float32) + shift_heads(far_half, 0, 1).astype(jnp.float32)
    chip_sum = chip_sum.reshape(SIDE, rows, *own_half.shape[1:])
    total = chip_sum[0]
    for step in range(1, SIDE):
        total = total + shift_heads(chip_sum[step].astype(far_half.dtype), step, 0).astype(
            jnp.float32
        )
    return total


def scatter_dp(parts):
    place_z = lax.axis_index("dp") // SIDE
    place_x = lax.axis_index("dp") % SIDE
    kind = parts.dtype
    grid = parts.reshape(SIDE, SIDE, *parts.shape[1:])

    def pick(array, place, axis):
        return lax.dynamic_index_in_dim(array, place % SIDE, axis, keepdims=False)

    total = pick(grid, place_x, 1).astype(jnp.float32)
    for step in range(1, SIDE):
        total = total + shift_dp(pick(grid, place_x + step, 1), 0, step).astype(jnp.float32)
    column = total.astype(kind)
    total = pick(total, place_z, 0)
    for step in range(1, SIDE):
        total = total + shift_dp(pick(column, place_z + step, 0), step, 0).astype(jnp.float32)
    return total


def gather_dp(own):
    ring = jnp.concatenate([own] + [shift_dp(own, 0, step) for step in range(1, SIDE)], axis=0)
    return jnp.concatenate([ring] + [shift_dp(ring, step, 0) for step in range(1, SIDE)], axis=0)


def visible(ids_q, ids_k, first_row, rows, cols):
    query_at = first_row + lax.broadcasted_iota(jnp.int32, (rows, cols), 0)
    key_at = lax.broadcasted_iota(jnp.int32, (rows, cols), 1)
    return (ids_q == ids_k) & (key_at <= query_at)


def block_at(index, piece):
    return pl.ds(pl.multiple_of(index * piece, piece), piece)


def store_by_distance(where, rows_ref, near_ref, far_ref, piece):
    core = where[SIDE * CORES]
    for step in range(SIDE):
        near = CORES * step + core
        far = CORES * step + 1 - core
        near_ref[block_at(where[near], piece), :] = rows_ref[block_at(near, piece), :]
        far_ref[block_at(where[far] - SIDE, piece), :] = rows_ref[block_at(far, piece), :]


def attend_kernel(where, owner, *refs):
    pieces = refs[: SIDE * CORES]
    weight, cosine, sine, ids_q, ids_k = refs[SIDE * CORES : SIDE * CORES + 5]
    packed, query_out, near_out, far_out, lse_out, mixed_rows = refs[SIDE * CORES + 5 :]
    latent_width, head_dim = weight.shape
    piece = pieces[0].shape[0]
    block = CORES * piece
    scale = head_dim ** (-0.5)

    @pl.when(pl.program_id(0) == 0)
    def _():
        for index, source in enumerate(pieces):
            packed[block_at(owner[index], piece), :] = source[...]

    key_cols = slice(latent_width, latent_width + head_dim)
    value_cols = slice(latent_width + head_dim, latent_width + 2 * head_dim)
    for index in range(SIDE):
        first = index * block
        end = first + block
        rows = slice(first, end)
        query = matmul(packed[rows, :latent_width], weight[...])
        query = rotate(query, cosine[rows, :], sine[rows, :]).astype(low_type)
        query_out[rows, :] = query
        scores = matmul_nt(query, packed[:end, key_cols]) * scale
        allowed = visible(ids_q[rows, :], ids_k[:, :end], first, block, end)
        scores = jnp.where(allowed, scores, -1e30)
        row_max = jnp.max(scores, axis=-1, keepdims=True)
        exponent = jnp.exp(scores - row_max)
        row_total = jnp.sum(exponent, axis=-1, keepdims=True)
        probs = (exponent * (1.0 / row_total)).astype(low_type)
        lse_out[0, rows, :] = row_max + jnp.log(row_total)
        mixed_rows[rows, :] = matmul(probs, packed[:end, value_cols]).astype(low_type)
    store_by_distance(where, mixed_rows, near_out, far_out, piece)


def attend(where, owner, pieces, w_q_up, head_dim, cosine, sine, row_ids):
    piece, packed_width = pieces[0].shape
    row_len = piece * SIDE * CORES
    latent_width, width = w_q_up.shape
    count = width // head_dim
    whole = lambda head, where, owner: (0, 0)
    column = lambda head, where, owner: (0, head)
    return pl.pallas_call(
        attend_kernel,
        grid_spec=pltpu.PrefetchScalarGridSpec(
            num_scalar_prefetch=2,
            grid=(count,),
            in_specs=[pl.BlockSpec((piece, packed_width), whole)] * (SIDE * CORES)
            + [
                pl.BlockSpec((latent_width, head_dim), column),
                pl.BlockSpec((row_len, head_dim // 2), whole),
                pl.BlockSpec((row_len, head_dim // 2), whole),
                pl.BlockSpec((row_len, 1), whole),
                pl.BlockSpec((1, row_len), whole),
            ],
            out_specs=[
                pl.BlockSpec((row_len, packed_width), whole),
                pl.BlockSpec((row_len, head_dim), column),
                pl.BlockSpec((row_len // 2, head_dim), column),
                pl.BlockSpec((row_len // 2, head_dim), column),
                pl.BlockSpec((1, row_len, 1), lambda head, where, owner: (head, 0, 0)),
            ],
            scratch_shapes=[pltpu.VMEM((row_len, head_dim), low_type)],
        ),
        out_shape=[
            jax.ShapeDtypeStruct((row_len, packed_width), low_type),
            jax.ShapeDtypeStruct((row_len, width), low_type),
            jax.ShapeDtypeStruct((row_len // 2, width), low_type),
            jax.ShapeDtypeStruct((row_len // 2, width), low_type),
            jax.ShapeDtypeStruct((count, row_len, 1), jnp.float32),
        ],
        compiler_params=pltpu.CompilerParams(vmem_limit_bytes=vmem_bytes),
        cost_estimate=pl.CostEstimate(
            flops=2 * width * row_len * (latent_width + 2 * row_len),
            bytes_accessed=8 * row_len * width,
            transcendentals=count * row_len * row_len,
        ),
        name="attend",
    )(where, owner, *pieces, w_q_up, cosine, sine, row_ids[:, None], row_ids[None, :])


def attend_back_kernel(
    where,
    query_in,
    packed,
    mixed_back,
    lse,
    cosine,
    sine,
    ids_q,
    ids_k,
    weight,
    weight_back,
    near_out,
    far_out,
    query_back,
    totals,
):
    row_len, packed_width = packed.shape
    latent_width, head_dim = weight.shape
    piece = row_len // (SIDE * CORES)
    block = CORES * piece
    scale = head_dim ** (-0.5)
    head = pl.program_id(0)
    key_cols = slice(latent_width, latent_width + head_dim)
    value_cols = slice(latent_width + head_dim, latent_width + 2 * head_dim)

    @pl.when(head == 0)
    def _():
        totals[...] = jnp.zeros_like(totals)

    for index in range(SIDE):
        first = index * block
        end = first + block
        rows = slice(first, end)
        query = query_in[rows, :]
        back = jnp.concatenate(
            [
                mixed_back[block_at(where[CORES * index + side], piece), :]
                for side in range(CORES)
            ],
            axis=0,
        )
        keys = packed[:end, key_cols]
        scores = matmul_nt(query, keys) * scale
        allowed = visible(ids_q[rows, :], ids_k[:, :end], first, block, end)
        probs = jnp.where(allowed, jnp.exp(scores - lse[0, rows, :]), 0.0)
        probs_back = matmul_nt(back, packed[:end, value_cols])
        inner = jnp.sum(probs * probs_back, axis=-1, keepdims=True)
        score_back = (probs * (probs_back - inner)).astype(low_type)
        totals[:end, value_cols] += matmul_tn(probs.astype(low_type), back)
        totals[:end, key_cols] += matmul_tn(score_back, query) * scale
        query_grad = matmul(score_back, keys) * scale
        query_back[rows, :] = rotate_back(query_grad, cosine[rows, :], sine[rows, :]).astype(
            low_type
        )
    weight_back[...] = matmul_tn(packed[:, :latent_width], query_back[...]).astype(low_type)
    for index in range(SIDE):
        rows = slice(index * block, (index + 1) * block)
        totals[rows, :latent_width] += matmul_nt(query_back[rows, :], weight[...])

    @pl.when(head == pl.num_programs(0) - 1)
    def _():
        core = where[SIDE * CORES]
        for step in range(SIDE):
            near = CORES * step + core
            far = CORES * step + 1 - core
            near_out[block_at(where[near], piece), :] = totals[block_at(near, piece), :].astype(
                low_type
            )
            far_out[block_at(where[far] - SIDE, piece), :] = totals[
                block_at(far, piece), :
            ].astype(low_type)


def attend_back(where, query_rows, packed, mixed_back, lse, cosine, sine, row_ids, w_q_up):
    row_len, packed_width = packed.shape
    latent_width, width = w_q_up.shape
    head_dim = (packed_width - latent_width) // 2
    count = width // head_dim
    whole = lambda head, where: (0, 0)
    column = lambda head, where: (0, head)
    return pl.pallas_call(
        attend_back_kernel,
        grid_spec=pltpu.PrefetchScalarGridSpec(
            num_scalar_prefetch=1,
            grid=(count,),
            in_specs=[
                pl.BlockSpec((row_len, head_dim), column),
                pl.BlockSpec((row_len, packed_width), whole),
                pl.BlockSpec((row_len, head_dim), column),
                pl.BlockSpec((1, row_len, 1), lambda head, where: (head, 0, 0)),
                pl.BlockSpec((row_len, head_dim // 2), whole),
                pl.BlockSpec((row_len, head_dim // 2), whole),
                pl.BlockSpec((row_len, 1), whole),
                pl.BlockSpec((1, row_len), whole),
                pl.BlockSpec((latent_width, head_dim), column),
            ],
            out_specs=[
                pl.BlockSpec((latent_width, head_dim), column),
                pl.BlockSpec((row_len // 2, packed_width), whole),
                pl.BlockSpec((row_len // 2, packed_width), whole),
            ],
            scratch_shapes=[
                pltpu.VMEM((row_len, head_dim), low_type),
                pltpu.VMEM((row_len, packed_width), jnp.float32),
            ],
        ),
        out_shape=[
            jax.ShapeDtypeStruct((latent_width, width), low_type),
            jax.ShapeDtypeStruct((row_len // 2, packed_width), low_type),
            jax.ShapeDtypeStruct((row_len // 2, packed_width), low_type),
        ],
        compiler_params=pltpu.CompilerParams(vmem_limit_bytes=vmem_bytes),
        cost_estimate=pl.CostEstimate(
            flops=10 * width * row_len * row_len,
            bytes_accessed=8 * row_len * width,
            transcendentals=count * row_len * row_len,
        ),
        name="attend_back",
    )(
        where,
        query_rows,
        packed,
        mixed_back,
        lse,
        cosine,
        sine,
        row_ids[:, None],
        row_ids[None, :],
        w_q_up,
    )


def place_kernel(where, source, target):
    target[...] = source[...]


def place_blocks(where, rows, count):
    piece = rows.shape[0] // count
    width = rows.shape[1]
    return pl.pallas_call(
        place_kernel,
        grid_spec=pltpu.PrefetchScalarGridSpec(
            num_scalar_prefetch=1,
            grid=(count,),
            in_specs=[pl.BlockSpec((piece, width), lambda index, where: (index, 0))],
            out_specs=pl.BlockSpec((piece, width), lambda index, where: (where[index], 0)),
        ),
        out_shape=jax.ShapeDtypeStruct(rows.shape, rows.dtype),
        cost_estimate=pl.CostEstimate(
            flops=0, bytes_accessed=4 * rows.shape[0] * width, transcendentals=0
        ),
        name="place_blocks",
    )(where, rows)


def ffn_grads_kernel(features, grads, gate_back, up_back, middle, target):
    width = gate_back.shape[1]
    stride = target.shape[1] // 3
    pairs = ((features, gate_back), (features, up_back), (grads, middle))
    for index, (left, right) in enumerate(pairs):
        first = index * stride
        target[:, first : first + width] = matmul_tn(left[...], right[...]).astype(low_type)
        if stride > width:
            target[:, first + width : first + stride] = jnp.zeros(
                (target.shape[0], stride - width), low_type
            )


def ffn_grads(features, grads, gate_back, up_back, middle):
    row_len, model_width = features.shape
    width = gate_back.shape[1]
    stride = -(-width // 128) * 128
    block = model_width // 8
    whole = lambda index: (0, 0)
    column = lambda index: (0, index)
    return pl.pallas_call(
        ffn_grads_kernel,
        grid=(8,),
        in_specs=[
            pl.BlockSpec((row_len, block), column),
            pl.BlockSpec((row_len, block), column),
            pl.BlockSpec((row_len, width), whole),
            pl.BlockSpec((row_len, width), whole),
            pl.BlockSpec((row_len, width), whole),
        ],
        out_specs=pl.BlockSpec((block, 3 * stride), lambda index: (index, 0)),
        out_shape=jax.ShapeDtypeStruct((model_width, 3 * stride), low_type),
        compiler_params=pltpu.CompilerParams(vmem_limit_bytes=vmem_bytes),
        cost_estimate=pl.CostEstimate(
            flops=6 * row_len * model_width * width,
            bytes_accessed=4 * row_len * model_width + 6 * model_width * width,
            transcendentals=0,
        ),
        name="ffn_grads",
    )(features, grads, gate_back, up_back, middle)


def polish(gram, gram_low, change_low, once_low, iterate, size):
    block = min(size, 256)
    count = size // block
    for step_index in range(NS_STEPS):
        last = step_index + 1 == NS_STEPS
        if last:
            first_term = matmul(iterate.astype(low_type), gram_low[...])
            second_term = matmul(first_term.astype(low_type), gram_low[...])
            return coef_first * iterate + coef_second * first_term + coef_third * second_term

        def make_change(index, carry):
            rows = block_at(index, block)
            square = matmul(gram_low[rows, :], gram_low[...])
            change_low[rows, :] = (coef_second * gram[rows, :] + coef_third * square).astype(
                low_type
            )
            return carry

        def make_once(index, carry):
            rows = block_at(index, block)
            once = matmul(gram_low[rows, :], change_low[...])
            once_low[rows, :] = once.astype(low_type)
            gram[rows, :] = (coef_first * coef_first) * gram[rows, :] + (2.0 * coef_first) * once
            return carry

        def make_gram(index, carry):
            rows = block_at(index, block)
            total = gram[rows, :] + matmul(once_low[rows, :], change_low[...])
            gram[rows, :] = total
            gram_low[rows, :] = total.astype(low_type)
            return carry

        lax.fori_loop(0, count, make_change, 0)
        iterate = coef_first * iterate + matmul(iterate.astype(low_type), change_low[...])
        lax.fori_loop(0, count, make_once, 0)
        lax.fori_loop(0, count, make_gram, 0)


def shared_kernel(*refs):
    pieces = refs[: SIDE * CORES]
    own, target, gram, gram_low, change_low, once_low = refs[SIDE * CORES :]
    rows_each = pieces[0].shape[0] - own.shape[0]
    wide = gram.shape[0]
    narrow = (own.shape[1] - wide) // 2
    for first, size in ((0, wide), (wide, narrow), (wide + narrow, narrow)):
        cols = slice(first, first + size)
        area = (slice(0, size), slice(0, size))
        block = min(size, 256)
        trace = jnp.zeros((1, 1), jnp.float32)
        for index in range(size // block):
            rows = slice(index * block, (index + 1) * block)
            part = slice(first + index * block, first + (index + 1) * block)
            total = jnp.zeros((block, size), jnp.float32)
            for source in pieces:
                total += matmul_tn(source[:rows_each, part], source[:rows_each, cols])
            gram[rows, area[1]] = total
            row_at = index * block + lax.broadcasted_iota(jnp.int32, (block, size), 0)
            col_at = lax.broadcasted_iota(jnp.int32, (block, size), 1)
            diagonal = jnp.where(row_at == col_at, total, 0.0)
            trace += jnp.sum(jnp.sum(diagonal, axis=0, keepdims=True), axis=1, keepdims=True)
        factor = 1.0 / (jnp.sqrt(trace) + 1e-07)
        for index in range(size // block):
            rows = slice(index * block, (index + 1) * block)
            scaled = gram[rows, area[1]] * (factor * factor)
            gram[rows, area[1]] = scaled
            gram_low[rows, area[1]] = scaled.astype(low_type)
        target[:, cols] = polish(
            gram.at[area],
            gram_low.at[area],
            change_low.at[area],
            once_low.at[area],
            own[:, cols] * factor,
            size,
        )


def shared_ortho(pieces, own, wide):
    return pl.pallas_call(
        shared_kernel,
        out_shape=jax.ShapeDtypeStruct(own.shape, jnp.float32),
        scratch_shapes=[pltpu.VMEM((wide, wide), jnp.float32)]
        + [pltpu.VMEM((wide, wide), low_type)] * 3,
        compiler_params=pltpu.CompilerParams(vmem_limit_bytes=vmem_bytes),
        cost_estimate=pl.CostEstimate(
            flops=20 * wide * wide * wide, bytes_accessed=8 * wide * wide, transcendentals=0
        ),
        name="shared_ortho",
    )(*pieces, own)


def gram_of(blocks):
    low = blocks.astype(low_type)
    return jnp.einsum("brc,brd->bcd", low, low, preferred_element_type=jnp.float32)


def times(left, right):
    return jnp.einsum(
        "brc,bcd->brd",
        left.astype(low_type),
        right.astype(low_type),
        preferred_element_type=jnp.float32,
    )


def orthogonal(blocks, gram_sums):
    diagonal = jnp.eye(gram_sums.shape[-1], dtype=jnp.bool_)
    trace_sum = jnp.sum(jnp.where(diagonal, gram_sums, 0.0), axis=(1, 2))
    factor = 1.0 / (jnp.sqrt(trace_sum) + 1e-07)
    iterate = blocks * factor[:, None, None]
    gram = gram_sums * (factor * factor)[:, None, None]
    for step_index in range(NS_STEPS):
        first_term = times(iterate, gram)
        second_term = times(first_term, gram)
        iterate = coef_first * iterate + coef_second * first_term + coef_third * second_term
        if step_index + 1 < NS_STEPS:
            change = coef_second * gram + coef_third * times(gram, gram)
            once = times(gram, change)
            twice = times(once, change)
            gram = (coef_first * coef_first) * gram + (2.0 * coef_first) * once + twice
    return iterate


def split_columns(matrix, block_cols):
    row_count = matrix.shape[0]
    return matrix.reshape(row_count, matrix.shape[1] // block_cols, block_cols).transpose(1, 0, 2)


def join_columns(blocks):
    return blocks.transpose(1, 0, 2).reshape(blocks.shape[1], blocks.shape[0] * blocks.shape[2])


def own_rows(weight, count, rank):
    share_rows = weight.shape[0] // count
    return lax.dynamic_slice_in_dim(weight, rank * share_rows, share_rows, 0).astype(jnp.float32)


def on_device(
    tokens_in,
    cotangent,
    seg_starts,
    gains,
    w_q_down,
    w_key,
    w_value,
    w_q_up,
    w_out,
    w_gate,
    w_up,
    w_down,
    mom_gains,
    mom_q_down,
    mom_key,
    mom_value,
    mom_q_up,
    mom_out,
    mom_gate,
    mom_up,
    mom_down,
):
    heads_count = lax.axis_size("heads")
    heads_rank = lax.axis_index("heads")
    dp_count = lax.axis_size("dp")
    dp_rank = lax.axis_index("dp")
    all_rank = lax.axis_index(("dp", "heads"))
    all_count = dp_count * heads_count
    local_rows = tokens_in.shape[0]
    row_len = local_rows * heads_count
    half_len = row_len // 2
    model_width = tokens_in.shape[1]
    latent_width = w_q_down.shape[1]
    head_dim = w_key.shape[1]
    local_q = w_q_up.shape[1]
    local_ff = w_gate.shape[1]
    starts = seg_starts[0]
    whole_index = jnp.arange(row_len, dtype=jnp.int32)
    own_index = heads_rank * local_rows + jnp.arange(local_rows, dtype=jnp.int32)
    own_core = heads_rank % CORES
    own_step = heads_rank // CORES
    ranks = jnp.arange(heads_count, dtype=jnp.int32)
    where = SIDE * ((ranks % CORES) ^ own_core) + (ranks // CORES - own_step) % SIDE
    owner = CORES * ((ranks % SIDE + own_step) % SIDE) + ((ranks // SIDE) ^ own_core)
    where_core = jnp.concatenate([where, own_core[None].astype(jnp.int32)])
    gain_one = gains[:model_width]
    gain_latent = gains[model_width : model_width + latent_width]
    gain_two = gains[model_width + latent_width :]
    inputs = tokens_in.astype(jnp.float32)
    scale_one = rms_scale(inputs)
    normed_one = (inputs * scale_one * gain_one).astype(low_type)
    latent_raw = matmul(normed_one, w_q_down)
    scale_latent = rms_scale(latent_raw)
    latent_normed = (latent_raw * scale_latent * gain_latent).astype(low_type)
    own_pos = segment_info(starts, own_index)[1]
    own_cos, own_sin = rotary_tables(own_pos, head_dim)
    key_local = rotate(matmul(normed_one, w_key), own_cos, own_sin).astype(low_type)
    value_local = matmul(normed_one, w_value).astype(low_type)
    row_ids, row_pos = segment_info(starts, whole_index)
    row_cos, row_sin = rotary_tables(row_pos, head_dim)
    grad_gathered = lax.all_gather(cotangent, "heads", axis=0, tiled=True)
    pieces = gather_heads(jnp.concatenate([latent_normed, key_local, value_local], axis=1))
    share_rows = model_width // all_count
    normed_columns = (
        normed_one.reshape(local_rows, dp_count, heads_count, share_rows)
        .transpose(2, 0, 1, 3)
        .reshape(heads_count, local_rows, dp_count * share_rows)
    )
    normed_parts = [None] * heads_count
    for core in range(CORES):
        for step in range(SIDE):
            part = lax.dynamic_index_in_dim(
                normed_columns, owner[SIDE * core + step], 0, keepdims=False
            )
            if core or step:
                part = shift_heads(part, step, core)
            normed_parts[SIDE * core + (-step) % SIDE] = part
    normed_parts = jnp.concatenate(normed_parts, axis=0)
    pieces, normed_parts = lax.optimization_barrier((pieces, normed_parts))
    packed, query_rows, attended_near, attended_far, lse = attend(
        where_core, owner, pieces, w_q_up, head_dim, row_cos, row_sin, row_ids
    )
    grad_rows = place_blocks(where, grad_gathered, heads_count)
    attn_mixed = scatter_heads(
        matmul_nt(attended_far, w_out).astype(low_type), matmul_nt(attended_near, w_out)
    )
    hidden_one = inputs + attn_mixed
    scale_two = rms_scale(hidden_one)
    normed_two = (hidden_one * scale_two * gain_two).astype(low_type)
    ffn_input = jnp.concatenate(gather_heads(normed_two), axis=0)
    gate_raw = matmul(ffn_input, w_gate)
    up_raw = matmul(ffn_input, w_up)
    sigmoid_gate = jax.nn.sigmoid(gate_raw)
    activated = gate_raw * sigmoid_gate
    hidden_mid = (activated * up_raw).astype(low_type)
    mid_back = matmul(grad_rows, w_down)
    gate_back = (mid_back * up_raw * sigmoid_gate * (1.0 + gate_raw * (1.0 - sigmoid_gate))).astype(
        low_type
    )
    up_back = (mid_back * activated).astype(low_type)
    normed_two_back = scatter_heads(
        (matmul_nt(gate_back[half_len:], w_gate) + matmul_nt(up_back[half_len:], w_up)).astype(
            low_type
        ),
        matmul_nt(gate_back[:half_len], w_gate) + matmul_nt(up_back[:half_len], w_up),
    )
    ffn_sums = lax.psum_scatter(
        ffn_grads(ffn_input, grad_rows, gate_back, up_back, hidden_mid),
        "dp",
        scatter_dimension=0,
        tiled=True,
    ).astype(jnp.float32)
    hidden_part, gain_two_grad = norm_back(hidden_one, scale_two, gain_two, normed_two_back)
    hidden_back = cotangent.astype(jnp.float32) + hidden_part
    hidden_rows = jnp.concatenate(gather_heads(hidden_back.astype(low_type)), axis=0)
    attended_back = matmul(hidden_rows, w_out).astype(low_type)
    out_w_part = matmul_tn(
        hidden_rows, jnp.concatenate([attended_near, attended_far], axis=0)
    ).astype(low_type)
    q_up_part, sums_near, sums_far = attend_back(
        where_core, query_rows, packed, attended_back, lse, row_cos, row_sin, row_ids, w_q_up
    )
    packed_sums = scatter_heads(sums_far, sums_near)
    head_sums = scatter_dp(
        jnp.concatenate(
            [
                q_up_part.reshape(dp_count, -1, local_q),
                out_w_part.reshape(dp_count, -1, local_q),
            ],
            axis=1,
        )
    )
    q_up_rows = w_q_up.shape[0] // dp_count
    q_up_grad = head_sums[:q_up_rows]
    out_w_grad = head_sums[q_up_rows:]
    latent_back = packed_sums[:, :latent_width]
    key_sum = packed_sums[:, latent_width : latent_width + head_dim]
    value_sum = packed_sums[:, latent_width + head_dim :]
    latent_raw_grad, gain_latent_grad = norm_back(
        latent_raw, scale_latent, gain_latent, latent_back
    )
    latent_raw_back = latent_raw_grad.astype(low_type)
    key_pre_back = rotate_back(key_sum, own_cos, own_sin).astype(low_type)
    values_low = value_sum.astype(low_type)
    packed_back = jnp.concatenate(
        gather_heads(jnp.concatenate([latent_raw_back, key_pre_back, values_low], axis=1)), axis=0
    )
    shared_part = matmul_tn(normed_parts, packed_back).astype(low_type)
    ffn_stride = ffn_sums.shape[1] // 3
    gate_w_grad = ffn_sums[:, :local_ff]
    up_w_grad = ffn_sums[:, ffn_stride : ffn_stride + local_ff]
    down_w_grad = ffn_sums[:, 2 * ffn_stride : 2 * ffn_stride + local_ff]
    gate_w_mom = decay_rate * mom_gate + gate_w_grad
    up_w_mom = decay_rate * mom_up + up_w_grad
    down_w_mom = decay_rate * mom_down + down_w_grad
    ffn_count = w_gate.shape[1] // FF_BLOCK
    ffn_blocks = jnp.concatenate(
        [
            split_columns(gate_w_mom, FF_BLOCK),
            split_columns(up_w_mom, FF_BLOCK),
            split_columns(down_w_mom, FF_BLOCK),
        ],
        axis=0,
    )
    ffn_gram = gram_of(ffn_blocks).astype(low_type)
    normed_one_back = (
        matmul_nt(latent_raw_back, w_q_down)
        + matmul_nt(key_pre_back, w_key)
        + matmul_nt(values_low, w_value)
    )
    input_part, gain_one_grad = norm_back(inputs, scale_one, gain_one, normed_one_back)
    input_grad = hidden_back + input_part
    share_gains = gains.shape[0] // all_count
    gains_part = jnp.concatenate([gain_one_grad, gain_latent_grad, gain_two_grad])
    gains_part = gains_part.reshape(dp_count, heads_count, share_gains).astype(low_type)
    gains_part = jnp.pad(
        gains_part, ((0, 0), (0, share_rows - heads_count), (0, 128 - share_gains))
    )
    mixed_far = matmul_nt(hidden_mid[half_len:], w_down).astype(low_type)
    mixed_near = matmul_nt(hidden_mid[:half_len], w_down).astype(low_type)
    shared_part, ffn_gram, mixed_far, mixed_near = lax.optimization_barrier(
        (shared_part, ffn_gram, mixed_far, mixed_near)
    )
    ffn_gram = lax.psum(ffn_gram, "dp").astype(jnp.float32)
    packed_width = shared_part.shape[1]
    shared_grad = scatter_dp(
        jnp.concatenate(
            [shared_part.reshape(dp_count, share_rows, packed_width), gains_part], axis=2
        )
    )
    layer_out = (hidden_one + scatter_heads(mixed_far, mixed_near)).astype(low_type)
    q_down_grad = shared_grad[:, :latent_width]
    key_w_grad = shared_grad[:, latent_width : latent_width + head_dim]
    value_w_grad = shared_grad[:, latent_width + head_dim : packed_width]
    q_down_mom = decay_rate * mom_q_down + q_down_grad
    key_w_mom = decay_rate * mom_key + key_w_grad
    value_w_mom = decay_rate * mom_value + value_w_grad
    shared_mom = jnp.concatenate([q_down_mom, key_w_mom, value_w_mom], axis=1)
    gains_rows = jnp.pad(
        shared_grad[:, packed_width : packed_width + share_gains],
        ((0, 0), (0, packed_width - share_gains)),
    )
    mom_pieces = gather_heads(
        jnp.concatenate(
            [gather_dp(shared_mom.astype(low_type)), gains_rows.astype(low_type)], axis=0
        )
    )
    gains_grad = sum(
        lax.dynamic_index_in_dim(
            piece[dp_count * share_rows :, :share_gains], heads_rank, 0, keepdims=False
        ).astype(jnp.float32)
        for piece in mom_pieces
    )
    shared_done = shared_ortho(mom_pieces, shared_mom, latent_width)
    gains_mom = decay_rate * mom_gains + gains_grad
    q_up_mom = decay_rate * mom_q_up + q_up_grad
    out_w_mom = decay_rate * mom_out + out_w_grad
    gains_new = own_rows(gains, all_count, all_rank) - gain_rate * gains_mom
    ffn_ortho = orthogonal(ffn_blocks, ffn_gram)
    query_blocks = split_columns(q_up_mom, head_dim)
    output_blocks = split_columns(out_w_mom, head_dim)
    head_grams = jnp.concatenate([gram_of(query_blocks), gram_of(output_blocks)], axis=0)
    gram_rows = head_dim // dp_count
    head_count = query_blocks.shape[0]
    head_grams = (
        head_grams.astype(low_type)
        .reshape(2 * head_count, dp_count, gram_rows, head_dim)
        .transpose(1, 0, 2, 3)
        .reshape(dp_count, 2 * head_count * gram_rows, head_dim)
    )
    head_grams = scatter_dp(head_grams).astype(low_type)
    place_z = dp_rank // SIDE
    place_x = dp_rank % SIDE
    head_grams = gather_dp(head_grams[None])
    head_grams = head_grams.reshape(SIDE, SIDE, 2 * head_count, gram_rows, head_dim)
    order_z = (place_z - jnp.arange(SIDE)) % SIDE
    order_x = (place_x - jnp.arange(SIDE)) % SIDE
    head_grams = jnp.concatenate(
        [lax.dynamic_index_in_dim(head_grams, order_z[z], 0) for z in range(SIDE)], axis=0
    )
    head_grams = jnp.concatenate(
        [lax.dynamic_index_in_dim(head_grams, order_x[x], 1) for x in range(SIDE)], axis=1
    )
    head_grams = head_grams.transpose(2, 0, 1, 3, 4).reshape(2 * head_count, head_dim, head_dim)
    head_grams = head_grams.astype(jnp.float32)
    query_ortho = orthogonal(query_blocks, head_grams[:head_count])
    output_ortho = orthogonal(output_blocks, head_grams[head_count:])
    q_up_new = own_rows(w_q_up, dp_count, dp_rank) - muon_rate * math.sqrt(
        w_q_up.shape[0] / head_dim
    ) * join_columns(query_ortho)
    out_w_new = own_rows(w_out, dp_count, dp_rank) - muon_rate * math.sqrt(
        w_out.shape[0] / head_dim
    ) * join_columns(output_ortho)
    ffn_factor = muon_rate * math.sqrt(w_gate.shape[0] / FF_BLOCK)
    gate_w_new = own_rows(w_gate, dp_count, dp_rank) - ffn_factor * join_columns(
        ffn_ortho[:ffn_count]
    )
    up_w_new = own_rows(w_up, dp_count, dp_rank) - ffn_factor * join_columns(
        ffn_ortho[ffn_count : 2 * ffn_count]
    )
    down_w_new = own_rows(w_down, dp_count, dp_rank) - ffn_factor * join_columns(
        ffn_ortho[2 * ffn_count :]
    )
    q_down_new = (
        own_rows(w_q_down, all_count, all_rank)
        - muon_rate * math.sqrt(w_q_down.shape[0] / latent_width) * shared_done[:, :latent_width]
    )
    pair_factor = muon_rate * math.sqrt(w_key.shape[0] / head_dim)
    key_w_new = own_rows(w_key, all_count, all_rank) - pair_factor * shared_done[:, latent_width : latent_width + head_dim]
    value_w_new = own_rows(w_value, all_count, all_rank) - pair_factor * shared_done[:, latent_width + head_dim :]
    return (
        layer_out,
        input_grad,
        gains_grad,
        q_down_grad,
        key_w_grad,
        value_w_grad,
        q_up_grad,
        out_w_grad,
        gate_w_grad,
        up_w_grad,
        down_w_grad,
        gains_mom,
        q_down_mom,
        key_w_mom,
        value_w_mom,
        q_up_mom,
        out_w_mom,
        gate_w_mom,
        up_w_mom,
        down_w_mom,
        gains_new,
        q_down_new,
        key_w_new,
        value_w_new,
        q_up_new,
        out_w_new,
        gate_w_new,
        up_w_new,
        down_w_new,
    )


def solution(mesh):
    placed = (
        P(("dp", "heads"), None),
        P(("dp", "heads"), None),
        P("dp", None),
        P(),
        P(),
        P(),
        P(),
        P(None, "heads"),
        P(None, "heads"),
        P(None, "heads"),
        P(None, "heads"),
        P(None, "heads"),
        P(("dp", "heads")),
        P(("dp", "heads"), None),
        P(("dp", "heads"), None),
        P(("dp", "heads"), None),
        P("dp", "heads"),
        P("dp", "heads"),
        P("dp", "heads"),
        P("dp", "heads"),
        P("dp", "heads"),
    )
    return jax.shard_map(
        on_device,
        mesh=mesh,
        in_specs=placed,
        out_specs=(
            P(("dp", "heads"), None),
            P(("dp", "heads"), None),
            P(("dp", "heads")),
            P(("dp", "heads"), None),
            P(("dp", "heads"), None),
            P(("dp", "heads"), None),
            P("dp", "heads"),
            P("dp", "heads"),
            P("dp", "heads"),
            P("dp", "heads"),
            P("dp", "heads"),
            P(("dp", "heads")),
            P(("dp", "heads"), None),
            P(("dp", "heads"), None),
            P(("dp", "heads"), None),
            P("dp", "heads"),
            P("dp", "heads"),
            P("dp", "heads"),
            P("dp", "heads"),
            P("dp", "heads"),
            P(("dp", "heads")),
            P(("dp", "heads"), None),
            P(("dp", "heads"), None),
            P(("dp", "heads"), None),
            P("dp", "heads"),
            P("dp", "heads"),
            P("dp", "heads"),
            P("dp", "heads"),
            P("dp", "heads"),
        ),
        check_vma=False,
    )
```

```python
import math

import jax
import jax.numpy as jnp
from jax import lax
from jax.experimental import pallas as pl
from jax.experimental.pallas import tpu as pltpu
from jax.sharding import PartitionSpec as P

NS_STEPS = 3
FF_BLOCK = 352
SIDE = 4
CORES = 2
LANES = 128

coef_first = 3.4445
coef_second = -4.775
coef_third = 2.0315
muon_rate = 0.5
gain_rate = 0.004
decay_rate = 0.5
low_type = jnp.bfloat16


def matmul(left, right):
    return jnp.dot(left, right, preferred_element_type=jnp.float32)


def matmul_nt(left, right):
    return lax.dot_general(
        left, right, (((1,), (1,)), ((), ())), preferred_element_type=jnp.float32
    )


def matmul_tn(left, right):
    return lax.dot_general(
        left, right, (((0,), (0,)), ((), ())), preferred_element_type=jnp.float32
    )


def rms_scale(values):
    return lax.rsqrt(jnp.mean(values * values, axis=-1, keepdims=True) + 1e-05)


def norm_back(values, scale, gain, grad_out):
    weighted = gain * grad_out
    inner = jnp.mean(values * weighted, axis=-1, keepdims=True)
    grad_in = scale * weighted - values * (scale * scale * scale) * inner
    gain_grad = jnp.sum(grad_out * values * scale, axis=0)
    return (grad_in, gain_grad)


def segment_info(starts, token_index):
    started = starts[None, :] <= token_index[:, None]
    seg_ids = jnp.sum(started.astype(jnp.int32), axis=1)
    seg_begin = jnp.max(jnp.where(started, starts[None, :], 0), axis=1)
    return (seg_ids, token_index - seg_begin)


def rotary_tables(positions, head_dim):
    half_dim = head_dim // 2
    frequency = jnp.exp(
        jnp.arange(half_dim, dtype=jnp.float32) * (-2.0 * math.log(10000.0) / head_dim)
    )
    angles = positions.astype(jnp.float32)[:, None] * frequency[None, :]
    return (jnp.cos(angles), jnp.sin(angles))


def rotate(values, cosine, sine_part):
    half_dim = values.shape[-1] // 2
    first_half = values[..., :half_dim]
    second_half = values[..., half_dim:]
    return jnp.concatenate(
        [
            first_half * cosine - second_half * sine_part,
            second_half * cosine + first_half * sine_part,
        ],
        axis=-1,
    )


def rotate_back(grads, cosine, sine_part):
    return rotate(grads, cosine, -sine_part)


def shift_heads(values, step, core):
    pairs = [
        (CORES * place + side, CORES * ((place + step) % SIDE) + (side ^ core))
        for place in range(SIDE)
        for side in range(CORES)
    ]
    return lax.ppermute(values, "heads", pairs)


def shift_dp(values, step_z, step_x):
    pairs = [
        (SIDE * z + x, SIDE * ((z + step_z) % SIDE) + (x + step_x) % SIDE)
        for z in range(SIDE)
        for x in range(SIDE)
    ]
    return lax.ppermute(values, "dp", pairs)


def gather_heads(own):
    ring = [own] + [shift_heads(own, -step, 0) for step in range(1, SIDE)]
    return ring + [shift_heads(piece, 0, 1) for piece in ring]


def chip_sums(far_half, near_half):
    rows = near_half.shape[0] // SIDE
    total = near_half.astype(jnp.float32) + shift_heads(far_half, 0, 1).astype(jnp.float32)
    return total.astype(far_half.dtype).reshape(SIDE, rows, *near_half.shape[1:])


def ring_sums(chip):
    total = chip[0].astype(jnp.float32)
    for step in range(1, SIDE):
        total = total + shift_heads(chip[step], step, 0).astype(jnp.float32)
    return total


def pick(array, place, axis):
    return lax.dynamic_index_in_dim(array, place % SIDE, axis, keepdims=False)


def scatter_x(parts):
    place_x = lax.axis_index("dp") % SIDE
    grid = parts.reshape(SIDE, SIDE, *parts.shape[1:])
    total = pick(grid, place_x, 1).astype(jnp.float32)
    for step in range(1, SIDE):
        total = total + shift_dp(pick(grid, place_x + step, 1), 0, step).astype(jnp.float32)
    return total.astype(parts.dtype)


def scatter_z(column):
    place_z = lax.axis_index("dp") // SIDE
    total = pick(column, place_z, 0).astype(jnp.float32)
    for step in range(1, SIDE):
        total = total + shift_dp(pick(column, place_z + step, 0), step, 0).astype(jnp.float32)
    return total


def sum_dp(part):
    for axis in range(2):
        total = part.astype(jnp.float32)
        for step in range(1, SIDE):
            total = total + shift_dp(part, step * axis, step * (1 - axis)).astype(jnp.float32)
        part = total.astype(part.dtype)
    return part


def gather_dp(own):
    ring = jnp.concatenate([own] + [shift_dp(own, 0, step) for step in range(1, SIDE)], axis=0)
    return [ring] + [shift_dp(ring, step, 0) for step in range(1, SIDE)]


def after(values, *earlier):
    return lax.optimization_barrier((values, *earlier))[0]


vmem_mib = {
    "attend": 18,
    "attend_back": 30,
    "ffn_near": 30,
    "ffn_far": 30,
    "ffn_grads": 20,
    "shared_ortho": 28,
}


def kernel_call(body, name, grid, prefetch, in_specs, out_specs, out_shape, scratch, flops, moved):
    return pl.pallas_call(
        body,
        grid_spec=pltpu.PrefetchScalarGridSpec(
            num_scalar_prefetch=prefetch,
            grid=grid,
            in_specs=in_specs,
            out_specs=out_specs,
            scratch_shapes=scratch,
        ),
        out_shape=out_shape,
        compiler_params=pltpu.CompilerParams(vmem_limit_bytes=vmem_mib.get(name, 16) * 1024 * 1024),
        cost_estimate=pl.CostEstimate(flops=flops, bytes_accessed=moved, transcendentals=0),
        name=name,
    )


def shaped(shape, kind):
    return jax.ShapeDtypeStruct(shape, kind)


def fixed(shape):
    return pl.BlockSpec(
        shape, lambda *grid: (0,) * len(shape), pipeline_mode=pl.Buffered(buffer_count=1)
    )


def visible(ids_q, ids_k, first_row, rows, cols):
    query_at = first_row + lax.broadcasted_iota(jnp.int32, (rows, cols), 0)
    key_at = lax.broadcasted_iota(jnp.int32, (rows, cols), 1)
    return (ids_q == ids_k) & (key_at <= query_at)


def block_at(index, piece):
    return pl.ds(pl.multiple_of(index * piece, piece), piece)


def store_by_distance(where, rows_ref, near_ref, far_ref, piece):
    core = where[SIDE * CORES]
    for step in range(SIDE):
        near = CORES * step + core
        far = CORES * step + 1 - core
        near_ref[block_at(where[near], piece), :] = rows_ref[block_at(near, piece), :].astype(
            near_ref.dtype
        )
        far_ref[block_at(where[far] - SIDE, piece), :] = rows_ref[block_at(far, piece), :].astype(
            far_ref.dtype
        )


def attend_kernel(
    where, packed, weight, cosine, sine, ids_q, ids_k, query_out, near_out, far_out, lse_out, mixed
):
    latent_width, head_dim = weight.shape
    piece = packed.shape[0] // (SIDE * CORES)
    block = CORES * piece
    scale = head_dim ** (-0.5)
    key_cols = slice(latent_width, latent_width + head_dim)
    value_cols = slice(latent_width + head_dim, latent_width + 2 * head_dim)
    for index in range(SIDE):
        first = index * block
        end = first + block
        rows = slice(first, end)
        query = matmul(packed[rows, :latent_width], weight[...])
        query = rotate(query, cosine[rows, :], sine[rows, :]).astype(low_type)
        query_out[rows, :] = query
        scores = matmul_nt(query, packed[:end, key_cols]) * scale
        allowed = visible(ids_q[rows, :], ids_k[:, :end], first, block, end)
        scores = jnp.where(allowed, scores, -1e30)
        row_max = jnp.max(scores, axis=-1, keepdims=True)
        exponent = jnp.exp(scores - row_max)
        row_total = jnp.sum(exponent, axis=-1, keepdims=True)
        probs = (exponent * (1.0 / row_total)).astype(low_type)
        lse_out[0, rows, :] = row_max + jnp.log(row_total)
        mixed[rows, :] = matmul(probs, packed[:end, value_cols]).astype(low_type)
    store_by_distance(where, mixed, near_out, far_out, piece)


def attend(where, packed, w_q_up, head_dim, cosine, sine, row_ids):
    row_len, packed_width = packed.shape
    latent_width, width = w_q_up.shape
    count = width // head_dim
    column = lambda head, where: (0, head)
    return kernel_call(
        attend_kernel,
        "attend",
        (count,),
        1,
        [
            fixed((row_len, packed_width)),
            pl.BlockSpec((latent_width, head_dim), column),
            fixed((row_len, head_dim // 2)),
            fixed((row_len, head_dim // 2)),
            fixed((row_len, 1)),
            fixed((1, row_len)),
        ],
        [
            pl.BlockSpec((row_len, head_dim), column),
            pl.BlockSpec((row_len // 2, head_dim), column),
            pl.BlockSpec((row_len // 2, head_dim), column),
            pl.BlockSpec((1, row_len, 1), lambda head, where: (head, 0, 0)),
        ],
        [
            shaped((row_len, width), low_type),
            shaped((row_len // 2, width), low_type),
            shaped((row_len // 2, width), low_type),
            shaped((count, row_len, 1), jnp.float32),
        ],
        [pltpu.VMEM((row_len, head_dim), low_type)],
        2 * width * row_len * (latent_width + 2 * row_len),
        8 * row_len * width,
    )(where, packed, w_q_up, cosine, sine, row_ids[:, None], row_ids[None, :])


def attend_back_kernel(where, *refs):
    pieces = refs[: SIDE * CORES]
    query_in, packed, w_out, weight, lse, cosine, sine, ids_q, ids_k = refs[
        SIDE * CORES : SIDE * CORES + 9
    ]
    weight_back, near_out, far_out, query_back, back_rows, totals = refs[SIDE * CORES + 9 :]
    row_len = packed.shape[0]
    latent_width, head_dim = weight.shape
    piece = row_len // (SIDE * CORES)
    block = CORES * piece
    scale = head_dim ** (-0.5)
    head = pl.program_id(0)
    key_cols = slice(latent_width, latent_width + head_dim)
    value_cols = slice(latent_width + head_dim, latent_width + 2 * head_dim)

    @pl.when(head == 0)
    def _():
        totals[...] = jnp.zeros_like(totals)

    for index in range(0, SIDE * CORES, 2):
        pair = jnp.concatenate([pieces[index][...], pieces[index + 1][...]], axis=0)
        back_rows[index * piece : (index + 2) * piece, :] = matmul(pair, w_out[...]).astype(
            low_type
        )
    for index in range(SIDE):
        first = index * block
        end = first + block
        rows = slice(first, end)
        query = query_in[rows, :]
        back = jnp.concatenate(
            [
                back_rows[block_at(where[CORES * index + side], piece), :]
                for side in range(CORES)
            ],
            axis=0,
        )
        keys = packed[:end, key_cols]
        scores = matmul_nt(query, keys) * scale
        allowed = visible(ids_q[rows, :], ids_k[:, :end], first, block, end)
        probs = jnp.where(allowed, jnp.exp(scores - lse[0, rows, :]), 0.0)
        probs_back = matmul_nt(back, packed[:end, value_cols])
        inner = jnp.sum(probs * probs_back, axis=-1, keepdims=True)
        score_back = (probs * (probs_back - inner)).astype(low_type)
        totals[:end, value_cols] += matmul_tn(probs.astype(low_type), back)
        totals[:end, key_cols] += matmul_tn(score_back, query) * scale
        query_grad = matmul(score_back, keys) * scale
        query_back[rows, :] = rotate_back(query_grad, cosine[rows, :], sine[rows, :]).astype(
            low_type
        )
        totals[rows, :latent_width] += matmul_nt(query_back[rows, :], weight[...])
    weight_back[...] = matmul_tn(packed[:, :latent_width], query_back[...]).astype(low_type)

    @pl.when(head == pl.num_programs(0) - 1)
    def _():
        store_by_distance(where, totals, near_out, far_out, piece)


def attend_back(where, pieces, query_rows, packed, w_out, w_q_up, lse, cosine, sine, row_ids):
    row_len, packed_width = packed.shape
    latent_width, width = w_q_up.shape
    model_width = w_out.shape[0]
    head_dim = (packed_width - latent_width) // 2
    count = width // head_dim
    column = lambda head, where: (0, head)
    return kernel_call(
        attend_back_kernel,
        "attend_back",
        (count,),
        1,
        [fixed(pieces[0].shape)] * len(pieces)
        + [
            pl.BlockSpec((row_len, head_dim), column),
            fixed((row_len, packed_width)),
            pl.BlockSpec((model_width, head_dim), column),
            pl.BlockSpec((latent_width, head_dim), column),
            pl.BlockSpec((1, row_len, 1), lambda head, where: (head, 0, 0)),
            fixed((row_len, head_dim // 2)),
            fixed((row_len, head_dim // 2)),
            fixed((row_len, 1)),
            fixed((1, row_len)),
        ],
        [
            pl.BlockSpec((latent_width, head_dim), column),
            fixed((row_len // 2, packed_width)),
            fixed((row_len // 2, packed_width)),
        ],
        [
            shaped((latent_width, width), low_type),
            shaped((row_len // 2, packed_width), low_type),
            shaped((row_len // 2, packed_width), low_type),
        ],
        [
            pltpu.VMEM((row_len, head_dim), low_type),
            pltpu.VMEM((row_len, head_dim), low_type),
            pltpu.VMEM((row_len, packed_width), jnp.float32),
        ],
        2 * width * row_len * (5 * row_len + model_width + 2 * latent_width),
        8 * row_len * width,
    )(
        where,
        *pieces,
        query_rows,
        packed,
        w_out,
        w_q_up,
        lse,
        cosine,
        sine,
        row_ids[:, None],
        row_ids[None, :],
    )


def ffn_kernel(owner, *refs):
    pieces = refs[:SIDE]
    grads = refs[SIDE : 2 * SIDE]
    w_gate, w_up, w_down = refs[2 * SIDE : 2 * SIDE + 3]
    gate_out, up_out, middle_out, features_back = refs[2 * SIDE + 3 :]
    piece = pieces[0].shape[0]
    for index in range(0, SIDE, 2):
        cols = slice(index * piece, (index + 2) * piece)
        pair = jnp.concatenate([pieces[index][...], pieces[index + 1][...]], axis=0)
        grad_pair = jnp.concatenate([grads[index][...], grads[index + 1][...]], axis=0)
        gate = matmul_nt(w_gate[...], pair)
        up = matmul_nt(w_up[...], pair)
        middle_back = matmul_nt(w_down[...], grad_pair)
        sigmoid = jax.nn.sigmoid(gate)
        activated = gate * sigmoid
        gate_back = (middle_back * up * sigmoid * (1.0 + gate * (1.0 - sigmoid))).astype(low_type)
        up_back = (middle_back * activated).astype(low_type)
        middle_out[:, cols] = (activated * up).astype(low_type)
        gate_out[:, cols] = gate_back
        up_out[:, cols] = up_back
        features_back[cols, :] = (
            matmul_tn(gate_back, w_gate[...]) + matmul_tn(up_back, w_up[...])
        ).astype(low_type)


def ffn_half(owner, pieces, grads, w_gate, w_up, w_down, far):
    piece, model_width = pieces[0].shape
    width = w_gate.shape[0]
    rows = SIDE * piece
    grad_specs = [
        pl.BlockSpec(
            (piece, model_width),
            lambda index, owner, place=SIDE * far + step: (owner[place], 0),
            pipeline_mode=pl.Buffered(buffer_count=1),
        )
        for step in range(SIDE)
    ]
    return kernel_call(
        ffn_kernel,
        "ffn_far" if far else "ffn_near",
        (1,),
        1,
        [fixed((piece, model_width))] * SIDE + grad_specs + [fixed((width, model_width))] * 3,
        [fixed((width, rows))] * 3 + [fixed((rows, model_width))],
        [shaped((width, rows), low_type)] * 3 + [shaped((rows, model_width), low_type)],
        [],
        10 * rows * model_width * width,
        6 * model_width * width + 6 * rows * model_width,
    )(owner, *pieces, *([grads] * SIDE), w_gate, w_up, w_down)


def ffn_grads_kernel(owner, *refs):
    count = SIDE * CORES
    pieces, grads, halves, target = refs[:count], refs[count : 2 * count], refs[-7:-1], refs[-1]
    width, half_rows = halves[0].shape
    share = target.shape[2]
    features = jnp.concatenate([source[...] for source in pieces], axis=0)
    grads = jnp.concatenate([source[...] for source in grads], axis=0)
    for index, right in enumerate((features, features, grads)):
        total = matmul(halves[index][...], right[:half_rows, :])
        total += matmul(halves[index + 3][...], right[half_rows:, :])
        total = total.astype(low_type)
        for place in range(target.shape[0]):
            target[place, index * width : (index + 1) * width, :] = total[
                :, place * share : (place + 1) * share
            ]


def ffn_grads(owner, pieces, grads, halves, dp_count):
    piece, model_width = pieces[0].shape
    row_len = grads.shape[0]
    width = halves[0].shape[0]
    block = model_width // 8
    share = model_width // dp_count
    return kernel_call(
        ffn_grads_kernel,
        "ffn_grads",
        (8,),
        1,
        [pl.BlockSpec((piece, block), lambda index, owner: (0, index))] * len(pieces)
        + [
            pl.BlockSpec((piece, block), lambda index, owner, place=place: (owner[place], index))
            for place in range(len(pieces))
        ]
        + [fixed(halves[0].shape)] * 6,
        pl.BlockSpec((block // share, 3 * width, share), lambda index, owner: (index, 0, 0)),
        shaped((dp_count, 3 * width, share), low_type),
        [],
        6 * row_len * model_width * width,
        4 * row_len * model_width + 6 * model_width * width,
    )(owner, *pieces, *([grads] * len(pieces)), *halves)


def joined_tn(left, right, steps, name):
    piece, width = left[0].shape
    block = width // steps
    count = len(left)
    cols = right[0].shape[1]
    rows = piece * count

    def body(*refs):
        left, right, target = refs[:count], refs[count:-1], refs[-1]
        left = jnp.concatenate([source[...] for source in left], axis=0)
        right = jnp.concatenate([source[...] for source in right], axis=0)
        target[...] = matmul_tn(left, right).astype(target.dtype)

    return kernel_call(
        body,
        name,
        (steps,),
        0,
        [pl.BlockSpec((piece, block), lambda index: (0, index))] * count
        + [fixed(source.shape) for source in right],
        pl.BlockSpec((block, cols), lambda index: (index, 0)),
        shaped((width, cols), low_type),
        [],
        2 * rows * width * cols,
        2 * rows * (width + cols) + 2 * width * cols,
    )(*left, *right)


def joined(owner, left, right, name):
    count = len(right)
    width = left.shape[0] // count
    piece, cols = right[0].shape

    def body(owner, *refs):
        left, right, target = refs[:count], refs[count:-1], refs[-1]
        left = jnp.concatenate([source[...] for source in left], axis=1)
        right = jnp.concatenate([source[...] for source in right], axis=0)
        target[...] = matmul(left, right).astype(target.dtype)

    return kernel_call(
        body,
        name,
        (1,),
        1,
        [
            pl.BlockSpec((width, piece), lambda index, owner, place=place: (owner[place], 0))
            for place in range(count)
        ]
        + [fixed(source.shape) for source in right],
        fixed((width, cols)),
        shaped((width, cols), low_type),
        [],
        2 * piece * count * width * cols,
        2 * piece * count * (width + cols) + 2 * width * cols,
    )(owner, *([left] * count), *right)


def panel_places(block):
    panel = min(block, LANES)
    count = -(-block // panel)
    return panel, count, upper_blocks(count)


def upper_blocks(count):
    return [(row, col) for row in range(count) for col in range(row, count)]


def momentum_kernel(spans, block, turned, *refs):
    count = len(spans)
    sums, moms = refs[0], refs[1 : 1 + count]
    grad_out, mom_out = refs[1 + count : 1 + 2 * count], refs[1 + 2 * count : 1 + 3 * count]
    gram_out = refs[-1]
    panel, tiles, places = panel_places(block)
    place = 0
    for index, (row_at, rows) in enumerate(spans):
        grad = sums[row_at : row_at + rows, :].astype(jnp.float32)
        new = decay_rate * moms[index][...] + grad
        grad_out[index][...] = grad
        mom_out[index][...] = new
        low = new.astype(low_type)
        for first in range(0, low.shape[0 if turned else 1], block):
            if turned:
                part = low[first : first + block, :]
                if tiles * panel > block:
                    blank = jnp.zeros((tiles * panel - block, part.shape[1]), low_type)
                    part = jnp.concatenate([part, blank], axis=0)
                gram = matmul_nt(part, part).astype(low_type)
            else:
                part = low[:, first : first + block]
                gram = matmul_tn(part, part).astype(low_type)
            for row, col in places:
                gram_out[place * panel : (place + 1) * panel, :] = gram[
                    row * panel : (row + 1) * panel, col * panel : (col + 1) * panel
                ]
                place += 1


def momenta(sums, moms, block, turned, name):
    axis = 0 if turned else 1
    blocks = sum(mom.shape[axis] // block for mom in moms)
    panel, tiles, places = panel_places(block)
    spans, row_at = [], 0
    for mom in moms:
        spans.append((row_at, mom.shape[0]))
        row_at += mom.shape[0]

    def body(*refs):
        momentum_kernel(spans, block, turned, *refs)

    shapes = [mom.shape for mom in moms]
    panels = (blocks * len(places) * panel, panel)
    results = kernel_call(
        body,
        name,
        (1,),
        0,
        [fixed(sums.shape)] + [fixed(shape) for shape in shapes],
        [fixed(shape) for shape in shapes + shapes] + [fixed(panels)],
        [shaped(shape, jnp.float32) for shape in shapes + shapes] + [shaped(panels, low_type)],
        [],
        2 * block * sum(shape[0] * shape[1] for shape in shapes),
        16 * sum(shape[0] * shape[1] for shape in shapes),
    )(sums, *moms)
    count = len(moms)
    return results[:count], results[count : 2 * count], results[-1]


def trace_of(gram):
    rows = lax.broadcasted_iota(jnp.int32, gram.shape, 0)
    cols = lax.broadcasted_iota(jnp.int32, gram.shape, 1)
    diagonal = jnp.where(rows == cols, gram, 0.0)
    return jnp.sum(jnp.sum(diagonal, axis=0, keepdims=True), axis=1, keepdims=True)


def polish_small(gram, block, turned=False):
    def apply(values, right):
        values = values.astype(low_type)
        return matmul(right, values) if turned else matmul(values, right)

    factor = 1.0 / (jnp.sqrt(trace_of(gram)) + 1e-07)
    iterate = block * factor
    gram = gram * (factor * factor)
    for step_index in range(NS_STEPS):
        gram_low = gram.astype(low_type)
        if step_index + 1 == NS_STEPS:
            first_term = apply(iterate, gram_low)
            second_term = apply(first_term, gram_low)
            return coef_first * iterate + coef_second * first_term + coef_third * second_term
        change = (coef_second * gram + coef_third * matmul(gram_low, gram_low)).astype(low_type)
        iterate = coef_first * iterate + apply(iterate, change)
        once = matmul(gram_low, change)
        twice = matmul(once.astype(low_type), change)
        gram = (coef_first * coef_first) * gram + (2.0 * coef_first) * once + twice


def update_kernel(block, turned, rates, origin, *refs):
    count = len(rates)
    flat = refs[-1]
    sources = refs[: -1 - 3 * count]
    moms, weights = refs[-1 - 3 * count : -1 - 2 * count], refs[-1 - 2 * count : -1 - count]
    targets = refs[-1 - count : -1]
    panel, tiles, places = panel_places(block)
    if len(sources) == 1:
        flat = sources[0]
    else:
        chunk = sources[0].shape[0] // SIDE
        for index, source in enumerate(sources):
            for part in range(SIDE):
                flat[block_at(origin[1 + SIDE * index + part], chunk), :] = source[
                    part * chunk : (part + 1) * chunk, :
                ]
    place = 0
    for index, rate in enumerate(rates):
        for first in range(0, moms[index].shape[0 if turned else 1], block):
            parts = {}
            for row, col in places:
                parts[row, col] = flat[place * panel : (place + 1) * panel, :].astype(jnp.float32)
                if row != col:
                    parts[col, row] = parts[row, col].T
                place += 1
            gram = jnp.concatenate(
                [
                    jnp.concatenate([parts[row, col] for col in range(tiles)], axis=1)
                    for row in range(tiles)
                ],
                axis=0,
            )
            part = slice(first, first + block)
            area = (part, slice(None)) if turned else (slice(None), part)
            start = moms[index][area]
            if turned and tiles * panel > block:
                blank = jnp.zeros((tiles * panel - block, start.shape[1]), jnp.float32)
                start = jnp.concatenate([start, blank], axis=0)
            ortho = polish_small(gram, start, turned)
            if turned:
                ortho = ortho[:block, :]
            targets[index][area] = weights[index][area].astype(jnp.float32) - rate * ortho


def updates(origin, panels, moms, weights, block, turned, name):
    axis = 1 if turned else 0
    rates = [muon_rate * math.sqrt(weight.shape[axis] / block) for weight in weights]

    def body(origin, *refs):
        update_kernel(block, turned, rates, origin, *refs)

    shapes = [mom.shape for mom in moms]
    where_own = (
        (lambda index, origin: (0, origin[0])) if turned else (lambda index, origin: (origin[0], 0))
    )
    rows = sum(source.shape[0] for source in panels)
    panel = panels[0].shape[1]
    return kernel_call(
        body,
        name,
        (1,),
        1,
        [fixed(source.shape) for source in panels]
        + [fixed(shape) for shape in shapes]
        + [pl.BlockSpec(shape, where_own) for shape in shapes],
        [fixed(shape) for shape in shapes],
        [shaped(shape, jnp.float32) for shape in shapes],
        [pltpu.VMEM((rows, panel), low_type)],
        14 * rows * panel * block,
        sum(12 * shape[0] * shape[1] for shape in shapes),
    )(origin, *panels, *moms, *weights)


def polish(gram, gram_low, change_low, once_low, iterate, size):
    block = min(size, 256)
    count = size // block
    for step_index in range(NS_STEPS):
        last = step_index + 1 == NS_STEPS
        if last:
            first_term = matmul(iterate.astype(low_type), gram_low[...])
            second_term = matmul(first_term.astype(low_type), gram_low[...])
            return coef_first * iterate + coef_second * first_term + coef_third * second_term

        def make_change(index, carry):
            rows = block_at(index, block)
            square = matmul(gram_low[rows, :], gram_low[...])
            change_low[rows, :] = (coef_second * gram[rows, :] + coef_third * square).astype(
                low_type
            )
            return carry

        def make_once(index, carry):
            rows = block_at(index, block)
            once = matmul(gram_low[rows, :], change_low[...])
            once_low[rows, :] = once.astype(low_type)
            gram[rows, :] = (coef_first * coef_first) * gram[rows, :] + (2.0 * coef_first) * once
            return carry

        def make_gram(index, carry):
            rows = block_at(index, block)
            total = gram[rows, :] + matmul(once_low[rows, :], change_low[...])
            gram[rows, :] = total
            gram_low[rows, :] = total.astype(low_type)
            return carry

        lax.fori_loop(0, count, make_change, 0)
        iterate = coef_first * iterate + matmul(iterate.astype(low_type), change_low[...])
        lax.fori_loop(0, count, make_once, 0)
        lax.fori_loop(0, count, make_gram, 0)


def gram_parts_kernel(where, *refs):
    pieces, gains, near_out, far_out, blocks = refs[:SIDE], refs[-4], refs[-3], refs[-2], refs[-1]
    narrow = blocks.shape[1]
    chunk = blocks.shape[0] // (SIDE * CORES)
    extra = gains.shape[0] // (SIDE * CORES)
    rows = jnp.concatenate([source[...] for source in pieces], axis=0)
    wide = rows.shape[1] // narrow
    places = upper_blocks(wide - 2) + [(wide - 2, wide - 2), (wide - 1, wide - 1)]
    for index, (left, right) in enumerate(places):
        blocks[index * narrow : (index + 1) * narrow, :] = matmul_tn(
            rows[:, left * narrow : (left + 1) * narrow],
            rows[:, right * narrow : (right + 1) * narrow],
        ).astype(low_type)
    core = where[SIDE * CORES]
    for step in range(SIDE):
        near = CORES * step + core
        far = CORES * step + 1 - core
        for target, source, place in ((near_out, near, 0), (far_out, far, SIDE)):
            start = pl.multiple_of((where[source] - place) * (chunk + extra), extra)
            target[pl.ds(start, chunk), :] = blocks[block_at(source, chunk), :]
            start = pl.multiple_of(start + chunk, extra)
            target[pl.ds(start, extra), :] = gains[block_at(source, extra), :]


def gram_parts(where, pieces, gains, narrow):
    wide = pieces[0].shape[1] // narrow - 2
    total = (wide * (wide + 1) // 2 + 2) * narrow
    out_rows = (total + gains.shape[0]) // CORES
    rows = SIDE * pieces[0].shape[0]
    return kernel_call(
        gram_parts_kernel,
        "gram_parts",
        (1,),
        1,
        [fixed(piece.shape) for piece in pieces] + [fixed(gains.shape)],
        [fixed((out_rows, narrow))] * 2,
        [shaped((out_rows, narrow), low_type)] * 2,
        [pltpu.VMEM((total, narrow), low_type)],
        2 * rows * total * narrow,
        4 * total * narrow,
    )(where, *pieces, gains)


def shared_kernel(owner, *refs):
    pieces = refs[: SIDE * CORES]
    own, target, blocks, gram, gram_low, change_low, once_low = refs[SIDE * CORES :]
    chunk, narrow = pieces[0].shape
    wide = gram.shape[0]
    for index, source in enumerate(pieces):
        blocks[block_at(owner[index], chunk), :] = source[...]
    places = upper_blocks(wide // narrow)
    trace = jnp.zeros((1, 1), jnp.float32)
    for index, (left, right) in enumerate(places):
        if left == right:
            trace += trace_of(blocks[index * narrow : (index + 1) * narrow, :].astype(jnp.float32))
    factor = 1.0 / (jnp.sqrt(trace) + 1e-07)
    for index, (left, right) in enumerate(places):
        block = blocks[index * narrow : (index + 1) * narrow, :].astype(jnp.float32)
        block = block * (factor * factor)
        rows = slice(left * narrow, (left + 1) * narrow)
        cols = slice(right * narrow, (right + 1) * narrow)
        gram[rows, cols] = block
        gram_low[rows, cols] = block.astype(low_type)
        if left != right:
            turned = block.T
            gram[cols, rows] = turned
            gram_low[cols, rows] = turned.astype(low_type)
    for index in range(2):
        cols = slice(wide + index * narrow, wide + (index + 1) * narrow)
        first = (len(places) + index) * narrow
        small = blocks[first : first + narrow, :].astype(jnp.float32)
        target[:, cols] = polish_small(small, own[:, cols])
    target[:, :wide] = polish(gram, gram_low, change_low, once_low, own[:, :wide] * factor, wide)


def shared_ortho(owner, pieces, own, wide):
    chunk, narrow = pieces[0].shape
    return kernel_call(
        shared_kernel,
        "shared_ortho",
        (1,),
        1,
        [fixed(piece.shape) for piece in pieces] + [fixed(own.shape)],
        fixed(own.shape),
        shaped(own.shape, jnp.float32),
        [pltpu.VMEM((SIDE * CORES * chunk, narrow), low_type), pltpu.VMEM((wide, wide), jnp.float32)]
        + [pltpu.VMEM((wide, wide), low_type)] * 3,
        20 * wide * wide * wide,
        8 * wide * wide,
    )(owner, *pieces, own)


def own_rows(weight, count, rank):
    share_rows = weight.shape[0] // count
    return lax.dynamic_slice_in_dim(weight, rank * share_rows, share_rows, 0).astype(jnp.float32)


def on_device(
    tokens_in,
    cotangent,
    seg_starts,
    gains,
    w_q_down,
    w_key,
    w_value,
    w_q_up,
    w_out,
    w_gate,
    w_up,
    w_down,
    mom_gains,
    mom_q_down,
    mom_key,
    mom_value,
    mom_q_up,
    mom_out,
    mom_gate,
    mom_up,
    mom_down,
):
    heads_count = lax.axis_size("heads")
    heads_rank = lax.axis_index("heads")
    dp_count = lax.axis_size("dp")
    dp_rank = lax.axis_index("dp")
    all_rank = lax.axis_index(("dp", "heads"))
    all_count = dp_count * heads_count
    local_rows = tokens_in.shape[0]
    row_len = local_rows * heads_count
    model_width = tokens_in.shape[1]
    latent_width = w_q_down.shape[1]
    head_dim = w_key.shape[1]
    local_q = w_q_up.shape[1]
    share_rows = model_width // all_count
    share_gains = gains.shape[0] // all_count
    starts = seg_starts[0]
    whole_index = jnp.arange(row_len, dtype=jnp.int32)
    own_index = heads_rank * local_rows + jnp.arange(local_rows, dtype=jnp.int32)
    own_core = heads_rank % CORES
    own_step = heads_rank // CORES
    ranks = jnp.arange(heads_count, dtype=jnp.int32)
    where = SIDE * ((ranks % CORES) ^ own_core) + (ranks // CORES - own_step) % SIDE
    where = jnp.concatenate([where, own_core[None]]).astype(jnp.int32)
    owner = CORES * ((ranks % SIDE + own_step) % SIDE) + ((ranks // SIDE) ^ own_core)
    owner = owner.astype(jnp.int32)
    shifts = jnp.arange(SIDE, dtype=jnp.int32)
    origin_z = (dp_rank // SIDE - shifts) % SIDE
    origin_x = (dp_rank % SIDE - shifts) % SIDE
    origin = (SIDE * origin_z[:, None] + origin_x[None, :]).reshape(dp_count)
    origin = jnp.concatenate([dp_rank[None], origin]).astype(jnp.int32)
    gain_one = gains[:model_width]
    gain_latent = gains[model_width : model_width + latent_width]
    gain_two = gains[model_width + latent_width :]

    inputs = tokens_in.astype(jnp.float32)
    scale_one = rms_scale(inputs)
    normed_one = (inputs * scale_one * gain_one).astype(low_type)
    latent_raw = matmul(normed_one, w_q_down)
    scale_latent = rms_scale(latent_raw)
    latent_normed = (latent_raw * scale_latent * gain_latent).astype(low_type)
    own_pos = segment_info(starts, own_index)[1]
    own_cos, own_sin = rotary_tables(own_pos, head_dim)
    key_local = rotate(matmul(normed_one, w_key), own_cos, own_sin).astype(low_type)
    value_local = matmul(normed_one, w_value).astype(low_type)
    packed = lax.all_gather(
        jnp.concatenate([latent_normed, key_local, value_local], axis=1), "heads", axis=0, tiled=True
    )
    grad_rows = lax.all_gather(after(cotangent, packed), "heads", axis=0, tiled=True)
    normed_parts = lax.all_to_all(
        normed_one.T.reshape(dp_count, heads_count, share_rows, local_rows)
        .transpose(1, 0, 2, 3)
        .reshape(model_width, local_rows),
        "heads",
        split_axis=0,
        concat_axis=0,
        tiled=True,
    )
    packed, normed_parts = lax.optimization_barrier((packed, normed_parts))
    row_ids, row_pos = segment_info(starts, whole_index)
    row_cos, row_sin = rotary_tables(row_pos, head_dim)
    query_rows, attended_near, attended_far, lse = attend(
        where, packed, w_q_up, head_dim, row_cos, row_sin, row_ids
    )
    attn_mixed = ring_sums(
        chip_sums(
            matmul_nt(attended_far, w_out).astype(low_type),
            matmul_nt(attended_near, w_out).astype(low_type),
        )
    )
    hidden_one = inputs + attn_mixed
    scale_two = rms_scale(hidden_one)
    normed_two = (hidden_one * scale_two * gain_two).astype(low_type)

    gate_turned, up_turned, down_turned = w_gate.T, w_up.T, w_down.T
    pieces_two = gather_heads(normed_two)
    gate_near, up_near, middle_near, back_near = ffn_half(
        owner, pieces_two[:SIDE], grad_rows, gate_turned, up_turned, down_turned, 0
    )
    gate_far, up_far, middle_far, back_far = ffn_half(
        owner, pieces_two[SIDE:], grad_rows, gate_turned, up_turned, down_turned, 1
    )
    chip_two = chip_sums(back_far, back_near)
    normed_two_back = ring_sums(chip_two)
    ffn_part = ffn_grads(
        owner,
        pieces_two,
        grad_rows,
        (after(gate_near, chip_two), up_near, middle_near, gate_far, up_far, middle_far),
        dp_count,
    )
    ffn_sums = lax.psum_scatter(ffn_part, "dp", scatter_dimension=0, tiled=True)[0]
    mixed_far = matmul_tn(after(middle_far, chip_two), down_turned).astype(low_type)
    mixed_near = matmul_tn(middle_near, down_turned).astype(low_type)
    hidden_part, gain_two_grad = norm_back(hidden_one, scale_two, gain_two, normed_two_back)
    hidden_back = cotangent.astype(jnp.float32) + hidden_part

    hidden_low = after(hidden_back.astype(low_type), ffn_part, mixed_far, mixed_near)
    pieces_hidden = gather_heads(hidden_low)
    q_up_part, sums_near, sums_far = attend_back(
        where, pieces_hidden, query_rows, packed, w_out, w_q_up, lse, row_cos, row_sin, row_ids
    )
    ffn_grad, ffn_mom, ffn_gram = momenta(
        ffn_sums, (mom_gate.T, mom_up.T, mom_down.T), FF_BLOCK, True, "ffn_momenta"
    )
    chip_back, ffn_gram = lax.optimization_barrier((chip_sums(sums_far, sums_near), ffn_gram))
    ffn_column = scatter_x(ffn_gram.reshape(dp_count, -1, ffn_gram.shape[1]))
    packed_sums = ring_sums(chip_back)
    out_w_part = joined_tn(pieces_hidden, (attended_near, attended_far), 8, "out_grads")
    out_w_part, packed_sums, ffn_column = lax.optimization_barrier(
        (out_w_part, packed_sums, ffn_column)
    )
    latent_back = packed_sums[:, :latent_width]
    key_sum = packed_sums[:, latent_width : latent_width + head_dim]
    value_sum = packed_sums[:, latent_width + head_dim :]
    latent_raw_grad, gain_latent_grad = norm_back(
        latent_raw, scale_latent, gain_latent, latent_back
    )
    latent_raw_back = latent_raw_grad.astype(low_type)
    key_pre_back = rotate_back(key_sum, own_cos, own_sin).astype(low_type)
    values_low = value_sum.astype(low_type)

    back_low = jnp.concatenate([latent_raw_back, key_pre_back, values_low], axis=1)
    pieces_back = gather_heads(back_low)
    head_column = scatter_x(
        jnp.concatenate(
            [
                after(q_up_part, packed_sums).reshape(dp_count, -1, local_q),
                out_w_part.reshape(dp_count, -1, local_q),
            ],
            axis=1,
        )
    )
    ffn_chunk = scatter_z(ffn_column).astype(low_type)
    pieces_back, head_column, ffn_chunk = lax.optimization_barrier(
        (pieces_back, head_column, ffn_chunk)
    )
    shared_part = joined(owner, normed_parts, pieces_back, "shared_grads")
    normed_one_back = (
        matmul_nt(latent_raw_back, w_q_down)
        + matmul_nt(key_pre_back, w_key)
        + matmul_nt(values_low, w_value)
    )
    input_part, gain_one_grad = norm_back(inputs, scale_one, gain_one, normed_one_back)
    input_grad = hidden_back + input_part
    gains_part = jnp.concatenate([gain_one_grad, gain_latent_grad, gain_two_grad])
    gains_part = gains_part.reshape(dp_count, heads_count, share_gains).astype(low_type)
    gains_part = jnp.pad(
        gains_part, ((0, 0), (0, share_rows - heads_count), (0, LANES - share_gains))
    )

    shared_part, gains_part = lax.optimization_barrier((shared_part, gains_part))
    packed_width = shared_part.shape[1]
    shared_grad = scatter_z(
        scatter_x(
            jnp.concatenate(
                [shared_part.reshape(dp_count, share_rows, packed_width), gains_part], axis=2
            )
        )
    )
    head_sums = scatter_z(head_column)
    ffn_panels = gather_dp(ffn_chunk)
    shared_grad, head_sums, ffn_panels = lax.optimization_barrier(
        (shared_grad, head_sums, ffn_panels)
    )
    q_down_grad = shared_grad[:, :latent_width]
    key_w_grad = shared_grad[:, latent_width : latent_width + head_dim]
    value_w_grad = shared_grad[:, latent_width + head_dim : packed_width]
    q_down_mom = decay_rate * mom_q_down + q_down_grad
    key_w_mom = decay_rate * mom_key + key_w_grad
    value_w_mom = decay_rate * mom_value + value_w_grad

    shared_mom = jnp.concatenate([q_down_mom, key_w_mom, value_w_mom], axis=1)
    gains_rows = shared_grad[:heads_count, packed_width : packed_width + share_gains]
    gains_rows = jnp.pad(
        gains_rows.astype(low_type)[:, None, :],
        ((0, 0), (0, share_rows - 1), (0, head_dim - share_gains)),
    ).reshape(heads_count * share_rows, head_dim)
    pieces_mom = gather_dp(shared_mom.astype(low_type))
    gram_near, gram_far = gram_parts(where, pieces_mom, gains_rows, head_dim)
    gram_sums = ring_sums(chip_sums(gram_far, gram_near))
    gram_chunk = gram_sums.shape[0] - share_rows
    pieces_gram = gather_heads(gram_sums[:gram_chunk].astype(low_type))
    chip_mixed = chip_sums(after(mixed_far, shared_grad), mixed_near)
    layer_out = (hidden_one + ring_sums(after(chip_mixed, *pieces_gram))).astype(low_type)
    gains_grad = gram_sums[gram_chunk, :share_gains]
    gains_mom = decay_rate * mom_gains + gains_grad
    gains_new = own_rows(gains, all_count, all_rank) - gain_rate * gains_mom

    head_grad, head_mom, head_gram = momenta(
        head_sums, (mom_q_up, mom_out), head_dim, False, "head_momenta"
    )
    head_gram = sum_dp(after(head_gram, *pieces_mom))
    ffn_new = updates(
        origin,
        ffn_panels,
        ffn_mom,
        (gate_turned, up_turned, down_turned),
        FF_BLOCK,
        True,
        "ffn_updates",
    )
    pieces_gram, ffn_new = lax.optimization_barrier((pieces_gram, ffn_new))
    shared_done = shared_ortho(owner, pieces_gram, shared_mom, latent_width)
    q_up_new, out_w_new = updates(
        origin,
        (after(head_gram, shared_done),),
        head_mom,
        (w_q_up, w_out),
        head_dim,
        False,
        "head_updates",
    )
    q_down_new = (
        own_rows(w_q_down, all_count, all_rank)
        - muon_rate * math.sqrt(model_width / latent_width) * shared_done[:, :latent_width]
    )
    pair_factor = muon_rate * math.sqrt(model_width / head_dim)
    key_w_new = (
        own_rows(w_key, all_count, all_rank)
        - pair_factor * shared_done[:, latent_width : latent_width + head_dim]
    )
    value_w_new = (
        own_rows(w_value, all_count, all_rank)
        - pair_factor * shared_done[:, latent_width + head_dim :]
    )
    ffn_grad, ffn_mom, ffn_new = [
        [array.T for array in arrays] for arrays in (ffn_grad, ffn_mom, ffn_new)
    ]
    return (
        layer_out,
        input_grad,
        gains_grad,
        q_down_grad,
        key_w_grad,
        value_w_grad,
        *head_grad,
        *ffn_grad,
        gains_mom,
        q_down_mom,
        key_w_mom,
        value_w_mom,
        *head_mom,
        *ffn_mom,
        gains_new,
        q_down_new,
        key_w_new,
        value_w_new,
        q_up_new,
        out_w_new,
        *ffn_new,
    )


def solution(mesh):
    placed = (
        P(("dp", "heads"), None),
        P(("dp", "heads"), None),
        P("dp", None),
        P(),
        P(),
        P(),
        P(),
        P(None, "heads"),
        P(None, "heads"),
        P(None, "heads"),
        P(None, "heads"),
        P(None, "heads"),
        P(("dp", "heads")),
        P(("dp", "heads"), None),
        P(("dp", "heads"), None),
        P(("dp", "heads"), None),
        P("dp", "heads"),
        P("dp", "heads"),
        P("dp", "heads"),
        P("dp", "heads"),
        P("dp", "heads"),
    )
    return jax.shard_map(
        on_device,
        mesh=mesh,
        in_specs=placed,
        out_specs=(
            P(("dp", "heads"), None),
            P(("dp", "heads"), None),
            P(("dp", "heads")),
            P(("dp", "heads"), None),
            P(("dp", "heads"), None),
            P(("dp", "heads"), None),
            P("dp", "heads"),
            P("dp", "heads"),
            P("dp", "heads"),
            P("dp", "heads"),
            P("dp", "heads"),
            P(("dp", "heads")),
            P(("dp", "heads"), None),
            P(("dp", "heads"), None),
            P(("dp", "heads"), None),
            P("dp", "heads"),
            P("dp", "heads"),
            P("dp", "heads"),
            P("dp", "heads"),
            P("dp", "heads"),
            P(("dp", "heads")),
            P(("dp", "heads"), None),
            P(("dp", "heads"), None),
            P(("dp", "heads"), None),
            P("dp", "heads"),
            P("dp", "heads"),
            P("dp", "heads"),
            P("dp", "heads"),
            P("dp", "heads"),
        ),
        check_vma=False,
    )
```

```python
import math

import jax
import jax.numpy as jnp
from jax import lax
from jax.experimental import pallas as pl
from jax.experimental.pallas import tpu as pltpu
from jax.sharding import PartitionSpec as P

NS_STEPS = 3
FF_BLOCK = 352
SIDE = 4
CORES = 2
LANES = 128

coef_first = 3.4445
coef_second = -4.775
coef_third = 2.0315
muon_rate = 0.5
gain_rate = 0.004
decay_rate = 0.5
low_type = jnp.bfloat16


def matmul(left, right):
    return jnp.dot(left, right, preferred_element_type=jnp.float32)


def matmul_nt(left, right):
    return lax.dot_general(
        left, right, (((1,), (1,)), ((), ())), preferred_element_type=jnp.float32
    )


def matmul_tn(left, right):
    return lax.dot_general(
        left, right, (((0,), (0,)), ((), ())), preferred_element_type=jnp.float32
    )


def rms_scale(values):
    return lax.rsqrt(jnp.mean(values * values, axis=-1, keepdims=True) + 1e-05)


def norm_back(values, scale, gain, grad_out):
    weighted = gain * grad_out
    inner = jnp.mean(values * weighted, axis=-1, keepdims=True)
    grad_in = scale * weighted - values * (scale * scale * scale) * inner
    gain_grad = jnp.sum(grad_out * values * scale, axis=0)
    return (grad_in, gain_grad)


def segment_info(starts, token_index):
    started = starts[None, :] <= token_index[:, None]
    seg_ids = jnp.sum(started.astype(jnp.int32), axis=1)
    seg_begin = jnp.max(jnp.where(started, starts[None, :], 0), axis=1)
    return (seg_ids, token_index - seg_begin)


def rotary_tables(positions, head_dim):
    half_dim = head_dim // 2
    frequency = jnp.exp(
        jnp.arange(half_dim, dtype=jnp.float32) * (-2.0 * math.log(10000.0) / head_dim)
    )
    angles = positions.astype(jnp.float32)[:, None] * frequency[None, :]
    return (jnp.cos(angles), jnp.sin(angles))


def rotate(values, cosine, sine_part):
    half_dim = values.shape[-1] // 2
    first_half = values[..., :half_dim]
    second_half = values[..., half_dim:]
    return jnp.concatenate(
        [
            first_half * cosine - second_half * sine_part,
            second_half * cosine + first_half * sine_part,
        ],
        axis=-1,
    )


def rotate_back(grads, cosine, sine_part):
    return rotate(grads, cosine, -sine_part)


def shift_heads(values, step, core):
    pairs = [
        (CORES * place + side, CORES * ((place + step) % SIDE) + (side ^ core))
        for place in range(SIDE)
        for side in range(CORES)
    ]
    return lax.ppermute(values, "heads", pairs)


def shift_dp(values, step_z, step_x):
    pairs = [
        (SIDE * z + x, SIDE * ((z + step_z) % SIDE) + (x + step_x) % SIDE)
        for z in range(SIDE)
        for x in range(SIDE)
    ]
    return lax.ppermute(values, "dp", pairs)


def gather_heads(own, beside=()):
    ring = [own] + [shift_heads(own, -step, 0) for step in range(1, SIDE)]
    ring, beside = lax.optimization_barrier((ring, beside))
    pieces = ring + [shift_heads(piece, 0, 1) for piece in ring]
    return (pieces, *beside) if beside else pieces


def chip_sums(far_half, near_half):
    rows = near_half.shape[0] // SIDE
    total = near_half.astype(jnp.float32) + shift_heads(far_half, 0, 1).astype(jnp.float32)
    return total.astype(far_half.dtype).reshape(SIDE, rows, *near_half.shape[1:])


def ring_operands(chip):
    return lax.optimization_barrier([chip[step] for step in range(SIDE)])


def ring_sums(operands):
    total = operands[0].astype(jnp.float32)
    for step in range(1, SIDE):
        total = total + shift_heads(operands[step], step, 0).astype(jnp.float32)
    return total


def pick(array, place, axis):
    return lax.dynamic_index_in_dim(array, place % SIDE, axis, keepdims=False)


def scatter_x(parts):
    place_x = lax.axis_index("dp") % SIDE
    grid = parts.reshape(SIDE, SIDE, *parts.shape[1:])
    total = pick(grid, place_x, 1).astype(jnp.float32)
    for step in range(1, SIDE):
        total = total + shift_dp(pick(grid, place_x + step, 1), 0, step).astype(jnp.float32)
    return total.astype(parts.dtype)


def scatter_z(column):
    place_z = lax.axis_index("dp") // SIDE
    total = pick(column, place_z, 0).astype(jnp.float32)
    for step in range(1, SIDE):
        total = total + shift_dp(pick(column, place_z + step, 0), step, 0).astype(jnp.float32)
    return total


def line_sum(part, axis):
    total = part.astype(jnp.float32)
    for step in range(1, SIDE):
        total = total + shift_dp(part, step * axis, step * (1 - axis)).astype(jnp.float32)
    return total.astype(part.dtype)


def exchange_dp(parts):
    return lax.all_to_all(parts, "dp", split_axis=0, concat_axis=0, tiled=True)


def after(values, *earlier):
    return lax.optimization_barrier((values, *earlier))[0]


vmem_mib = {
    "attend": 14,
    "attend_back": 20,
    "ffn_near": 26,
    "ffn_far": 26,
    "ffn_grads": 32,
    "head_grads": 16,
    "shared_updates": 24,
    "block_updates": 28,
}


def in_hbm(array):
    return pltpu.with_memory_space_constraint(array, pltpu.HBM)


def streamed_call(
    body, name, scalars, resident, arrays, out_shape, scratch, flops, moved, cuts, merged
):
    kinds, pieces = [], []
    for index, array in enumerate(arrays):
        rows = array.shape[0] if index not in cuts else cuts[index][0]
        if index < merged:
            rows = merged * array.shape[0] if index == 0 else 16
        kinds.append(pltpu.VMEM((rows, *array.shape[1:]), array.dtype))
        pieces.append(1 if index not in cuts else cuts[index][1])
    count, outs = len(arrays), len(out_shape)

    def wrapped(*refs):
        numbers, refs = refs[: len(scalars)], refs[len(scalars) :]
        still, refs = refs[: len(resident)], refs[len(resident) :]
        sources, refs = refs[:count], refs[count:]
        targets, refs = refs[:outs], refs[outs:]
        held, sems, rest = refs[:count], refs[count], refs[count + 1 :]
        copies, place = [], 0
        for index, source in enumerate(sources):
            parts = [(source, held[index])]
            if index < merged:
                rows = source.shape[0]
                parts = [(source, held[0].at[index * rows : (index + 1) * rows, :])]
            if index in cuts:
                parts = cuts[index][2](numbers, source, held[index])
            group = []
            for part_from, part_to in parts:
                group.append(pltpu.make_async_copy(part_from, part_to, sems.at[place]))
                place += 1
            copies.append(group)
        for group in copies:
            for copy in group:
                copy.start()
        done = [0]

        def ready(index):
            while done[0] <= index:
                for copy in copies[done[0]]:
                    copy.wait()
                done[0] += 1

        body(ready, numbers, still, held, targets, rest)
        ready(count - 1)

    return pl.pallas_call(
        wrapped,
        grid_spec=pltpu.PrefetchScalarGridSpec(
            num_scalar_prefetch=len(scalars),
            grid=(1,),
            in_specs=[pl.BlockSpec(memory_space=pltpu.VMEM)] * len(resident)
            + [pl.BlockSpec(memory_space=pltpu.HBM)] * count,
            out_specs=[pl.BlockSpec(memory_space=pltpu.VMEM)] * outs,
            scratch_shapes=[*kinds, pltpu.SemaphoreType.DMA((sum(pieces),)), *scratch],
        ),
        out_shape=out_shape,
        compiler_params=pltpu.CompilerParams(
            vmem_limit_bytes=vmem_mib.get(name, 12) * 1024 * 1024
        ),
        cost_estimate=pl.CostEstimate(flops=flops, bytes_accessed=moved, transcendentals=0),
        name=name,
    )(*scalars, *resident, *[in_hbm(array) for array in arrays])


def whole_call(body, name, scalars, arrays, out_shape, scratch, flops, moved):
    return pl.pallas_call(
        body,
        in_specs=[pl.BlockSpec(memory_space=pltpu.SMEM)] * len(scalars)
        + [pl.BlockSpec(memory_space=pltpu.VMEM)] * len(arrays),
        out_specs=jax.tree.map(lambda _: pl.BlockSpec(memory_space=pltpu.VMEM), out_shape),
        out_shape=out_shape,
        scratch_shapes=scratch,
        compiler_params=pltpu.CompilerParams(
            vmem_limit_bytes=vmem_mib.get(name, 12) * 1024 * 1024
        ),
        cost_estimate=pl.CostEstimate(flops=flops, bytes_accessed=moved, transcendentals=0),
        name=name,
    )(*scalars, *arrays)


def kernel_call(body, name, grid, prefetch, in_specs, out_specs, out_shape, scratch, flops, moved):
    return pl.pallas_call(
        body,
        grid_spec=pltpu.PrefetchScalarGridSpec(
            num_scalar_prefetch=prefetch,
            grid=grid,
            in_specs=in_specs,
            out_specs=out_specs,
            scratch_shapes=scratch,
        ),
        out_shape=out_shape,
        compiler_params=pltpu.CompilerParams(vmem_limit_bytes=vmem_mib.get(name, 12) * 1024 * 1024),
        cost_estimate=pl.CostEstimate(flops=flops, bytes_accessed=moved, transcendentals=0),
        name=name,
    )


def shaped(shape, kind):
    return jax.ShapeDtypeStruct(shape, kind)


def fixed(shape):
    return pl.BlockSpec(
        shape, lambda *grid: (0,) * len(shape), pipeline_mode=pl.Buffered(buffer_count=1)
    )


def visible(ids_q, ids_k, first_row, rows, cols):
    query_at = first_row + lax.broadcasted_iota(jnp.int32, (rows, cols), 0)
    key_at = lax.broadcasted_iota(jnp.int32, (rows, cols), 1)
    return (ids_q == ids_k) & (key_at <= query_at)


def block_at(index, piece):
    return pl.ds(pl.multiple_of(index * piece, piece), piece)


def store_by_distance(where, rows_ref, near_ref, far_ref, piece):
    core = where[SIDE * CORES]
    for step in range(SIDE):
        near = CORES * step + core
        far = CORES * step + 1 - core
        near_ref[block_at(where[near], piece), :] = rows_ref[block_at(near, piece), :].astype(
            near_ref.dtype
        )
        far_ref[block_at(where[far] - SIDE, piece), :] = rows_ref[block_at(far, piece), :].astype(
            far_ref.dtype
        )


def attend_kernel(
    where, packed, w_q_up, cosine, sine, ids_q, ids_k, query_out, near_out, far_out, lse_out, mixed
):
    row_len, packed_width = packed.shape
    latent_width, width = w_q_up.shape
    head_dim = (packed_width - latent_width) // 2
    piece = row_len // (SIDE * CORES)
    block = CORES * piece
    scale = head_dim ** (-0.5)
    key_cols = slice(latent_width, latent_width + head_dim)
    value_cols = slice(latent_width + head_dim, latent_width + 2 * head_dim)
    for head in range(width // head_dim):
        cols = slice(head * head_dim, (head + 1) * head_dim)
        for index in range(SIDE):
            first = index * block
            end = first + block
            rows = slice(first, end)
            query = matmul(packed[rows, :latent_width], w_q_up[:, cols])
            query = rotate(query, cosine[rows, :], sine[rows, :]).astype(low_type)
            query_out[rows, cols] = query
            scores = matmul_nt(query, packed[:end, key_cols]) * scale
            allowed = visible(ids_q[rows, :], ids_k[:, :end], first, block, end)
            scores = jnp.where(allowed, scores, -1e30)
            row_max = jnp.max(scores, axis=-1, keepdims=True)
            exponent = jnp.exp(scores - row_max)
            row_total = jnp.sum(exponent, axis=-1, keepdims=True)
            probs = (exponent * (1.0 / row_total)).astype(low_type)
            lse_out[head, rows, :] = row_max + jnp.log(row_total)
            mixed[rows, cols] = matmul(probs, packed[:end, value_cols]).astype(low_type)
    store_by_distance(where, mixed, near_out, far_out, piece)


def attend(where, packed, w_q_up, head_dim, cosine, sine, row_ids):
    row_len = packed.shape[0]
    latent_width, width = w_q_up.shape
    return whole_call(
        attend_kernel,
        "attend",
        [where],
        [packed, w_q_up, cosine, sine, row_ids[:, None], row_ids[None, :]],
        [
            shaped((row_len, width), low_type),
            shaped((row_len // 2, width), low_type),
            shaped((row_len // 2, width), low_type),
            shaped((width // head_dim, row_len, 1), jnp.float32),
        ],
        [pltpu.VMEM((row_len, width), low_type)],
        2 * width * row_len * (latent_width + 2 * row_len),
        8 * row_len * width,
    )


def attend_back_kernel(where, *refs):
    pieces = refs[: SIDE * CORES]
    query_in, packed, w_out, w_q_up, lse, cosine, sine, ids_q, ids_k = refs[
        SIDE * CORES : SIDE * CORES + 9
    ]
    weight_back, near_out, far_out, query_back, back_rows, totals = refs[SIDE * CORES + 9 :]
    row_len, packed_width = packed.shape
    latent_width, width = w_q_up.shape
    head_dim = (packed_width - latent_width) // 2
    piece = row_len // (SIDE * CORES)
    block = CORES * piece
    scale = head_dim ** (-0.5)
    key_cols = slice(latent_width, latent_width + head_dim)
    value_cols = slice(latent_width + head_dim, latent_width + 2 * head_dim)
    for index in range(0, SIDE * CORES, 2):
        pair = jnp.concatenate([pieces[index][...], pieces[index + 1][...]], axis=0)
        back_rows[index * piece : (index + 2) * piece, :] = matmul(pair, w_out[...]).astype(
            low_type
        )
    totals[:, latent_width:] = jnp.zeros((row_len, 2 * head_dim), jnp.float32)
    for head in range(width // head_dim):
        cols = slice(head * head_dim, (head + 1) * head_dim)
        for index in range(SIDE):
            first = index * block
            end = first + block
            rows = slice(first, end)
            query = query_in[rows, cols]
            back = jnp.concatenate(
                [
                    back_rows[block_at(where[CORES * index + side], piece), cols]
                    for side in range(CORES)
                ],
                axis=0,
            )
            keys = packed[:end, key_cols]
            scores = matmul_nt(query, keys) * scale
            allowed = visible(ids_q[rows, :], ids_k[:, :end], first, block, end)
            probs = jnp.where(allowed, jnp.exp(scores - lse[head, rows, :]), 0.0)
            probs_back = matmul_nt(back, packed[:end, value_cols])
            inner = jnp.sum(probs * probs_back, axis=-1, keepdims=True)
            score_back = (probs * (probs_back - inner)).astype(low_type)
            totals[:end, value_cols] += matmul_tn(probs.astype(low_type), back)
            totals[:end, key_cols] += matmul_tn(score_back, query) * scale
            query_grad = matmul(score_back, keys) * scale
            query_back[rows, cols] = rotate_back(
                query_grad, cosine[rows, :], sine[rows, :]
            ).astype(low_type)
    for index in range(SIDE):
        rows = slice(index * block, (index + 1) * block)
        totals[rows, :latent_width] = matmul_nt(query_back[rows, :], w_q_up[...])
    store_by_distance(where, totals, near_out, far_out, piece)
    weight_back[...] = matmul_tn(packed[:, :latent_width], query_back[...]).astype(low_type)


def attend_back(where, pieces, query_rows, packed, w_out, w_q_up, lse, cosine, sine, row_ids):
    row_len, packed_width = packed.shape
    latent_width, width = w_q_up.shape
    model_width = w_out.shape[0]
    return whole_call(
        attend_back_kernel,
        "attend_back",
        [where],
        [
            *pieces,
            query_rows,
            packed,
            w_out,
            w_q_up,
            lse,
            cosine,
            sine,
            row_ids[:, None],
            row_ids[None, :],
        ],
        [
            shaped((latent_width, width), low_type),
            shaped((row_len // 2, packed_width), low_type),
            shaped((row_len // 2, packed_width), low_type),
        ],
        [
            pltpu.VMEM((row_len, width), low_type),
            pltpu.VMEM((row_len, width), low_type),
            pltpu.VMEM((row_len, packed_width), jnp.float32),
        ],
        2 * width * row_len * (5 * row_len + model_width + 2 * latent_width),
        8 * row_len * width,
    )


def ffn_kernel(ready, numbers, still, held, targets, rest):
    w_gate = still[0]
    features, (w_up, grads, w_down) = held[0], held[SIDE:]
    gate_out, up_out, middle_out, features_back = targets
    gate_raw, up_raw = rest
    width = w_gate.shape[0]
    chunk = width // 2
    tile = features.shape[1] // 4

    def rows_of(part):
        return pl.ds(pl.multiple_of(part * chunk, chunk), chunk)

    def make_gate(part, carry):
        rows = rows_of(part)
        gate_raw[rows, :] = matmul_nt(w_gate[rows, :], features[...])
        return carry

    def make_up(part, carry):
        rows = rows_of(part)
        up_raw[rows, :] = matmul_nt(w_up[rows, :], features[...])
        return carry

    def make_backs(part, carry):
        rows = rows_of(part)
        middle_back = matmul_nt(w_down[rows, :], grads[...])
        gate, up = gate_raw[rows, :], up_raw[rows, :]
        sigmoid = jax.nn.sigmoid(gate)
        activated = gate * sigmoid
        middle_out[rows, :] = (activated * up).astype(low_type)
        gate_out[rows, :] = (
            middle_back * up * sigmoid * (1.0 + gate * (1.0 - sigmoid))
        ).astype(low_type)
        up_out[rows, :] = (middle_back * activated).astype(low_type)
        return carry

    def make_features(part, carry):
        area = pl.ds(pl.multiple_of(part * tile, tile), tile)
        features_back[:, area] = (
            matmul_tn(gate_out[...], w_gate[:, area]) + matmul_tn(up_out[...], w_up[:, area])
        ).astype(low_type)
        return carry

    ready(SIDE - 1)
    lax.fori_loop(0, 2, make_gate, 0)
    ready(SIDE)
    lax.fori_loop(0, 2, make_up, 0)
    ready(SIDE + 2)
    lax.fori_loop(0, 2, make_backs, 0)
    lax.fori_loop(0, 4, make_features, 0)


def ffn_half(owner, pieces, grads, w_gate, w_up, w_down, far):
    piece, model_width = pieces[0].shape
    width = w_gate.shape[0]
    rows = SIDE * piece

    def own_blocks(numbers, source, target):
        return [
            (
                source.at[block_at(numbers[0][SIDE * far + step], piece), :],
                target.at[step * piece : (step + 1) * piece, :],
            )
            for step in range(SIDE)
        ]

    return streamed_call(
        ffn_kernel,
        "ffn_far" if far else "ffn_near",
        [owner],
        [w_gate],
        [*pieces, w_up, grads, w_down],
        [shaped((width, rows), low_type)] * 3 + [shaped((rows, model_width), low_type)],
        [pltpu.VMEM((width, rows), jnp.float32)] * 2,
        10 * rows * model_width * width,
        6 * model_width * width + 6 * rows * model_width,
        {SIDE + 1: (rows, SIDE, own_blocks)},
        SIDE,
    )


def ffn_grads_kernel(owner, *refs):
    count = SIDE * CORES
    pieces, grads, halves, target = refs[:count], refs[count], refs[count + 1 : -1], refs[-1]
    width, half_rows = halves[0].shape
    piece = pieces[0].shape[0]
    places, share = target.shape[0], target.shape[2]
    block = places * share
    cols = pl.ds(pl.multiple_of(pl.program_id(0) * block, block), block)
    features = jnp.concatenate([source[:, cols] for source in pieces], axis=0)
    grads = jnp.concatenate(
        [grads[block_at(owner[index], piece), cols] for index in range(count)], axis=0
    )
    for index, right in enumerate((features, features, grads)):
        total = matmul(halves[index][...], right[:half_rows, :])
        total += matmul(halves[index + 3][...], right[half_rows:, :])
        total = total.astype(low_type)
        for place in range(places):
            target[place, index * width : (index + 1) * width, :] = total[
                :, place * share : (place + 1) * share
            ]


def ffn_grads(owner, pieces, grads, halves, dp_count):
    piece, model_width = pieces[0].shape
    row_len = grads.shape[0]
    width = halves[0].shape[0]
    block = model_width // 4
    share = model_width // dp_count
    return kernel_call(
        ffn_grads_kernel,
        "ffn_grads",
        (4,),
        1,
        [fixed((piece, model_width))] * len(pieces)
        + [fixed((row_len, model_width))]
        + [fixed(halves[0].shape)] * 6,
        pl.BlockSpec((block // share, 3 * width, share), lambda index, owner: (index, 0, 0)),
        pltpu.HBM((dp_count, 3 * width, share), low_type),
        [],
        6 * row_len * model_width * width,
        4 * row_len * model_width + 6 * model_width * width,
    )(owner, *map(in_hbm, pieces), in_hbm(grads), *halves)


def head_grads(pieces, halves, q_up_part, dp_count):
    piece, model_width = pieces[0].shape
    count = len(pieces)
    width = halves[0].shape[1]
    steps = 4
    block = model_width // steps
    each = dp_count // steps
    q_up_rows = q_up_part.shape[0] // dp_count
    out_rows = model_width // dp_count
    rows = piece * count

    def body(*refs):
        sources, (near, far, above, target) = refs[:count], refs[count:]
        cols = pl.ds(pl.multiple_of(pl.program_id(0) * block, block), block)
        left = jnp.concatenate([source[:, cols] for source in sources], axis=0)
        right = jnp.concatenate([near[...], far[...]], axis=0)
        total = matmul_tn(left, right)
        for index in range(each):
            first = index * q_up_rows
            target[index, :q_up_rows, :] = above[first : first + q_up_rows, :]
            first = index * out_rows
            target[index, q_up_rows:, :] = total[first : first + out_rows, :].astype(low_type)

    return kernel_call(
        body,
        "head_grads",
        (steps,),
        0,
        [fixed((piece, model_width))] * count
        + [fixed(source.shape) for source in halves]
        + [pl.BlockSpec((each * q_up_rows, width), lambda index: (index, 0))],
        pl.BlockSpec((each, q_up_rows + out_rows, width), lambda index: (index, 0, 0)),
        pltpu.HBM((dp_count, q_up_rows + out_rows, width), low_type),
        [],
        2 * rows * model_width * width,
        2 * rows * (model_width + width) + 4 * model_width * width,
    )(*map(in_hbm, pieces), *map(in_hbm, halves), q_up_part)


def shared_parts_kernel(count, owner, *refs):
    left, right, gains, target = refs[:count], refs[count:-2], refs[-2], refs[-1]
    left = jnp.concatenate([source[...] for source in left], axis=1)
    right = jnp.concatenate([source[...] for source in right], axis=0)
    total = matmul(left, right).astype(low_type)
    places, extra = gains.shape[0], gains.shape[1]
    rows = total.shape[0] // places
    tiles = total.shape[1] // LANES
    for place in range(places):
        for tile in range(tiles):
            target[place, tile * rows : (tile + 1) * rows, :] = total[
                place * rows : (place + 1) * rows, tile * LANES : (tile + 1) * LANES
            ]
        first = tiles * rows
        target[place, first : first + extra, :] = gains[place, :, :]


def shared_parts_of(owner, left, right, gains):
    count = len(right)
    width = left.shape[0] // count
    piece, cols = right[0].shape
    places = gains.shape[0]
    rows = width // places * (cols // LANES) + gains.shape[1]

    def body(owner, *refs):
        shared_parts_kernel(count, owner, *refs)

    return kernel_call(
        body,
        "shared_parts",
        (1,),
        1,
        [
            pl.BlockSpec((width, piece), lambda index, owner, place=place: (owner[place], 0))
            for place in range(count)
        ]
        + [fixed(source.shape) for source in right]
        + [fixed(gains.shape)],
        fixed((places, rows, LANES)),
        shaped((places, rows, LANES), low_type),
        [],
        2 * piece * count * width * cols,
        2 * piece * count * (width + cols) + 2 * width * cols,
    )(owner, *([in_hbm(left)] * count), *right, gains)


def shared_momenta_kernel(parts, q_down, key, value, *refs):
    grads, moms, gains_out, own, target = refs[:3], refs[3:6], refs[6], refs[7], refs[8]
    total = parts[0].astype(jnp.float32)
    for place in range(1, parts.shape[0]):
        total += parts[place].astype(jnp.float32)
    rows = q_down.shape[0]
    tiles = own.shape[1] // LANES
    first = 0
    for tile in range(tiles):
        own[:, tile * LANES : (tile + 1) * LANES] = total[tile * rows : (tile + 1) * rows, :]
    for old, grad_out, mom_out in zip((q_down, key, value), grads, moms):
        cols = slice(first, first + old.shape[1])
        grad = own[:, cols]
        new = decay_rate * old[...] + grad
        grad_out[...] = grad
        mom_out[...] = new
        own[:, cols] = new
        first += old.shape[1]
    head = tiles * rows
    extra = gains_out.shape[0]
    gains_out[...] = total[head : head + extra, :]
    for place in range(target.shape[0]):
        for tile in range(tiles):
            target[place, tile * rows : (tile + 1) * rows, :] = own[
                :, tile * LANES : (tile + 1) * LANES
            ].astype(low_type)


def shared_momenta(parts, old, extra):
    places, rows, _ = parts.shape
    shapes = [array.shape for array in old]
    width = sum(shape[1] for shape in shapes)
    return whole_call(
        shared_momenta_kernel,
        "shared_momenta",
        [],
        [parts, *old],
        [shaped(shape, jnp.float32) for shape in shapes + shapes]
        + [
            shaped((extra, LANES), jnp.float32),
            shaped((shapes[0][0], width), jnp.float32),
            shaped((places, rows - extra, LANES), low_type),
        ],
        [],
        places * rows * LANES,
        4 * places * rows * LANES,
    )


def panel_places(block):
    panel = min(block, LANES)
    count = -(-block // panel)
    return panel, count, upper_blocks(count)


def upper_blocks(count):
    return [(row, col) for row in range(count) for col in range(row, count)]


def momentum_kernel(spans, block, turned, *refs):
    count = len(spans)
    sums, moms = refs[0], refs[1 : 1 + count]
    grad_out, mom_out = refs[1 + count : 1 + 2 * count], refs[1 + 2 * count : 1 + 3 * count]
    gram_out = refs[-1]
    kind = gram_out.dtype
    panel, tiles, places = panel_places(block)
    place = 0
    for index, (row_at, rows) in enumerate(spans):
        grad = sums[row_at : row_at + rows, :].astype(jnp.float32)
        new = decay_rate * moms[index][...] + grad
        grad_out[index][...] = grad
        mom_out[index][...] = new
        low = new.astype(low_type)
        for first in range(0, low.shape[0 if turned else 1], block):
            if turned:
                part = low[first : first + block, :]
                if tiles * panel > block:
                    blank = jnp.zeros((tiles * panel - block, part.shape[1]), low_type)
                    part = jnp.concatenate([part, blank], axis=0)
                gram = matmul_nt(part, part).astype(kind)
            else:
                part = low[:, first : first + block]
                gram = matmul_tn(part, part).astype(kind)
            for row, col in places:
                gram_out[place * panel : (place + 1) * panel, :] = gram[
                    row * panel : (row + 1) * panel, col * panel : (col + 1) * panel
                ]
                place += 1


def momenta(sums, moms, block, turned, name):
    axis = 0 if turned else 1
    blocks = sum(mom.shape[axis] // block for mom in moms)
    panel, tiles, places = panel_places(block)
    spans, row_at = [], 0
    for mom in moms:
        spans.append((row_at, mom.shape[0]))
        row_at += mom.shape[0]

    def body(*refs):
        momentum_kernel(spans, block, turned, *refs)

    shapes = [mom.shape for mom in moms]
    panels = (blocks * len(places) * panel, panel)
    results = whole_call(
        body,
        name,
        [],
        [sums, *moms],
        [shaped(shape, jnp.float32) for shape in shapes + shapes]
        + [shaped(panels, low_type)],
        [],
        2 * block * sum(shape[0] * shape[1] for shape in shapes),
        16 * sum(shape[0] * shape[1] for shape in shapes),
    )
    count = len(moms)
    return results[:count], results[count : 2 * count], results[-1]


def trace_of(gram):
    rows = lax.broadcasted_iota(jnp.int32, gram.shape, 0)
    cols = lax.broadcasted_iota(jnp.int32, gram.shape, 1)
    diagonal = jnp.where(rows == cols, gram, 0.0)
    return jnp.sum(jnp.sum(diagonal, axis=0, keepdims=True), axis=1, keepdims=True)


def polish_small(grams, blocks, turned):
    def apply(values, right, turn):
        values = values.astype(low_type)
        return matmul(right, values) if turn else matmul(values, right)

    factors = [1.0 / (jnp.sqrt(trace_of(gram)) + 1e-07) for gram in grams]
    iterates = [block * factor for block, factor in zip(blocks, factors)]
    grams = [gram * (factor * factor) for gram, factor in zip(grams, factors)]
    for step_index in range(NS_STEPS):
        lows = [gram.astype(low_type) for gram in grams]
        if step_index + 1 == NS_STEPS:
            first = [apply(*args) for args in zip(iterates, lows, turned)]
            second = [apply(*args) for args in zip(first, lows, turned)]
            return [
                coef_first * iterate + coef_second * one + coef_third * two
                for iterate, one, two in zip(iterates, first, second)
            ]
        squares = [matmul(low, low) for low in lows]
        changes = [
            (coef_second * gram + coef_third * square).astype(low_type)
            for gram, square in zip(grams, squares)
        ]
        moves = [apply(*args) for args in zip(iterates, changes, turned)]
        iterates = [coef_first * iterate + move for iterate, move in zip(iterates, moves)]
        once = [matmul(low, change) for low, change in zip(lows, changes)]
        twice = [matmul(one.astype(low_type), change) for one, change in zip(once, changes)]
        grams = [
            (coef_first * coef_first) * gram + (2.0 * coef_first) * one + two
            for gram, one, two in zip(grams, once, twice)
        ]


def gram_from_panels(panels, first, block):
    panel, tiles, places = panel_places(block)
    parts = {}
    for index, (row, col) in enumerate(places):
        start = (first + index) * panel
        parts[row, col] = panels[start : start + panel, :].astype(jnp.float32)
        if row != col:
            parts[col, row] = parts[row, col].T
    return jnp.concatenate(
        [
            jnp.concatenate([parts[row, col] for col in range(tiles)], axis=1)
            for row in range(tiles)
        ],
        axis=0,
    )


def updates(rank, panels, groups, name):
    groups = [(None, *group) for group in groups]
    counts = [len(group[1]) for group in groups]
    total = sum(counts)
    moms = [mom for group in groups for mom in group[1]]
    weights = [weight for group in groups for weight in group[2]]
    flags = [group[4] for group in groups for _ in group[1]]
    shapes = [mom.shape for mom in moms]

    places = panels.shape[0]
    chunks, starts = [], []
    for _, group_moms, _, block, turned in groups:
        panel, _, tile_places = panel_places(block)
        count = sum(mom.shape[0 if turned else 1] // block for mom in group_moms)
        starts.append(sum(chunks))
        chunks.append(count * len(tile_places) * panel // places)

    def body(rank, *refs):
        parts, refs, flats = refs[0], refs[1 : 1 + 3 * total], refs[1 + 3 * total :]
        mom_refs, weight_refs, targets = refs[:total], refs[total : 2 * total], refs[2 * total :]
        for flat, chunk, at in zip(flats, chunks, starts):
            for place in range(places):
                flat[place * chunk : (place + 1) * chunk, :] = parts[place, at : at + chunk, :]
        grams, blocks, turns, targets_at = [], [], [], []
        index = 0
        for group, source in zip(groups, flats):
            block, turned = group[3], group[4]
            panel, tiles, tile_places = panel_places(block)
            first = 0
            for weight in group[2]:
                rate = muon_rate * math.sqrt(weight.shape[1 if turned else 0] / block)
                for start in range(0, shapes[index][0 if turned else 1], block):
                    grams.append(gram_from_panels(source, first, block))
                    first += len(tile_places)
                    part = slice(start, start + block)
                    area = (part, slice(None)) if turned else (slice(None), part)
                    values = mom_refs[index][area]
                    if turned and tiles * panel > block:
                        blank = jnp.zeros((tiles * panel - block, values.shape[1]), jnp.float32)
                        values = jnp.concatenate([values, blank], axis=0)
                    blocks.append(values)
                    turns.append(turned)
                    targets_at.append((index, area, rate, block))
                index += 1
        for ortho, turn, (index, area, rate, block) in zip(
            polish_small(grams, blocks, turns), turns, targets_at
        ):
            if turn:
                ortho = ortho[:block, :]
            targets[index][area] = weight_refs[index][area].astype(jnp.float32) - rate * ortho

    def own_block(shape, turned):
        if turned:
            return pl.BlockSpec(shape, lambda index, rank: (0, rank[0]))
        return pl.BlockSpec(shape, lambda index, rank: (rank[0], 0))

    results = kernel_call(
        body,
        name,
        (1,),
        1,
        [fixed(panels.shape)]
        + [fixed(shape) for shape in shapes]
        + [own_block(shape, flag) for shape, flag in zip(shapes, flags)],
        [fixed(shape) for shape in shapes],
        [shaped(shape, jnp.float32) for shape in shapes],
        [pltpu.VMEM((places * chunk, panels.shape[2]), low_type) for chunk in chunks],
        14 * panels.size * groups[-1][3],
        sum(12 * shape[0] * shape[1] for shape in shapes),
    )(rank, panels, *map(in_hbm, moms), *map(in_hbm, weights))
    split, place = [], 0
    for count in counts:
        split.append(results[place : place + count])
        place += count
    return split


def panel_sums_kernel(parts, target):
    total = parts[0].astype(jnp.float32)
    for place in range(1, parts.shape[0]):
        total += parts[place].astype(jnp.float32)
    total = total.astype(low_type)
    for place in range(target.shape[0]):
        target[place, :, :] = total


def panel_sums(parts):
    return whole_call(
        panel_sums_kernel,
        "panel_sums",
        [],
        [parts],
        [shaped(parts.shape, low_type)],
        [],
        parts.size,
        4 * parts.size,
    )[0]


def polish(gram, gram_low, change_low, once_low, iterate, size):
    block = min(size, 512)
    count = size // block
    for step_index in range(NS_STEPS):
        last = step_index + 1 == NS_STEPS
        if last:
            first_term = matmul(iterate.astype(low_type), gram_low[...])
            second_term = matmul(first_term.astype(low_type), gram_low[...])
            return coef_first * iterate + coef_second * first_term + coef_third * second_term

        def make_change(index, carry):
            rows = block_at(index, block)
            square = matmul(gram_low[rows, :], gram_low[...])
            change_low[rows, :] = (coef_second * gram[rows, :] + coef_third * square).astype(
                low_type
            )
            return carry

        def make_once(index, carry):
            rows = block_at(index, block)
            once = matmul(gram_low[rows, :], change_low[...])
            once_low[rows, :] = once.astype(low_type)
            gram[rows, :] = (coef_first * coef_first) * gram[rows, :] + (2.0 * coef_first) * once
            return carry

        def make_gram(index, carry):
            rows = block_at(index, block)
            total = gram[rows, :] + matmul(once_low[rows, :], change_low[...])
            gram[rows, :] = total
            gram_low[rows, :] = total.astype(low_type)
            return carry

        lax.fori_loop(0, count, make_change, 0)
        iterate = coef_first * iterate + matmul(iterate.astype(low_type), change_low[...])
        lax.fori_loop(0, count, make_once, 0)
        lax.fori_loop(0, count, make_gram, 0)


def gram_parts_kernel(where, *refs):
    parts, gains, near_out, far_out, blocks = refs
    narrow = blocks.shape[1]
    chunk = blocks.shape[0] // (SIDE * CORES)
    extra = gains.shape[0] // (SIDE * CORES)
    places = parts.shape[0]
    tiles = parts.shape[1] // extra
    rows = jnp.concatenate(
        [
            jnp.concatenate(
                [parts[place, tile * extra : (tile + 1) * extra, :] for place in range(places)],
                axis=0,
            )
            for tile in range(tiles)
        ],
        axis=1,
    )
    wide = rows.shape[1] // narrow
    places = upper_blocks(wide - 2) + [(wide - 2, wide - 2), (wide - 1, wide - 1)]
    for index, (left, right) in enumerate(places):
        blocks[index * narrow : (index + 1) * narrow, :] = matmul_tn(
            rows[:, left * narrow : (left + 1) * narrow],
            rows[:, right * narrow : (right + 1) * narrow],
        ).astype(low_type)
    core = where[SIDE * CORES]
    for step in range(SIDE):
        near = CORES * step + core
        far = CORES * step + 1 - core
        for target, source, place in ((near_out, near, 0), (far_out, far, SIDE)):
            start = pl.multiple_of((where[source] - place) * (chunk + extra), extra)
            target[pl.ds(start, chunk), :] = blocks[block_at(source, chunk), :]
            start = pl.multiple_of(start + chunk, extra)
            target[pl.ds(start, extra), :] = gains[block_at(source, extra), :]


def gram_parts(where, parts, gains, narrow):
    places = parts.shape[0]
    extra = gains.shape[0] // (SIDE * CORES)
    width = parts.shape[1] // extra * LANES
    wide = width // narrow - 2
    total = (wide * (wide + 1) // 2 + 2) * narrow
    out_rows = (total + gains.shape[0]) // CORES
    return whole_call(
        gram_parts_kernel,
        "gram_parts",
        [where],
        [parts, gains],
        [shaped((out_rows, narrow), low_type)] * 2,
        [pltpu.VMEM((total, narrow), low_type)],
        2 * places * extra * total * narrow,
        4 * total * narrow,
    )


def shared_kernel(rows_all, owner, *refs):
    pieces = refs[: SIDE * CORES]
    own, *refs = refs[SIDE * CORES :]
    weights, targets, refs = refs[:3], refs[3:6], refs[6:]
    blocks, gram, gram_low, change_low, once_low = refs
    chunk, narrow = pieces[0].shape
    wide = gram.shape[0]
    for index, source in enumerate(pieces):
        blocks[block_at(owner[index], chunk), :] = source[...]
    places = upper_blocks(wide // narrow)
    trace = jnp.zeros((1, 1), jnp.float32)
    for index, (left, right) in enumerate(places):
        if left == right:
            trace += trace_of(blocks[index * narrow : (index + 1) * narrow, :].astype(jnp.float32))
    factor = 1.0 / (jnp.sqrt(trace) + 1e-07)
    for index, (left, right) in enumerate(places):
        block = blocks[index * narrow : (index + 1) * narrow, :].astype(jnp.float32)
        block = block * (factor * factor)
        rows = slice(left * narrow, (left + 1) * narrow)
        cols = slice(right * narrow, (right + 1) * narrow)
        gram[rows, cols] = block
        gram_low[rows, cols] = block.astype(low_type)
        if left != right:
            turned = block.T
            gram[cols, rows] = turned
            gram_low[cols, rows] = turned.astype(low_type)
    grams, starts = [], []
    for index in range(2):
        first = (len(places) + index) * narrow
        grams.append(blocks[first : first + narrow, :].astype(jnp.float32))
        starts.append(own[:, wide + index * narrow : wide + (index + 1) * narrow])
    for index, ortho in enumerate(polish_small(grams, starts, [False, False])):
        rate = muon_rate * math.sqrt(rows_all / narrow)
        targets[1 + index][...] = weights[1 + index][...].astype(jnp.float32) - rate * ortho
    ortho = polish(gram, gram_low, change_low, once_low, own[:, :wide] * factor, wide)
    rate = muon_rate * math.sqrt(rows_all / wide)
    targets[0][...] = weights[0][...].astype(jnp.float32) - rate * ortho


def shared_updates(owner, pieces, own, weights, rows_all):
    chunk, narrow = pieces[0].shape
    wide = weights[0].shape[1]

    def body(owner, *refs):
        shared_kernel(rows_all, owner, *refs)

    return whole_call(
        body,
        "shared_updates",
        [owner],
        [*map(in_hbm, pieces), in_hbm(own), *map(in_hbm, weights)],
        [shaped(weight.shape, jnp.float32) for weight in weights],
        [pltpu.VMEM((SIDE * CORES * chunk, narrow), low_type), pltpu.VMEM((wide, wide), jnp.float32)]
        + [pltpu.VMEM((wide, wide), low_type)] * 3,
        20 * wide * wide * wide,
        8 * wide * wide,
    )


def own_rows(weight, count, rank):
    share_rows = weight.shape[0] // count
    return lax.dynamic_slice_in_dim(weight, rank * share_rows, share_rows, 0)


def on_device(
    tokens_in,
    cotangent,
    seg_starts,
    gains,
    w_q_down,
    w_key,
    w_value,
    w_q_up,
    w_out,
    w_gate,
    w_up,
    w_down,
    mom_gains,
    mom_q_down,
    mom_key,
    mom_value,
    mom_q_up,
    mom_out,
    mom_gate,
    mom_up,
    mom_down,
):
    heads_count = lax.axis_size("heads")
    heads_rank = lax.axis_index("heads")
    dp_count = lax.axis_size("dp")
    dp_rank = lax.axis_index("dp")
    all_rank = lax.axis_index(("dp", "heads"))
    all_count = dp_count * heads_count
    local_rows = tokens_in.shape[0]
    row_len = local_rows * heads_count
    model_width = tokens_in.shape[1]
    latent_width = w_q_down.shape[1]
    head_dim = w_key.shape[1]
    local_q = w_q_up.shape[1]
    share_rows = model_width // all_count
    share_gains = gains.shape[0] // all_count
    starts = seg_starts[0]
    whole_index = jnp.arange(row_len, dtype=jnp.int32)
    own_index = heads_rank * local_rows + jnp.arange(local_rows, dtype=jnp.int32)
    own_core = heads_rank % CORES
    own_step = heads_rank // CORES
    ranks = jnp.arange(heads_count, dtype=jnp.int32)
    where = SIDE * ((ranks % CORES) ^ own_core) + (ranks // CORES - own_step) % SIDE
    where = jnp.concatenate([where, own_core[None]]).astype(jnp.int32)
    owner = CORES * ((ranks % SIDE + own_step) % SIDE) + ((ranks // SIDE) ^ own_core)
    owner = owner.astype(jnp.int32)
    dp_place = dp_rank[None].astype(jnp.int32)
    gain_one = gains[:model_width]
    gain_latent = gains[model_width : model_width + latent_width]
    gain_two = gains[model_width + latent_width :]

    inputs = tokens_in.astype(jnp.float32)
    scale_one = rms_scale(inputs)
    normed_one = (inputs * scale_one * gain_one).astype(low_type)
    latent_raw = matmul(normed_one, w_q_down)
    scale_latent = rms_scale(latent_raw)
    latent_normed = (latent_raw * scale_latent * gain_latent).astype(low_type)
    own_pos = segment_info(starts, own_index)[1]
    own_cos, own_sin = rotary_tables(own_pos, head_dim)
    key_local = rotate(matmul(normed_one, w_key), own_cos, own_sin).astype(low_type)
    value_local = matmul(normed_one, w_value).astype(low_type)
    packed = lax.all_gather(
        jnp.concatenate([latent_normed, key_local, value_local], axis=1), "heads", axis=0, tiled=True
    )
    grad_rows = lax.all_gather(after(cotangent, packed), "heads", axis=0, tiled=True)
    normed_parts = lax.all_to_all(
        normed_one.T.reshape(dp_count, heads_count, share_rows, local_rows)
        .transpose(1, 0, 2, 3)
        .reshape(model_width, local_rows),
        "heads",
        split_axis=0,
        concat_axis=0,
        tiled=True,
    )
    shared_rows = [own_rows(weight, all_count, all_rank) for weight in (w_q_down, w_key, w_value)]
    packed, normed_parts, shared_rows = lax.optimization_barrier(
        (packed, normed_parts, shared_rows)
    )
    row_ids, row_pos = segment_info(starts, whole_index)
    row_cos, row_sin = rotary_tables(row_pos, head_dim)
    query_rows, attended_near, attended_far, lse = attend(
        where, packed, w_q_up, head_dim, row_cos, row_sin, row_ids
    )
    attn_mixed = ring_sums(
        ring_operands(
            chip_sums(
                matmul_nt(attended_far, w_out).astype(low_type),
                matmul_nt(attended_near, w_out).astype(low_type),
            )
        )
    )
    hidden_one = inputs + attn_mixed
    scale_two = rms_scale(hidden_one)
    normed_two = (hidden_one * scale_two * gain_two).astype(low_type)

    gate_turned, up_turned, down_turned = w_gate.T, w_up.T, w_down.T
    pieces_two = gather_heads(normed_two)
    gate_near, up_near, middle_near, back_near = ffn_half(
        owner, pieces_two[:SIDE], grad_rows, gate_turned, up_turned, down_turned, 0
    )
    gate_far, up_far, middle_far, back_far = ffn_half(
        owner, pieces_two[SIDE:], grad_rows, gate_turned, up_turned, down_turned, 1
    )
    chip_two = ring_operands(chip_sums(back_far, back_near))
    normed_two_back = ring_sums(chip_two)
    ffn_part = ffn_grads(
        owner,
        pieces_two,
        grad_rows,
        (after(gate_near, *chip_two), up_near, middle_near, gate_far, up_far, middle_far),
        dp_count,
    )
    ffn_sums = lax.psum_scatter(ffn_part, "dp", scatter_dimension=0, tiled=True)[0]
    mixed_far = matmul_tn(after(middle_far, *chip_two), down_turned).astype(low_type)
    mixed_near = matmul_tn(after(middle_near, *chip_two), down_turned).astype(low_type)
    hidden_part, gain_two_grad = norm_back(hidden_one, scale_two, gain_two, normed_two_back)
    hidden_back = cotangent.astype(jnp.float32) + hidden_part

    hidden_low = after(hidden_back.astype(low_type), ffn_part, mixed_far, mixed_near)
    pieces_hidden, *chip_mixed = gather_heads(
        hidden_low, tuple(ring_operands(chip_sums(mixed_far, mixed_near)))
    )
    q_up_part, sums_near, sums_far = attend_back(
        where, pieces_hidden, query_rows, packed, w_out, w_q_up, lse, row_cos, row_sin, row_ids
    )
    chip_back = ring_operands(chip_sums(sums_far, sums_near))
    packed_sums = ring_sums(chip_back)
    head_parts = head_grads(
        pieces_hidden, (after(attended_near, *chip_back), attended_far), q_up_part, dp_count
    )
    packed_sums, head_parts = lax.optimization_barrier((packed_sums, head_parts))
    head_sums = lax.psum_scatter(head_parts, "dp", scatter_dimension=0, tiled=True)[0]
    latent_back = packed_sums[:, :latent_width]
    key_sum = packed_sums[:, latent_width : latent_width + head_dim]
    value_sum = packed_sums[:, latent_width + head_dim :]
    latent_raw_grad, gain_latent_grad = norm_back(
        latent_raw, scale_latent, gain_latent, latent_back
    )
    latent_raw_back = latent_raw_grad.astype(low_type)
    key_pre_back = rotate_back(key_sum, own_cos, own_sin).astype(low_type)
    values_low = value_sum.astype(low_type)

    back_low = jnp.concatenate([latent_raw_back, key_pre_back, values_low], axis=1)
    latent_out = matmul_nt(latent_raw_back, w_q_down)
    pieces_back, latent_out = gather_heads(back_low, (latent_out,))
    normed_one_back = (
        latent_out
        + matmul_nt(key_pre_back, w_key)
        + matmul_nt(values_low, w_value)
    )
    input_part, gain_one_grad = norm_back(inputs, scale_one, gain_one, normed_one_back)
    input_grad = hidden_back + input_part
    gains_part = jnp.concatenate([gain_one_grad, gain_latent_grad, gain_two_grad])
    gains_part = gains_part.reshape(dp_count, heads_count, share_gains).astype(low_type)
    gains_part = jnp.pad(
        gains_part, ((0, 0), (0, share_rows - heads_count), (0, LANES - share_gains))
    )

    shared_part = shared_parts_of(owner, normed_parts, pieces_back, gains_part)
    *shared_grads, gains_dp, shared_mom, next_parts = shared_momenta(
        exchange_dp(shared_part), (mom_q_down, mom_key, mom_value), share_rows
    )
    q_down_grad, key_w_grad, value_w_grad, q_down_mom, key_w_mom, value_w_mom = shared_grads

    gains_rows = jnp.pad(
        gains_dp[:heads_count, None, :share_gains].astype(low_type),
        ((0, 0), (0, share_rows - 1), (0, head_dim - share_gains)),
    ).reshape(heads_count * share_rows, head_dim)
    ffn_grad, ffn_mom, ffn_gram = momenta(
        after(ffn_sums, shared_mom),
        (mom_gate.T, mom_up.T, mom_down.T),
        FF_BLOCK,
        True,
        "ffn_momenta",
    )
    parts_mom, ffn_gram = lax.optimization_barrier((exchange_dp(next_parts), ffn_gram))
    gram_near, gram_far = gram_parts(where, parts_mom, gains_rows, head_dim)
    chip_gram = ring_operands(chip_sums(gram_far, gram_near))
    gram_sums = ring_sums(chip_gram)
    head_grad, head_mom, head_gram = momenta(
        head_sums, (mom_q_up, mom_out), head_dim, False, "head_momenta"
    )
    gram_chunk = gram_sums.shape[0] - share_rows
    panels = jnp.concatenate(
        [
            after(panel, gram_sums).reshape(dp_count, -1, panel.shape[1])
            for panel in (ffn_gram, head_gram)
        ],
        axis=1,
    )
    pieces_gram, panels = gather_heads(
        gram_sums[:gram_chunk].astype(low_type), (exchange_dp(panels),)
    )
    panels = panel_sums(panels)
    pieces_gram, panels, chip_mixed = lax.optimization_barrier((pieces_gram, panels, chip_mixed))
    panels = exchange_dp(panels)
    layer_out = (hidden_one + ring_sums(chip_mixed)).astype(low_type)
    gains_grad = gram_sums[gram_chunk, :share_gains]
    gains_mom = decay_rate * mom_gains + gains_grad
    gains_new = own_rows(gains, all_count, all_rank) - gain_rate * gains_mom

    shared_new = shared_updates(
        owner,
        pieces_gram,
        shared_mom,
        shared_rows,
        model_width,
    )
    shared_new, panels, layer_out = lax.optimization_barrier((shared_new, panels, layer_out))
    ffn_new, (q_up_new, out_w_new) = updates(
        dp_place,
        panels,
        (
            (ffn_mom, (gate_turned, up_turned, down_turned), FF_BLOCK, True),
            (head_mom, (w_q_up, w_out), head_dim, False),
        ),
        "block_updates",
    )
    ffn_grad, ffn_mom, ffn_new = [
        [array.T for array in arrays] for arrays in (ffn_grad, ffn_mom, ffn_new)
    ]
    return (
        layer_out,
        input_grad,
        gains_grad,
        q_down_grad,
        key_w_grad,
        value_w_grad,
        *head_grad,
        *ffn_grad,
        gains_mom,
        q_down_mom,
        key_w_mom,
        value_w_mom,
        *head_mom,
        *ffn_mom,
        gains_new,
        *shared_new,
        q_up_new,
        out_w_new,
        *ffn_new,
    )


def solution(mesh):
    placed = (
        P(("dp", "heads"), None),
        P(("dp", "heads"), None),
        P("dp", None),
        P(),
        P(),
        P(),
        P(),
        P(None, "heads"),
        P(None, "heads"),
        P(None, "heads"),
        P(None, "heads"),
        P(None, "heads"),
        P(("dp", "heads")),
        P(("dp", "heads"), None),
        P(("dp", "heads"), None),
        P(("dp", "heads"), None),
        P("dp", "heads"),
        P("dp", "heads"),
        P("dp", "heads"),
        P("dp", "heads"),
        P("dp", "heads"),
    )
    return jax.shard_map(
        on_device,
        mesh=mesh,
        in_specs=placed,
        out_specs=(
            P(("dp", "heads"), None),
            P(("dp", "heads"), None),
            P(("dp", "heads")),
            P(("dp", "heads"), None),
            P(("dp", "heads"), None),
            P(("dp", "heads"), None),
            P("dp", "heads"),
            P("dp", "heads"),
            P("dp", "heads"),
            P("dp", "heads"),
            P("dp", "heads"),
            P(("dp", "heads")),
            P(("dp", "heads"), None),
            P(("dp", "heads"), None),
            P(("dp", "heads"), None),
            P("dp", "heads"),
            P("dp", "heads"),
            P("dp", "heads"),
            P("dp", "heads"),
            P("dp", "heads"),
            P(("dp", "heads")),
            P(("dp", "heads"), None),
            P(("dp", "heads"), None),
            P(("dp", "heads"), None),
            P("dp", "heads"),
            P("dp", "heads"),
            P("dp", "heads"),
            P("dp", "heads"),
            P("dp", "heads"),
        ),
        check_vma=False,
    )
```

```python
import math

import jax
import jax.numpy as jnp
from jax import lax
from jax.experimental import pallas as pl
from jax.experimental.pallas import tpu as pltpu
from jax.sharding import PartitionSpec as P

NS_STEPS = 3
FF_BLOCK = 352
SIDE = 4
CORES = 2
LANES = 128

coef_first = 3.4445
coef_second = -4.775
coef_third = 2.0315
muon_rate = 0.5
gain_rate = 0.004
decay_rate = 0.5
low_type = jnp.bfloat16


def matmul(left, right):
    return jnp.dot(left, right, preferred_element_type=jnp.float32)


def matmul_nt(left, right):
    return lax.dot_general(
        left, right, (((1,), (1,)), ((), ())), preferred_element_type=jnp.float32
    )


def matmul_tn(left, right):
    return lax.dot_general(
        left, right, (((0,), (0,)), ((), ())), preferred_element_type=jnp.float32
    )


def rms_scale(values):
    return lax.rsqrt(jnp.mean(values * values, axis=-1, keepdims=True) + 1e-05)


def norm_back(values, scale, gain, grad_out):
    weighted = gain * grad_out
    inner = jnp.mean(values * weighted, axis=-1, keepdims=True)
    grad_in = scale * weighted - values * (scale * scale * scale) * inner
    gain_grad = jnp.sum(grad_out * values * scale, axis=0)
    return (grad_in, gain_grad)


def segment_info(starts, token_index):
    started = starts[None, :] <= token_index[:, None]
    seg_ids = jnp.sum(started.astype(jnp.int32), axis=1)
    seg_begin = jnp.max(jnp.where(started, starts[None, :], 0), axis=1)
    return (seg_ids, token_index - seg_begin)


def rotary_tables(positions, head_dim):
    half_dim = head_dim // 2
    frequency = jnp.exp(
        jnp.arange(half_dim, dtype=jnp.float32) * (-2.0 * math.log(10000.0) / head_dim)
    )
    angles = positions.astype(jnp.float32)[:, None] * frequency[None, :]
    return (jnp.cos(angles), jnp.sin(angles))


def rotate(values, cosine, sine_part):
    half_dim = values.shape[-1] // 2
    first_half = values[..., :half_dim]
    second_half = values[..., half_dim:]
    return jnp.concatenate(
        [
            first_half * cosine - second_half * sine_part,
            second_half * cosine + first_half * sine_part,
        ],
        axis=-1,
    )


def rotate_back(grads, cosine, sine_part):
    return rotate(grads, cosine, -sine_part)


def shift_heads(values, step, core):
    pairs = [
        (CORES * place + side, CORES * ((place + step) % SIDE) + (side ^ core))
        for place in range(SIDE)
        for side in range(CORES)
    ]
    return lax.ppermute(values, "heads", pairs)


def shift_dp(values, step_z, step_x):
    pairs = [
        (SIDE * z + x, SIDE * ((z + step_z) % SIDE) + (x + step_x) % SIDE)
        for z in range(SIDE)
        for x in range(SIDE)
    ]
    return lax.ppermute(values, "dp", pairs)


def gather_heads(own, beside=()):
    ring = [own] + [shift_heads(own, -step, 0) for step in range(1, SIDE)]
    ring, beside = lax.optimization_barrier((ring, beside))
    pieces = ring + [shift_heads(piece, 0, 1) for piece in ring]
    return (pieces, *beside) if beside else pieces


def chip_sums(far_half, near_half):
    rows = near_half.shape[0] // SIDE
    total = near_half.astype(jnp.float32) + shift_heads(far_half, 0, 1).astype(jnp.float32)
    return total.astype(far_half.dtype).reshape(SIDE, rows, *near_half.shape[1:])


def ring_operands(chip):
    return lax.optimization_barrier([chip[step] for step in range(SIDE)])


def ring_sums(operands):
    total = operands[0].astype(jnp.float32)
    for step in range(1, SIDE):
        total = total + shift_heads(operands[step], step, 0).astype(jnp.float32)
    return total


def pick(array, place, axis):
    return lax.dynamic_index_in_dim(array, place % SIDE, axis, keepdims=False)


def scatter_x(parts):
    place_x = lax.axis_index("dp") % SIDE
    grid = parts.reshape(SIDE, SIDE, *parts.shape[1:])
    total = pick(grid, place_x, 1).astype(jnp.float32)
    for step in range(1, SIDE):
        total = total + shift_dp(pick(grid, place_x + step, 1), 0, step).astype(jnp.float32)
    return total.astype(parts.dtype)


def scatter_z(column):
    place_z = lax.axis_index("dp") // SIDE
    total = pick(column, place_z, 0).astype(jnp.float32)
    for step in range(1, SIDE):
        total = total + shift_dp(pick(column, place_z + step, 0), step, 0).astype(jnp.float32)
    return total


def line_sum(part, axis):
    total = part.astype(jnp.float32)
    for step in range(1, SIDE):
        total = total + shift_dp(part, step * axis, step * (1 - axis)).astype(jnp.float32)
    return total.astype(part.dtype)


def exchange_dp(parts):
    return lax.all_to_all(parts, "dp", split_axis=0, concat_axis=0, tiled=True)


def after(values, *earlier):
    return lax.optimization_barrier((values, *earlier))[0]


vmem_mib = {
    "attend": 14,
    "attend_back": 20,
    "ffn_near": 26,
    "ffn_far": 26,
    "ffn_grads": 32,
    "head_grads": 16,
    "shared_updates": 24,
    "block_updates": 28,
}


def in_hbm(array):
    return pltpu.with_memory_space_constraint(array, pltpu.HBM)


def streamed_call(
    body, name, scalars, resident, arrays, out_shape, scratch, flops, moved, cuts, merged
):
    kinds, pieces = [], []
    for index, array in enumerate(arrays):
        rows = array.shape[0] if index not in cuts else cuts[index][0]
        if index < merged:
            rows = merged * array.shape[0] if index == 0 else 16
        kinds.append(pltpu.VMEM((rows, *array.shape[1:]), array.dtype))
        pieces.append(1 if index not in cuts else cuts[index][1])
    count, outs = len(arrays), len(out_shape)

    def wrapped(*refs):
        numbers, refs = refs[: len(scalars)], refs[len(scalars) :]
        still, refs = refs[: len(resident)], refs[len(resident) :]
        sources, refs = refs[:count], refs[count:]
        targets, refs = refs[:outs], refs[outs:]
        held, sems, rest = refs[:count], refs[count], refs[count + 1 :]
        copies, place = [], 0
        for index, source in enumerate(sources):
            parts = [(source, held[index])]
            if index < merged:
                rows = source.shape[0]
                parts = [(source, held[0].at[index * rows : (index + 1) * rows, :])]
            if index in cuts:
                parts = cuts[index][2](numbers, source, held[index])
            group = []
            for part_from, part_to in parts:
                group.append(pltpu.make_async_copy(part_from, part_to, sems.at[place]))
                place += 1
            copies.append(group)
        for group in copies:
            for copy in group:
                copy.start()
        done = [0]

        def ready(index):
            while done[0] <= index:
                for copy in copies[done[0]]:
                    copy.wait()
                done[0] += 1

        body(ready, numbers, still, held, targets, rest)
        ready(count - 1)

    return pl.pallas_call(
        wrapped,
        grid_spec=pltpu.PrefetchScalarGridSpec(
            num_scalar_prefetch=len(scalars),
            grid=(1,),
            in_specs=[pl.BlockSpec(memory_space=pltpu.VMEM)] * len(resident)
            + [pl.BlockSpec(memory_space=pltpu.HBM)] * count,
            out_specs=[pl.BlockSpec(memory_space=pltpu.VMEM)] * outs,
            scratch_shapes=[*kinds, pltpu.SemaphoreType.DMA((sum(pieces),)), *scratch],
        ),
        out_shape=out_shape,
        compiler_params=pltpu.CompilerParams(
            vmem_limit_bytes=vmem_mib.get(name, 12) * 1024 * 1024
        ),
        cost_estimate=pl.CostEstimate(flops=flops, bytes_accessed=moved, transcendentals=0),
        name=name,
    )(*scalars, *resident, *[in_hbm(array) for array in arrays])


def whole_call(body, name, scalars, arrays, out_shape, scratch, flops, moved):
    return pl.pallas_call(
        body,
        in_specs=[pl.BlockSpec(memory_space=pltpu.SMEM)] * len(scalars)
        + [pl.BlockSpec(memory_space=pltpu.VMEM)] * len(arrays),
        out_specs=jax.tree.map(lambda _: pl.BlockSpec(memory_space=pltpu.VMEM), out_shape),
        out_shape=out_shape,
        scratch_shapes=scratch,
        compiler_params=pltpu.CompilerParams(
            vmem_limit_bytes=vmem_mib.get(name, 12) * 1024 * 1024
        ),
        cost_estimate=pl.CostEstimate(flops=flops, bytes_accessed=moved, transcendentals=0),
        name=name,
    )(*scalars, *arrays)


def kernel_call(body, name, grid, prefetch, in_specs, out_specs, out_shape, scratch, flops, moved):
    return pl.pallas_call(
        body,
        grid_spec=pltpu.PrefetchScalarGridSpec(
            num_scalar_prefetch=prefetch,
            grid=grid,
            in_specs=in_specs,
            out_specs=out_specs,
            scratch_shapes=scratch,
        ),
        out_shape=out_shape,
        compiler_params=pltpu.CompilerParams(vmem_limit_bytes=vmem_mib.get(name, 12) * 1024 * 1024),
        cost_estimate=pl.CostEstimate(flops=flops, bytes_accessed=moved, transcendentals=0),
        name=name,
    )


def shaped(shape, kind):
    return jax.ShapeDtypeStruct(shape, kind)


def fixed(shape):
    return pl.BlockSpec(
        shape, lambda *grid: (0,) * len(shape), pipeline_mode=pl.Buffered(buffer_count=1)
    )


def visible(ids_q, ids_k, first_row, rows, cols):
    query_at = first_row + lax.broadcasted_iota(jnp.int32, (rows, cols), 0)
    key_at = lax.broadcasted_iota(jnp.int32, (rows, cols), 1)
    return (ids_q == ids_k) & (key_at <= query_at)


def block_at(index, piece):
    return pl.ds(pl.multiple_of(index * piece, piece), piece)


def store_by_distance(where, rows_ref, near_ref, far_ref, piece):
    core = where[SIDE * CORES]
    for step in range(SIDE):
        near = CORES * step + core
        far = CORES * step + 1 - core
        near_ref[block_at(where[near], piece), :] = rows_ref[block_at(near, piece), :].astype(
            near_ref.dtype
        )
        far_ref[block_at(where[far] - SIDE, piece), :] = rows_ref[block_at(far, piece), :].astype(
            far_ref.dtype
        )


def attend_kernel(
    where, packed, w_q_up, cosine, sine, ids_q, ids_k, query_out, near_out, far_out, lse_out, mixed
):
    row_len, packed_width = packed.shape
    latent_width, width = w_q_up.shape
    head_dim = (packed_width - latent_width) // 2
    piece = row_len // (SIDE * CORES)
    block = CORES * piece
    scale = head_dim ** (-0.5)
    key_cols = slice(latent_width, latent_width + head_dim)
    value_cols = slice(latent_width + head_dim, latent_width + 2 * head_dim)
    for head in range(width // head_dim):
        cols = slice(head * head_dim, (head + 1) * head_dim)
        for index in range(SIDE):
            first = index * block
            end = first + block
            rows = slice(first, end)
            query = matmul(packed[rows, :latent_width], w_q_up[:, cols])
            query = rotate(query, cosine[rows, :], sine[rows, :]).astype(low_type)
            query_out[rows, cols] = query
            scores = matmul_nt(query, packed[:end, key_cols]) * scale
            allowed = visible(ids_q[rows, :], ids_k[:, :end], first, block, end)
            scores = jnp.where(allowed, scores, -1e30)
            row_max = jnp.max(scores, axis=-1, keepdims=True)
            exponent = jnp.exp(scores - row_max)
            row_total = jnp.sum(exponent, axis=-1, keepdims=True)
            probs = (exponent * (1.0 / row_total)).astype(low_type)
            lse_out[head, rows, :] = row_max + jnp.log(row_total)
            mixed[rows, cols] = matmul(probs, packed[:end, value_cols]).astype(low_type)
    store_by_distance(where, mixed, near_out, far_out, piece)


def attend(where, packed, w_q_up, head_dim, cosine, sine, row_ids):
    row_len = packed.shape[0]
    latent_width, width = w_q_up.shape
    return whole_call(
        attend_kernel,
        "attend",
        [where],
        [packed, w_q_up, cosine, sine, row_ids[:, None], row_ids[None, :]],
        [
            shaped((row_len, width), low_type),
            shaped((row_len // 2, width), low_type),
            shaped((row_len // 2, width), low_type),
            shaped((width // head_dim, row_len, 1), jnp.float32),
        ],
        [pltpu.VMEM((row_len, width), low_type)],
        2 * width * row_len * (latent_width + 2 * row_len),
        8 * row_len * width,
    )


def attend_back_kernel(where, *refs):
    pieces = refs[: SIDE * CORES]
    query_in, packed, w_out, w_q_up, lse, cosine, sine, ids_q, ids_k = refs[
        SIDE * CORES : SIDE * CORES + 9
    ]
    weight_back, near_out, far_out, query_back, back_rows, totals = refs[SIDE * CORES + 9 :]
    row_len, packed_width = packed.shape
    latent_width, width = w_q_up.shape
    head_dim = (packed_width - latent_width) // 2
    piece = row_len // (SIDE * CORES)
    block = CORES * piece
    scale = head_dim ** (-0.5)
    key_cols = slice(latent_width, latent_width + head_dim)
    value_cols = slice(latent_width + head_dim, latent_width + 2 * head_dim)
    for index in range(0, SIDE * CORES, 2):
        pair = jnp.concatenate([pieces[index][...], pieces[index + 1][...]], axis=0)
        back_rows[index * piece : (index + 2) * piece, :] = matmul(pair, w_out[...]).astype(
            low_type
        )
    totals[:, latent_width:] = jnp.zeros((row_len, 2 * head_dim), jnp.float32)
    for head in range(width // head_dim):
        cols = slice(head * head_dim, (head + 1) * head_dim)
        for index in range(SIDE):
            first = index * block
            end = first + block
            rows = slice(first, end)
            query = query_in[rows, cols]
            back = jnp.concatenate(
                [
                    back_rows[block_at(where[CORES * index + side], piece), cols]
                    for side in range(CORES)
                ],
                axis=0,
            )
            keys = packed[:end, key_cols]
            scores = matmul_nt(query, keys) * scale
            allowed = visible(ids_q[rows, :], ids_k[:, :end], first, block, end)
            probs = jnp.where(allowed, jnp.exp(scores - lse[head, rows, :]), 0.0)
            probs_back = matmul_nt(back, packed[:end, value_cols])
            inner = jnp.sum(probs * probs_back, axis=-1, keepdims=True)
            score_back = (probs * (probs_back - inner)).astype(low_type)
            totals[:end, value_cols] += matmul_tn(probs.astype(low_type), back)
            totals[:end, key_cols] += matmul_tn(score_back, query) * scale
            query_grad = matmul(score_back, keys) * scale
            query_back[rows, cols] = rotate_back(
                query_grad, cosine[rows, :], sine[rows, :]
            ).astype(low_type)
    for index in range(SIDE):
        rows = slice(index * block, (index + 1) * block)
        totals[rows, :latent_width] = matmul_nt(query_back[rows, :], w_q_up[...])
    store_by_distance(where, totals, near_out, far_out, piece)
    weight_back[...] = matmul_tn(packed[:, :latent_width], query_back[...]).astype(low_type)


def attend_back(where, pieces, query_rows, packed, w_out, w_q_up, lse, cosine, sine, row_ids):
    row_len, packed_width = packed.shape
    latent_width, width = w_q_up.shape
    model_width = w_out.shape[0]
    return whole_call(
        attend_back_kernel,
        "attend_back",
        [where],
        [
            *pieces,
            query_rows,
            packed,
            w_out,
            w_q_up,
            lse,
            cosine,
            sine,
            row_ids[:, None],
            row_ids[None, :],
        ],
        [
            shaped((latent_width, width), low_type),
            shaped((row_len // 2, packed_width), low_type),
            shaped((row_len // 2, packed_width), low_type),
        ],
        [
            pltpu.VMEM((row_len, width), low_type),
            pltpu.VMEM((row_len, width), low_type),
            pltpu.VMEM((row_len, packed_width), jnp.float32),
        ],
        2 * width * row_len * (5 * row_len + model_width + 2 * latent_width),
        8 * row_len * width,
    )


def ffn_kernel(ready, numbers, still, held, targets, rest):
    w_gate = still[0]
    features, (w_up, grads, w_down) = held[0], held[SIDE:]
    gate_out, up_out, middle_out, features_back = targets
    gate_raw, up_raw = rest
    width = w_gate.shape[0]
    chunk = width // 2
    tile = features.shape[1] // 4

    def rows_of(part):
        return pl.ds(pl.multiple_of(part * chunk, chunk), chunk)

    def make_gate(part, carry):
        rows = rows_of(part)
        gate_raw[rows, :] = matmul_nt(w_gate[rows, :], features[...])
        return carry

    def make_up(part, carry):
        rows = rows_of(part)
        up_raw[rows, :] = matmul_nt(w_up[rows, :], features[...])
        return carry

    def make_backs(part, carry):
        rows = rows_of(part)
        middle_back = matmul_nt(w_down[rows, :], grads[...])
        gate, up = gate_raw[rows, :], up_raw[rows, :]
        sigmoid = jax.nn.sigmoid(gate)
        activated = gate * sigmoid
        middle_out[rows, :] = (activated * up).astype(low_type)
        gate_out[rows, :] = (
            middle_back * up * sigmoid * (1.0 + gate * (1.0 - sigmoid))
        ).astype(low_type)
        up_out[rows, :] = (middle_back * activated).astype(low_type)
        return carry

    def make_features(part, carry):
        area = pl.ds(pl.multiple_of(part * tile, tile), tile)
        features_back[:, area] = (
            matmul_tn(gate_out[...], w_gate[:, area]) + matmul_tn(up_out[...], w_up[:, area])
        ).astype(low_type)
        return carry

    ready(SIDE - 1)
    lax.fori_loop(0, 2, make_gate, 0)
    ready(SIDE)
    lax.fori_loop(0, 2, make_up, 0)
    ready(SIDE + 2)
    lax.fori_loop(0, 2, make_backs, 0)
    lax.fori_loop(0, 4, make_features, 0)


def ffn_half(owner, pieces, grads, w_gate, w_up, w_down, far):
    piece, model_width = pieces[0].shape
    width = w_gate.shape[0]
    rows = SIDE * piece

    def own_blocks(numbers, source, target):
        return [
            (
                source.at[block_at(numbers[0][SIDE * far + step], piece), :],
                target.at[step * piece : (step + 1) * piece, :],
            )
            for step in range(SIDE)
        ]

    return streamed_call(
        ffn_kernel,
        "ffn_far" if far else "ffn_near",
        [owner],
        [w_gate],
        [*pieces, w_up, grads, w_down],
        [shaped((width, rows), low_type)] * 3 + [shaped((rows, model_width), low_type)],
        [pltpu.VMEM((width, rows), jnp.float32)] * 2,
        10 * rows * model_width * width,
        6 * model_width * width + 6 * rows * model_width,
        {SIDE + 1: (rows, SIDE, own_blocks)},
        SIDE,
    )


def ffn_grads_kernel(owner, *refs):
    count = SIDE * CORES
    pieces, grads, halves, target = refs[:count], refs[count], refs[count + 1 : -1], refs[-1]
    width, half_rows = halves[0].shape
    piece = pieces[0].shape[0]
    places, share = target.shape[0], target.shape[2]
    block = places * share
    cols = pl.ds(pl.multiple_of(pl.program_id(0) * block, block), block)
    features = jnp.concatenate([source[:, cols] for source in pieces], axis=0)
    grads = jnp.concatenate(
        [grads[block_at(owner[index], piece), cols] for index in range(count)], axis=0
    )
    for index, right in enumerate((features, features, grads)):
        total = matmul(halves[index][...], right[:half_rows, :])
        total += matmul(halves[index + 3][...], right[half_rows:, :])
        total = total.astype(low_type)
        for place in range(places):
            target[place, index * width : (index + 1) * width, :] = total[
                :, place * share : (place + 1) * share
            ]


def ffn_grads(owner, pieces, grads, halves, dp_count):
    piece, model_width = pieces[0].shape
    row_len = grads.shape[0]
    width = halves[0].shape[0]
    block = model_width // 4
    share = model_width // dp_count
    return kernel_call(
        ffn_grads_kernel,
        "ffn_grads",
        (4,),
        1,
        [fixed((piece, model_width))] * len(pieces)
        + [fixed((row_len, model_width))]
        + [fixed(halves[0].shape)] * 6,
        pl.BlockSpec((block // share, 3 * width, share), lambda index, owner: (index, 0, 0)),
        pltpu.HBM((dp_count, 3 * width, share), low_type),
        [],
        6 * row_len * model_width * width,
        4 * row_len * model_width + 6 * model_width * width,
    )(owner, *map(in_hbm, pieces), in_hbm(grads), *halves)


def head_grads(pieces, halves, q_up_part, dp_count):
    piece, model_width = pieces[0].shape
    count = len(pieces)
    width = halves[0].shape[1]
    steps = 4
    block = model_width // steps
    each = dp_count // steps
    q_up_rows = q_up_part.shape[0] // dp_count
    out_rows = model_width // dp_count
    rows = piece * count

    def body(*refs):
        sources, (near, far, above, target) = refs[:count], refs[count:]
        cols = pl.ds(pl.multiple_of(pl.program_id(0) * block, block), block)
        left = jnp.concatenate([source[:, cols] for source in sources], axis=0)
        right = jnp.concatenate([near[...], far[...]], axis=0)
        total = matmul_tn(left, right)
        for index in range(each):
            first = index * q_up_rows
            target[index, :q_up_rows, :] = above[first : first + q_up_rows, :]
            first = index * out_rows
            target[index, q_up_rows:, :] = total[first : first + out_rows, :].astype(low_type)

    return kernel_call(
        body,
        "head_grads",
        (steps,),
        0,
        [fixed((piece, model_width))] * count
        + [fixed(source.shape) for source in halves]
        + [pl.BlockSpec((each * q_up_rows, width), lambda index: (index, 0))],
        pl.BlockSpec((each, q_up_rows + out_rows, width), lambda index: (index, 0, 0)),
        pltpu.HBM((dp_count, q_up_rows + out_rows, width), low_type),
        [],
        2 * rows * model_width * width,
        2 * rows * (model_width + width) + 4 * model_width * width,
    )(*map(in_hbm, pieces), *map(in_hbm, halves), q_up_part)


def shared_parts_kernel(count, owner, *refs):
    left, right, gains, target = refs[:count], refs[count:-2], refs[-2], refs[-1]
    left = jnp.concatenate([source[...] for source in left], axis=1)
    right = jnp.concatenate([source[...] for source in right], axis=0)
    total = matmul(left, right).astype(low_type)
    places, extra = gains.shape[0], gains.shape[1]
    rows = total.shape[0] // places
    tiles = total.shape[1] // LANES
    for place in range(places):
        for tile in range(tiles):
            target[place, tile * rows : (tile + 1) * rows, :] = total[
                place * rows : (place + 1) * rows, tile * LANES : (tile + 1) * LANES
            ]
        first = tiles * rows
        target[place, first : first + extra, :] = gains[place, :, :]


def shared_parts_of(owner, left, right, gains):
    count = len(right)
    width = left.shape[0] // count
    piece, cols = right[0].shape
    places = gains.shape[0]
    rows = width // places * (cols // LANES) + gains.shape[1]

    def body(owner, *refs):
        shared_parts_kernel(count, owner, *refs)

    return kernel_call(
        body,
        "shared_parts",
        (1,),
        1,
        [
            pl.BlockSpec((width, piece), lambda index, owner, place=place: (owner[place], 0))
            for place in range(count)
        ]
        + [fixed(source.shape) for source in right]
        + [fixed(gains.shape)],
        fixed((places, rows, LANES)),
        shaped((places, rows, LANES), low_type),
        [],
        2 * piece * count * width * cols,
        2 * piece * count * (width + cols) + 2 * width * cols,
    )(owner, *([in_hbm(left)] * count), *right, gains)


def shared_momenta_kernel(parts, q_down, key, value, *refs):
    grads, moms, gains_out, own, target = refs[:3], refs[3:6], refs[6], refs[7], refs[8]
    total = parts[0].astype(jnp.float32)
    for place in range(1, parts.shape[0]):
        total += parts[place].astype(jnp.float32)
    rows = q_down.shape[0]
    tiles = own.shape[1] // LANES
    first = 0
    for tile in range(tiles):
        own[:, tile * LANES : (tile + 1) * LANES] = total[tile * rows : (tile + 1) * rows, :]
    for old, grad_out, mom_out in zip((q_down, key, value), grads, moms):
        cols = slice(first, first + old.shape[1])
        grad = own[:, cols]
        new = decay_rate * old[...] + grad
        grad_out[...] = grad
        mom_out[...] = new
        own[:, cols] = new
        first += old.shape[1]
    head = tiles * rows
    extra = gains_out.shape[0]
    gains_out[...] = total[head : head + extra, :]
    for place in range(target.shape[0]):
        for tile in range(tiles):
            target[place, tile * rows : (tile + 1) * rows, :] = own[
                :, tile * LANES : (tile + 1) * LANES
            ].astype(low_type)


def shared_momenta(parts, old, extra):
    places, rows, _ = parts.shape
    shapes = [array.shape for array in old]
    width = sum(shape[1] for shape in shapes)
    return whole_call(
        shared_momenta_kernel,
        "shared_momenta",
        [],
        [parts, *old],
        [shaped(shape, jnp.float32) for shape in shapes + shapes]
        + [
            shaped((extra, LANES), jnp.float32),
            shaped((shapes[0][0], width), jnp.float32),
            shaped((places, rows - extra, LANES), low_type),
        ],
        [],
        places * rows * LANES,
        4 * places * rows * LANES,
    )


def panel_places(block):
    panel = min(block, LANES)
    count = -(-block // panel)
    return panel, count, upper_blocks(count)


def upper_blocks(count):
    return [(row, col) for row in range(count) for col in range(row, count)]


def momentum_kernel(spans, block, turned, *refs):
    count = len(spans)
    sums, moms = refs[0], refs[1 : 1 + count]
    grad_out, mom_out = refs[1 + count : 1 + 2 * count], refs[1 + 2 * count : 1 + 3 * count]
    gram_out = refs[-1]
    kind = gram_out.dtype
    panel, tiles, places = panel_places(block)
    place = 0
    for index, (row_at, rows) in enumerate(spans):
        grad = sums[row_at : row_at + rows, :].astype(jnp.float32)
        new = decay_rate * moms[index][...] + grad
        grad_out[index][...] = grad
        mom_out[index][...] = new
        low = new.astype(low_type)
        for first in range(0, low.shape[0 if turned else 1], block):
            if turned:
                part = low[first : first + block, :]
                if tiles * panel > block:
                    blank = jnp.zeros((tiles * panel - block, part.shape[1]), low_type)
                    part = jnp.concatenate([part, blank], axis=0)
                gram = matmul_nt(part, part).astype(kind)
            else:
                part = low[:, first : first + block]
                gram = matmul_tn(part, part).astype(kind)
            for row, col in places:
                gram_out[place * panel : (place + 1) * panel, :] = gram[
                    row * panel : (row + 1) * panel, col * panel : (col + 1) * panel
                ]
                place += 1


def momenta(sums, moms, block, turned, name):
    axis = 0 if turned else 1
    blocks = sum(mom.shape[axis] // block for mom in moms)
    panel, tiles, places = panel_places(block)
    spans, row_at = [], 0
    for mom in moms:
        spans.append((row_at, mom.shape[0]))
        row_at += mom.shape[0]

    def body(*refs):
        momentum_kernel(spans, block, turned, *refs)

    shapes = [mom.shape for mom in moms]
    panels = (blocks * len(places) * panel, panel)
    results = whole_call(
        body,
        name,
        [],
        [sums, *moms],
        [shaped(shape, jnp.float32) for shape in shapes + shapes]
        + [shaped(panels, low_type)],
        [],
        2 * block * sum(shape[0] * shape[1] for shape in shapes),
        16 * sum(shape[0] * shape[1] for shape in shapes),
    )
    count = len(moms)
    return results[:count], results[count : 2 * count], results[-1]


def trace_of(gram):
    rows = lax.broadcasted_iota(jnp.int32, gram.shape, 0)
    cols = lax.broadcasted_iota(jnp.int32, gram.shape, 1)
    diagonal = jnp.where(rows == cols, gram, 0.0)
    return jnp.sum(jnp.sum(diagonal, axis=0, keepdims=True), axis=1, keepdims=True)


def polish_small(grams, blocks, turned):
    def apply(values, right, turn):
        values = values.astype(low_type)
        return matmul(right, values) if turn else matmul(values, right)

    factors = [1.0 / (jnp.sqrt(trace_of(gram)) + 1e-07) for gram in grams]
    iterates = [block * factor for block, factor in zip(blocks, factors)]
    grams = [gram * (factor * factor) for gram, factor in zip(grams, factors)]
    for step_index in range(NS_STEPS):
        lows = [gram.astype(low_type) for gram in grams]
        if step_index + 1 == NS_STEPS:
            first = [apply(*args) for args in zip(iterates, lows, turned)]
            second = [apply(*args) for args in zip(first, lows, turned)]
            return [
                coef_first * iterate + coef_second * one + coef_third * two
                for iterate, one, two in zip(iterates, first, second)
            ]
        squares = [matmul(low, low) for low in lows]
        changes = [
            (coef_second * gram + coef_third * square).astype(low_type)
            for gram, square in zip(grams, squares)
        ]
        moves = [apply(*args) for args in zip(iterates, changes, turned)]
        iterates = [coef_first * iterate + move for iterate, move in zip(iterates, moves)]
        once = [matmul(low, change) for low, change in zip(lows, changes)]
        twice = [matmul(one.astype(low_type), change) for one, change in zip(once, changes)]
        grams = [
            (coef_first * coef_first) * gram + (2.0 * coef_first) * one + two
            for gram, one, two in zip(grams, once, twice)
        ]


def gram_from_panels(panels, first, block):
    panel, tiles, places = panel_places(block)
    parts = {}
    for index, (row, col) in enumerate(places):
        start = (first + index) * panel
        parts[row, col] = panels[start : start + panel, :].astype(jnp.float32)
        if row != col:
            parts[col, row] = parts[row, col].T
    return jnp.concatenate(
        [
            jnp.concatenate([parts[row, col] for col in range(tiles)], axis=1)
            for row in range(tiles)
        ],
        axis=0,
    )


def updates(rank, panels, groups, name):
    groups = [(None, *group) for group in groups]
    counts = [len(group[1]) for group in groups]
    total = sum(counts)
    moms = [mom for group in groups for mom in group[1]]
    weights = [weight for group in groups for weight in group[2]]
    flags = [group[4] for group in groups for _ in group[1]]
    shapes = [mom.shape for mom in moms]

    places = panels.shape[0]
    chunks, starts = [], []
    for _, group_moms, _, block, turned in groups:
        panel, _, tile_places = panel_places(block)
        count = sum(mom.shape[0 if turned else 1] // block for mom in group_moms)
        starts.append(sum(chunks))
        chunks.append(count * len(tile_places) * panel // places)

    def body(rank, *refs):
        parts, refs, flats = refs[0], refs[1 : 1 + 3 * total], refs[1 + 3 * total :]
        mom_refs, weight_refs, targets = refs[:total], refs[total : 2 * total], refs[2 * total :]
        for flat, chunk, at in zip(flats, chunks, starts):
            for place in range(places):
                flat[place * chunk : (place + 1) * chunk, :] = parts[place, at : at + chunk, :]
        grams, blocks, turns, targets_at = [], [], [], []
        index = 0
        for group, source in zip(groups, flats):
            block, turned = group[3], group[4]
            panel, tiles, tile_places = panel_places(block)
            first = 0
            for weight in group[2]:
                rate = muon_rate * math.sqrt(weight.shape[1 if turned else 0] / block)
                for start in range(0, shapes[index][0 if turned else 1], block):
                    grams.append(gram_from_panels(source, first, block))
                    first += len(tile_places)
                    part = slice(start, start + block)
                    area = (part, slice(None)) if turned else (slice(None), part)
                    values = mom_refs[index][area]
                    if turned and tiles * panel > block:
                        blank = jnp.zeros((tiles * panel - block, values.shape[1]), jnp.float32)
                        values = jnp.concatenate([values, blank], axis=0)
                    blocks.append(values)
                    turns.append(turned)
                    targets_at.append((index, area, rate, block))
                index += 1
        for ortho, turn, (index, area, rate, block) in zip(
            polish_small(grams, blocks, turns), turns, targets_at
        ):
            if turn:
                ortho = ortho[:block, :]
            targets[index][area] = weight_refs[index][area].astype(jnp.float32) - rate * ortho

    def own_block(shape, turned):
        if turned:
            return pl.BlockSpec(shape, lambda index, rank: (0, rank[0]))
        return pl.BlockSpec(shape, lambda index, rank: (rank[0], 0))

    results = kernel_call(
        body,
        name,
        (1,),
        1,
        [fixed(panels.shape)]
        + [fixed(shape) for shape in shapes]
        + [own_block(shape, flag) for shape, flag in zip(shapes, flags)],
        [fixed(shape) for shape in shapes],
        [shaped(shape, jnp.float32) for shape in shapes],
        [pltpu.VMEM((places * chunk, panels.shape[2]), low_type) for chunk in chunks],
        14 * panels.size * groups[-1][3],
        sum(12 * shape[0] * shape[1] for shape in shapes),
    )(rank, panels, *map(in_hbm, moms), *map(in_hbm, weights))
    split, place = [], 0
    for count in counts:
        split.append(results[place : place + count])
        place += count
    return split


def panel_sums_kernel(parts, target):
    total = parts[0].astype(jnp.float32)
    for place in range(1, parts.shape[0]):
        total += parts[place].astype(jnp.float32)
    total = total.astype(low_type)
    for place in range(target.shape[0]):
        target[place, :, :] = total


def panel_sums(parts):
    return whole_call(
        panel_sums_kernel,
        "panel_sums",
        [],
        [parts],
        [shaped(parts.shape, low_type)],
        [],
        parts.size,
        4 * parts.size,
    )[0]


def polish(gram, gram_low, change_low, once_low, iterate, size):
    block = min(size, 512)
    count = size // block
    for step_index in range(NS_STEPS):
        last = step_index + 1 == NS_STEPS
        if last:
            first_term = matmul(iterate.astype(low_type), gram_low[...])
            second_term = matmul(first_term.astype(low_type), gram_low[...])
            return coef_first * iterate + coef_second * first_term + coef_third * second_term

        def make_change(index, carry):
            rows = block_at(index, block)
            square = matmul(gram_low[rows, :], gram_low[...])
            change_low[rows, :] = (coef_second * gram[rows, :] + coef_third * square).astype(
                low_type
            )
            return carry

        def make_once(index, carry):
            rows = block_at(index, block)
            once = matmul(gram_low[rows, :], change_low[...])
            once_low[rows, :] = once.astype(low_type)
            gram[rows, :] = (coef_first * coef_first) * gram[rows, :] + (2.0 * coef_first) * once
            return carry

        def make_gram(index, carry):
            rows = block_at(index, block)
            total = gram[rows, :] + matmul(once_low[rows, :], change_low[...])
            gram[rows, :] = total
            gram_low[rows, :] = total.astype(low_type)
            return carry

        lax.fori_loop(0, count, make_change, 0)
        iterate = coef_first * iterate + matmul(iterate.astype(low_type), change_low[...])
        lax.fori_loop(0, count, make_once, 0)
        lax.fori_loop(0, count, make_gram, 0)


def gram_parts_kernel(where, *refs):
    parts, gains, near_out, far_out, blocks = refs
    narrow = blocks.shape[1]
    chunk = blocks.shape[0] // (SIDE * CORES)
    extra = gains.shape[0] // (SIDE * CORES)
    places = parts.shape[0]
    tiles = parts.shape[1] // extra
    rows = jnp.concatenate(
        [
            jnp.concatenate(
                [parts[place, tile * extra : (tile + 1) * extra, :] for place in range(places)],
                axis=0,
            )
            for tile in range(tiles)
        ],
        axis=1,
    )
    wide = rows.shape[1] // narrow
    places = upper_blocks(wide - 2) + [(wide - 2, wide - 2), (wide - 1, wide - 1)]
    for index, (left, right) in enumerate(places):
        blocks[index * narrow : (index + 1) * narrow, :] = matmul_tn(
            rows[:, left * narrow : (left + 1) * narrow],
            rows[:, right * narrow : (right + 1) * narrow],
        ).astype(low_type)
    core = where[SIDE * CORES]
    for step in range(SIDE):
        near = CORES * step + core
        far = CORES * step + 1 - core
        for target, source, place in ((near_out, near, 0), (far_out, far, SIDE)):
            start = pl.multiple_of((where[source] - place) * (chunk + extra), extra)
            target[pl.ds(start, chunk), :] = blocks[block_at(source, chunk), :]
            start = pl.multiple_of(start + chunk, extra)
            target[pl.ds(start, extra), :] = gains[block_at(source, extra), :]


def gram_parts(where, parts, gains, narrow):
    places = parts.shape[0]
    extra = gains.shape[0] // (SIDE * CORES)
    width = parts.shape[1] // extra * LANES
    wide = width // narrow - 2
    total = (wide * (wide + 1) // 2 + 2) * narrow
    out_rows = (total + gains.shape[0]) // CORES
    return whole_call(
        gram_parts_kernel,
        "gram_parts",
        [where],
        [parts, gains],
        [shaped((out_rows, narrow), low_type)] * 2,
        [pltpu.VMEM((total, narrow), low_type)],
        2 * places * extra * total * narrow,
        4 * total * narrow,
    )


def shared_kernel(rows_all, owner, *refs):
    pieces = refs[: SIDE * CORES]
    own, *refs = refs[SIDE * CORES :]
    weights, targets, refs = refs[:3], refs[3:6], refs[6:]
    blocks, gram, gram_low, change_low, once_low = refs
    chunk, narrow = pieces[0].shape
    wide = gram.shape[0]
    for index, source in enumerate(pieces):
        blocks[block_at(owner[index], chunk), :] = source[...]
    places = upper_blocks(wide // narrow)
    trace = jnp.zeros((1, 1), jnp.float32)
    for index, (left, right) in enumerate(places):
        if left == right:
            trace += trace_of(blocks[index * narrow : (index + 1) * narrow, :].astype(jnp.float32))
    factor = 1.0 / (jnp.sqrt(trace) + 1e-07)
    for index, (left, right) in enumerate(places):
        block = blocks[index * narrow : (index + 1) * narrow, :].astype(jnp.float32)
        block = block * (factor * factor)
        rows = slice(left * narrow, (left + 1) * narrow)
        cols = slice(right * narrow, (right + 1) * narrow)
        gram[rows, cols] = block
        gram_low[rows, cols] = block.astype(low_type)
        if left != right:
            turned = block.T
            gram[cols, rows] = turned
            gram_low[cols, rows] = turned.astype(low_type)
    grams, starts = [], []
    for index in range(2):
        first = (len(places) + index) * narrow
        grams.append(blocks[first : first + narrow, :].astype(jnp.float32))
        starts.append(own[:, wide + index * narrow : wide + (index + 1) * narrow])
    for index, ortho in enumerate(polish_small(grams, starts, [False, False])):
        rate = muon_rate * math.sqrt(rows_all / narrow)
        targets[1 + index][...] = weights[1 + index][...].astype(jnp.float32) - rate * ortho
    ortho = polish(gram, gram_low, change_low, once_low, own[:, :wide] * factor, wide)
    rate = muon_rate * math.sqrt(rows_all / wide)
    targets[0][...] = weights[0][...].astype(jnp.float32) - rate * ortho


def shared_updates(owner, pieces, own, weights, rows_all):
    chunk, narrow = pieces[0].shape
    wide = weights[0].shape[1]

    def body(owner, *refs):
        shared_kernel(rows_all, owner, *refs)

    return whole_call(
        body,
        "shared_updates",
        [owner],
        [*map(in_hbm, pieces), in_hbm(own), *map(in_hbm, weights)],
        [shaped(weight.shape, jnp.float32) for weight in weights],
        [pltpu.VMEM((SIDE * CORES * chunk, narrow), low_type), pltpu.VMEM((wide, wide), jnp.float32)]
        + [pltpu.VMEM((wide, wide), low_type)] * 3,
        20 * wide * wide * wide,
        8 * wide * wide,
    )


def own_rows(weight, count, rank):
    share_rows = weight.shape[0] // count
    return lax.dynamic_slice_in_dim(weight, rank * share_rows, share_rows, 0)


def on_device(
    tokens_in,
    cotangent,
    seg_starts,
    gains,
    w_q_down,
    w_key,
    w_value,
    w_q_up,
    w_out,
    w_gate,
    w_up,
    w_down,
    mom_gains,
    mom_q_down,
    mom_key,
    mom_value,
    mom_q_up,
    mom_out,
    mom_gate,
    mom_up,
    mom_down,
):
    heads_count = lax.axis_size("heads")
    heads_rank = lax.axis_index("heads")
    dp_count = lax.axis_size("dp")
    dp_rank = lax.axis_index("dp")
    all_rank = lax.axis_index(("dp", "heads"))
    all_count = dp_count * heads_count
    local_rows = tokens_in.shape[0]
    row_len = local_rows * heads_count
    model_width = tokens_in.shape[1]
    latent_width = w_q_down.shape[1]
    head_dim = w_key.shape[1]
    local_q = w_q_up.shape[1]
    share_rows = model_width // all_count
    share_gains = gains.shape[0] // all_count
    starts = seg_starts[0]
    whole_index = jnp.arange(row_len, dtype=jnp.int32)
    own_index = heads_rank * local_rows + jnp.arange(local_rows, dtype=jnp.int32)
    own_core = heads_rank % CORES
    own_step = heads_rank // CORES
    ranks = jnp.arange(heads_count, dtype=jnp.int32)
    where = SIDE * ((ranks % CORES) ^ own_core) + (ranks // CORES - own_step) % SIDE
    where = jnp.concatenate([where, own_core[None]]).astype(jnp.int32)
    owner = CORES * ((ranks % SIDE + own_step) % SIDE) + ((ranks // SIDE) ^ own_core)
    owner = owner.astype(jnp.int32)
    dp_place = dp_rank[None].astype(jnp.int32)
    gain_one = gains[:model_width]
    gain_latent = gains[model_width : model_width + latent_width]
    gain_two = gains[model_width + latent_width :]

    inputs = tokens_in.astype(jnp.float32)
    scale_one = rms_scale(inputs)
    normed_one = (inputs * scale_one * gain_one).astype(low_type)
    latent_raw = matmul(normed_one, w_q_down)
    scale_latent = rms_scale(latent_raw)
    latent_normed = (latent_raw * scale_latent * gain_latent).astype(low_type)
    own_pos = segment_info(starts, own_index)[1]
    own_cos, own_sin = rotary_tables(own_pos, head_dim)
    key_local = rotate(matmul(normed_one, w_key), own_cos, own_sin).astype(low_type)
    value_local = matmul(normed_one, w_value).astype(low_type)
    packed = lax.all_gather(
        jnp.concatenate([latent_normed, key_local, value_local], axis=1), "heads", axis=0, tiled=True
    )
    grad_rows = lax.all_gather(after(cotangent, packed), "heads", axis=0, tiled=True)
    normed_parts = lax.all_to_all(
        normed_one.T.reshape(dp_count, heads_count, share_rows, local_rows)
        .transpose(1, 0, 2, 3)
        .reshape(model_width, local_rows),
        "heads",
        split_axis=0,
        concat_axis=0,
        tiled=True,
    )
    shared_rows = [own_rows(weight, all_count, all_rank) for weight in (w_q_down, w_key, w_value)]
    packed, normed_parts = lax.optimization_barrier((packed, normed_parts))
    row_ids, row_pos = segment_info(starts, whole_index)
    row_cos, row_sin = rotary_tables(row_pos, head_dim)
    query_rows, attended_near, attended_far, lse = attend(
        where, packed, w_q_up, head_dim, row_cos, row_sin, row_ids
    )
    attn_mixed = ring_sums(
        ring_operands(
            chip_sums(
                matmul_nt(attended_far, w_out).astype(low_type),
                matmul_nt(attended_near, w_out).astype(low_type),
            )
        )
    )
    attn_mixed, shared_rows = lax.optimization_barrier((attn_mixed, shared_rows))
    hidden_one = inputs + attn_mixed
    scale_two = rms_scale(hidden_one)
    normed_two = (hidden_one * scale_two * gain_two).astype(low_type)

    gate_turned, up_turned, down_turned = w_gate.T, w_up.T, w_down.T
    pieces_two = gather_heads(normed_two)
    gate_near, up_near, middle_near, back_near = ffn_half(
        owner, pieces_two[:SIDE], grad_rows, gate_turned, up_turned, down_turned, 0
    )
    gate_far, up_far, middle_far, back_far = ffn_half(
        owner, pieces_two[SIDE:], grad_rows, gate_turned, up_turned, down_turned, 1
    )
    chip_two = ring_operands(chip_sums(back_far, back_near))
    normed_two_back = ring_sums(chip_two)
    ffn_part = ffn_grads(
        owner,
        pieces_two,
        grad_rows,
        (after(gate_near, *chip_two), up_near, middle_near, gate_far, up_far, middle_far),
        dp_count,
    )
    ffn_sums = lax.psum_scatter(ffn_part, "dp", scatter_dimension=0, tiled=True)[0]
    hidden_part, gain_two_grad = norm_back(hidden_one, scale_two, gain_two, normed_two_back)
    hidden_back = cotangent.astype(jnp.float32) + hidden_part

    hidden_low = after(hidden_back.astype(low_type), ffn_part)
    mixed_far = matmul_tn(after(middle_far, hidden_low), down_turned).astype(low_type)
    mixed_near = matmul_tn(after(middle_near, hidden_low), down_turned).astype(low_type)
    pieces_hidden, mixed_far, mixed_near = gather_heads(hidden_low, (mixed_far, mixed_near))
    q_up_part, sums_near, sums_far = attend_back(
        where, pieces_hidden, query_rows, packed, w_out, w_q_up, lse, row_cos, row_sin, row_ids
    )
    chip_back = ring_operands(chip_sums(sums_far, sums_near))
    packed_sums = ring_sums(chip_back)
    head_parts = head_grads(
        pieces_hidden, (after(attended_near, *chip_back), attended_far), q_up_part, dp_count
    )
    packed_sums = after(packed_sums, head_parts)
    head_sums = lax.psum_scatter(head_parts, "dp", scatter_dimension=0, tiled=True)[0]
    latent_back = packed_sums[:, :latent_width]
    key_sum = packed_sums[:, latent_width : latent_width + head_dim]
    value_sum = packed_sums[:, latent_width + head_dim :]
    latent_raw_grad, gain_latent_grad = norm_back(
        latent_raw, scale_latent, gain_latent, latent_back
    )
    latent_raw_back = latent_raw_grad.astype(low_type)
    key_pre_back = rotate_back(key_sum, own_cos, own_sin).astype(low_type)
    values_low = value_sum.astype(low_type)

    back_low = jnp.concatenate([latent_raw_back, key_pre_back, values_low], axis=1)
    latent_out = matmul_nt(latent_raw_back, w_q_down)
    pieces_back, latent_out, *chip_mixed = gather_heads(
        back_low, (latent_out, *ring_operands(chip_sums(mixed_far, mixed_near)))
    )
    normed_one_back = (
        latent_out
        + matmul_nt(key_pre_back, w_key)
        + matmul_nt(values_low, w_value)
    )
    input_part, gain_one_grad = norm_back(inputs, scale_one, gain_one, normed_one_back)
    input_grad = hidden_back + input_part
    gains_part = jnp.concatenate([gain_one_grad, gain_latent_grad, gain_two_grad])
    gains_part = gains_part.reshape(dp_count, heads_count, share_gains).astype(low_type)
    gains_part = jnp.pad(
        gains_part, ((0, 0), (0, share_rows - heads_count), (0, LANES - share_gains))
    )

    shared_part = shared_parts_of(owner, normed_parts, pieces_back, gains_part)
    *shared_grads, gains_dp, shared_mom, next_parts = shared_momenta(
        exchange_dp(shared_part), (mom_q_down, mom_key, mom_value), share_rows
    )
    q_down_grad, key_w_grad, value_w_grad, q_down_mom, key_w_mom, value_w_mom = shared_grads

    gains_rows = jnp.pad(
        gains_dp[:heads_count, None, :share_gains].astype(low_type),
        ((0, 0), (0, share_rows - 1), (0, head_dim - share_gains)),
    ).reshape(heads_count * share_rows, head_dim)
    ffn_grad, ffn_mom, ffn_gram = momenta(
        after(ffn_sums, shared_mom),
        (mom_gate.T, mom_up.T, mom_down.T),
        FF_BLOCK,
        True,
        "ffn_momenta",
    )
    parts_mom, ffn_gram = lax.optimization_barrier((exchange_dp(next_parts), ffn_gram))
    gram_near, gram_far = gram_parts(where, parts_mom, gains_rows, head_dim)
    chip_gram = ring_operands(chip_sums(gram_far, gram_near))
    gram_sums = ring_sums(chip_gram)
    head_grad, head_mom, head_gram = momenta(
        head_sums, (mom_q_up, mom_out), head_dim, False, "head_momenta"
    )
    gram_chunk = gram_sums.shape[0] - share_rows
    panels = jnp.concatenate(
        [
            after(panel, gram_sums).reshape(dp_count, -1, panel.shape[1])
            for panel in (ffn_gram, head_gram)
        ],
        axis=1,
    )
    panels = exchange_dp(panels)
    pieces_gram = gather_heads(gram_sums[:gram_chunk].astype(low_type))
    panels = panel_sums(panels)
    pieces_gram, panels, chip_mixed = lax.optimization_barrier((pieces_gram, panels, chip_mixed))
    panels = exchange_dp(panels)
    layer_out = (hidden_one + ring_sums(chip_mixed)).astype(low_type)
    gains_grad = gram_sums[gram_chunk, :share_gains]
    gains_mom = decay_rate * mom_gains + gains_grad
    gains_new = own_rows(gains, all_count, all_rank) - gain_rate * gains_mom

    shared_new = shared_updates(
        owner,
        pieces_gram,
        shared_mom,
        shared_rows,
        model_width,
    )
    shared_new, panels, layer_out = lax.optimization_barrier((shared_new, panels, layer_out))
    ffn_new, (q_up_new, out_w_new) = updates(
        dp_place,
        panels,
        (
            (ffn_mom, (gate_turned, up_turned, down_turned), FF_BLOCK, True),
            (head_mom, (w_q_up, w_out), head_dim, False),
        ),
        "block_updates",
    )
    ffn_grad, ffn_mom, ffn_new = [
        [array.T for array in arrays] for arrays in (ffn_grad, ffn_mom, ffn_new)
    ]
    return (
        layer_out,
        input_grad,
        gains_grad,
        q_down_grad,
        key_w_grad,
        value_w_grad,
        *head_grad,
        *ffn_grad,
        gains_mom,
        q_down_mom,
        key_w_mom,
        value_w_mom,
        *head_mom,
        *ffn_mom,
        gains_new,
        *shared_new,
        q_up_new,
        out_w_new,
        *ffn_new,
    )


def solution(mesh):
    placed = (
        P(("dp", "heads"), None),
        P(("dp", "heads"), None),
        P("dp", None),
        P(),
        P(),
        P(),
        P(),
        P(None, "heads"),
        P(None, "heads"),
        P(None, "heads"),
        P(None, "heads"),
        P(None, "heads"),
        P(("dp", "heads")),
        P(("dp", "heads"), None),
        P(("dp", "heads"), None),
        P(("dp", "heads"), None),
        P("dp", "heads"),
        P("dp", "heads"),
        P("dp", "heads"),
        P("dp", "heads"),
        P("dp", "heads"),
    )
    return jax.shard_map(
        on_device,
        mesh=mesh,
        in_specs=placed,
        out_specs=(
            P(("dp", "heads"), None),
            P(("dp", "heads"), None),
            P(("dp", "heads")),
            P(("dp", "heads"), None),
            P(("dp", "heads"), None),
            P(("dp", "heads"), None),
            P("dp", "heads"),
            P("dp", "heads"),
            P("dp", "heads"),
            P("dp", "heads"),
            P("dp", "heads"),
            P(("dp", "heads")),
            P(("dp", "heads"), None),
            P(("dp", "heads"), None),
            P(("dp", "heads"), None),
            P("dp", "heads"),
            P("dp", "heads"),
            P("dp", "heads"),
            P("dp", "heads"),
            P("dp", "heads"),
            P(("dp", "heads")),
            P(("dp", "heads"), None),
            P(("dp", "heads"), None),
            P(("dp", "heads"), None),
            P("dp", "heads"),
            P("dp", "heads"),
            P("dp", "heads"),
            P("dp", "heads"),
            P("dp", "heads"),
        ),
        check_vma=False,
    )
```

```python
import math

import jax
import jax.numpy as jnp
from jax import lax
from jax.experimental import pallas as pl
from jax.experimental.pallas import tpu as pltpu
from jax.sharding import PartitionSpec as P

NS_STEPS = 3
FF_BLOCK = 352
SIDE = 4
CORES = 2
LANES = 128

coef_first = 3.4445
coef_second = -4.775
coef_third = 2.0315
muon_rate = 0.5
gain_rate = 0.004
decay_rate = 0.5
low_type = jnp.bfloat16


def matmul(left, right):
    return jnp.dot(left, right, preferred_element_type=jnp.float32)


def matmul_nt(left, right):
    return lax.dot_general(
        left, right, (((1,), (1,)), ((), ())), preferred_element_type=jnp.float32
    )


def matmul_tn(left, right):
    return lax.dot_general(
        left, right, (((0,), (0,)), ((), ())), preferred_element_type=jnp.float32
    )


def rms_scale(values):
    return lax.rsqrt(jnp.mean(values * values, axis=-1, keepdims=True) + 1e-05)


def norm_back(values, scale, gain, grad_out):
    weighted = gain * grad_out
    inner = jnp.mean(values * weighted, axis=-1, keepdims=True)
    grad_in = scale * weighted - values * (scale * scale * scale) * inner
    gain_grad = jnp.sum(grad_out * values * scale, axis=0)
    return (grad_in, gain_grad)


def segment_info(starts, token_index):
    started = starts[None, :] <= token_index[:, None]
    seg_ids = jnp.sum(started.astype(jnp.int32), axis=1)
    seg_begin = jnp.max(jnp.where(started, starts[None, :], 0), axis=1)
    return (seg_ids, token_index - seg_begin)


def rotary_tables(positions, head_dim):
    half_dim = head_dim // 2
    frequency = jnp.exp(
        jnp.arange(half_dim, dtype=jnp.float32) * (-2.0 * math.log(10000.0) / head_dim)
    )
    angles = positions.astype(jnp.float32)[:, None] * frequency[None, :]
    return (jnp.cos(angles), jnp.sin(angles))


def rotate(values, cosine, sine_part):
    half_dim = values.shape[-1] // 2
    first_half = values[..., :half_dim]
    second_half = values[..., half_dim:]
    return jnp.concatenate(
        [
            first_half * cosine - second_half * sine_part,
            second_half * cosine + first_half * sine_part,
        ],
        axis=-1,
    )


def rotate_back(grads, cosine, sine_part):
    return rotate(grads, cosine, -sine_part)


def shift_heads(values, step, core):
    pairs = [
        (CORES * place + side, CORES * ((place + step) % SIDE) + (side ^ core))
        for place in range(SIDE)
        for side in range(CORES)
    ]
    return lax.ppermute(values, "heads", pairs)


def shift_dp(values, step_z, step_x):
    pairs = [
        (SIDE * z + x, SIDE * ((z + step_z) % SIDE) + (x + step_x) % SIDE)
        for z in range(SIDE)
        for x in range(SIDE)
    ]
    return lax.ppermute(values, "dp", pairs)


def gather_heads(own, beside=()):
    ring = [own] + [shift_heads(own, -step, 0) for step in range(1, SIDE)]
    ring, beside = lax.optimization_barrier((ring, beside))
    pieces = ring + [shift_heads(piece, 0, 1) for piece in ring]
    return (pieces, *beside) if beside else pieces


def chip_sums(far_half, near_half):
    rows = near_half.shape[0] // SIDE
    total = near_half.astype(jnp.float32) + shift_heads(far_half, 0, 1).astype(jnp.float32)
    return total.astype(far_half.dtype).reshape(SIDE, rows, *near_half.shape[1:])


def ring_operands(chip):
    return lax.optimization_barrier([chip[step] for step in range(SIDE)])


def ring_sums(operands, first=None):
    if first is None:
        first = shift_heads(operands[1], 1, 0)
    total = operands[0].astype(jnp.float32) + first.astype(jnp.float32)
    for step in range(2, SIDE):
        total = total + shift_heads(operands[step], step, 0).astype(jnp.float32)
    return total


def pick(array, place, axis):
    return lax.dynamic_index_in_dim(array, place % SIDE, axis, keepdims=False)


def scatter_x(parts):
    place_x = lax.axis_index("dp") % SIDE
    grid = parts.reshape(SIDE, SIDE, *parts.shape[1:])
    total = pick(grid, place_x, 1).astype(jnp.float32)
    for step in range(1, SIDE):
        total = total + shift_dp(pick(grid, place_x + step, 1), 0, step).astype(jnp.float32)
    return total.astype(parts.dtype)


def scatter_z(column):
    place_z = lax.axis_index("dp") // SIDE
    total = pick(column, place_z, 0).astype(jnp.float32)
    for step in range(1, SIDE):
        total = total + shift_dp(pick(column, place_z + step, 0), step, 0).astype(jnp.float32)
    return total


def line_sum(part, axis):
    total = part.astype(jnp.float32)
    for step in range(1, SIDE):
        total = total + shift_dp(part, step * axis, step * (1 - axis)).astype(jnp.float32)
    return total.astype(part.dtype)


def exchange_dp(parts):
    return lax.all_to_all(parts, "dp", split_axis=0, concat_axis=0, tiled=True)


def after(values, *earlier):
    return lax.optimization_barrier((values, *earlier))[0]


vmem_mib = {
    "attend": 14,
    "attend_back": 20,
    "ffn_near": 26,
    "ffn_far": 26,
    "ffn_grads": 32,
    "head_grads": 16,
    "shared_updates": 24,
    "block_updates": 28,
}


def in_hbm(array):
    return pltpu.with_memory_space_constraint(array, pltpu.HBM)


def streamed_call(
    body, name, scalars, resident, arrays, out_shape, scratch, flops, moved, cuts, merged
):
    kinds, pieces = [], []
    for index, array in enumerate(arrays):
        rows = array.shape[0] if index not in cuts else cuts[index][0]
        if index < merged:
            rows = merged * array.shape[0] if index == 0 else 16
        kinds.append(pltpu.VMEM((rows, *array.shape[1:]), array.dtype))
        pieces.append(1 if index not in cuts else cuts[index][1])
    count, outs = len(arrays), len(out_shape)

    def wrapped(*refs):
        numbers, refs = refs[: len(scalars)], refs[len(scalars) :]
        still, refs = refs[: len(resident)], refs[len(resident) :]
        sources, refs = refs[:count], refs[count:]
        targets, refs = refs[:outs], refs[outs:]
        held, sems, rest = refs[:count], refs[count], refs[count + 1 :]
        copies, place = [], 0
        for index, source in enumerate(sources):
            parts = [(source, held[index])]
            if index < merged:
                rows = source.shape[0]
                parts = [(source, held[0].at[index * rows : (index + 1) * rows, :])]
            if index in cuts:
                parts = cuts[index][2](numbers, source, held[index])
            group = []
            for part_from, part_to in parts:
                group.append(pltpu.make_async_copy(part_from, part_to, sems.at[place]))
                place += 1
            copies.append(group)
        for group in copies:
            for copy in group:
                copy.start()
        done = [0]

        def ready(index):
            while done[0] <= index:
                for copy in copies[done[0]]:
                    copy.wait()
                done[0] += 1

        body(ready, numbers, still, held, targets, rest)
        ready(count - 1)

    return pl.pallas_call(
        wrapped,
        grid_spec=pltpu.PrefetchScalarGridSpec(
            num_scalar_prefetch=len(scalars),
            grid=(1,),
            in_specs=[pl.BlockSpec(memory_space=pltpu.VMEM)] * len(resident)
            + [pl.BlockSpec(memory_space=pltpu.HBM)] * count,
            out_specs=[pl.BlockSpec(memory_space=pltpu.VMEM)] * outs,
            scratch_shapes=[*kinds, pltpu.SemaphoreType.DMA((sum(pieces),)), *scratch],
        ),
        out_shape=out_shape,
        compiler_params=pltpu.CompilerParams(
            vmem_limit_bytes=vmem_mib.get(name, 12) * 1024 * 1024
        ),
        cost_estimate=pl.CostEstimate(flops=flops, bytes_accessed=moved, transcendentals=0),
        name=name,
    )(*scalars, *resident, *[in_hbm(array) for array in arrays])


def whole_call(body, name, scalars, arrays, out_shape, scratch, flops, moved):
    return pl.pallas_call(
        body,
        in_specs=[pl.BlockSpec(memory_space=pltpu.SMEM)] * len(scalars)
        + [pl.BlockSpec(memory_space=pltpu.VMEM)] * len(arrays),
        out_specs=jax.tree.map(lambda _: pl.BlockSpec(memory_space=pltpu.VMEM), out_shape),
        out_shape=out_shape,
        scratch_shapes=scratch,
        compiler_params=pltpu.CompilerParams(
            vmem_limit_bytes=vmem_mib.get(name, 12) * 1024 * 1024
        ),
        cost_estimate=pl.CostEstimate(flops=flops, bytes_accessed=moved, transcendentals=0),
        name=name,
    )(*scalars, *arrays)


def kernel_call(body, name, grid, prefetch, in_specs, out_specs, out_shape, scratch, flops, moved):
    return pl.pallas_call(
        body,
        grid_spec=pltpu.PrefetchScalarGridSpec(
            num_scalar_prefetch=prefetch,
            grid=grid,
            in_specs=in_specs,
            out_specs=out_specs,
            scratch_shapes=scratch,
        ),
        out_shape=out_shape,
        compiler_params=pltpu.CompilerParams(vmem_limit_bytes=vmem_mib.get(name, 12) * 1024 * 1024),
        cost_estimate=pl.CostEstimate(flops=flops, bytes_accessed=moved, transcendentals=0),
        name=name,
    )


def shaped(shape, kind):
    return jax.ShapeDtypeStruct(shape, kind)


def fixed(shape):
    return pl.BlockSpec(
        shape, lambda *grid: (0,) * len(shape), pipeline_mode=pl.Buffered(buffer_count=1)
    )


def visible(ids_q, ids_k, first_row, rows, cols):
    query_at = first_row + lax.broadcasted_iota(jnp.int32, (rows, cols), 0)
    key_at = lax.broadcasted_iota(jnp.int32, (rows, cols), 1)
    return (ids_q == ids_k) & (key_at <= query_at)


def block_at(index, piece):
    return pl.ds(pl.multiple_of(index * piece, piece), piece)


def store_by_distance(where, rows_ref, near_ref, far_ref, piece):
    core = where[SIDE * CORES]
    for step in range(SIDE):
        near = CORES * step + core
        far = CORES * step + 1 - core
        near_ref[block_at(where[near], piece), :] = rows_ref[block_at(near, piece), :].astype(
            near_ref.dtype
        )
        far_ref[block_at(where[far] - SIDE, piece), :] = rows_ref[block_at(far, piece), :].astype(
            far_ref.dtype
        )


def attend_kernel(
    where, packed, w_q_up, cosine, sine, ids_q, ids_k, query_out, near_out, far_out, lse_out, mixed
):
    row_len, packed_width = packed.shape
    latent_width, width = w_q_up.shape
    head_dim = (packed_width - latent_width) // 2
    piece = row_len // (SIDE * CORES)
    block = CORES * piece
    scale = head_dim ** (-0.5)
    key_cols = slice(latent_width, latent_width + head_dim)
    value_cols = slice(latent_width + head_dim, latent_width + 2 * head_dim)
    for head in range(width // head_dim):
        cols = slice(head * head_dim, (head + 1) * head_dim)
        for index in range(SIDE):
            first = index * block
            end = first + block
            rows = slice(first, end)
            query = matmul(packed[rows, :latent_width], w_q_up[:, cols])
            query = rotate(query, cosine[rows, :], sine[rows, :]).astype(low_type)
            query_out[rows, cols] = query
            scores = matmul_nt(query, packed[:end, key_cols]) * scale
            allowed = visible(ids_q[rows, :], ids_k[:, :end], first, block, end)
            scores = jnp.where(allowed, scores, -1e30)
            row_max = jnp.max(scores, axis=-1, keepdims=True)
            exponent = jnp.exp(scores - row_max)
            row_total = jnp.sum(exponent, axis=-1, keepdims=True)
            probs = (exponent * (1.0 / row_total)).astype(low_type)
            lse_out[head, rows, :] = row_max + jnp.log(row_total)
            mixed[rows, cols] = matmul(probs, packed[:end, value_cols]).astype(low_type)
    store_by_distance(where, mixed, near_out, far_out, piece)


def attend(where, packed, w_q_up, head_dim, cosine, sine, row_ids):
    row_len = packed.shape[0]
    latent_width, width = w_q_up.shape
    return whole_call(
        attend_kernel,
        "attend",
        [where],
        [packed, w_q_up, cosine, sine, row_ids[:, None], row_ids[None, :]],
        [
            shaped((row_len, width), low_type),
            shaped((row_len // 2, width), low_type),
            shaped((row_len // 2, width), low_type),
            shaped((width // head_dim, row_len, 1), jnp.float32),
        ],
        [pltpu.VMEM((row_len, width), low_type)],
        2 * width * row_len * (latent_width + 2 * row_len),
        8 * row_len * width,
    )


def attend_back_kernel(where, *refs):
    pieces = refs[: SIDE * CORES]
    query_in, packed, w_out, w_q_up, lse, cosine, sine, ids_q, ids_k = refs[
        SIDE * CORES : SIDE * CORES + 9
    ]
    weight_back, near_out, far_out, query_back, back_rows, totals = refs[SIDE * CORES + 9 :]
    row_len, packed_width = packed.shape
    latent_width, width = w_q_up.shape
    head_dim = (packed_width - latent_width) // 2
    piece = row_len // (SIDE * CORES)
    block = CORES * piece
    scale = head_dim ** (-0.5)
    key_cols = slice(latent_width, latent_width + head_dim)
    value_cols = slice(latent_width + head_dim, latent_width + 2 * head_dim)
    for index in range(0, SIDE * CORES, 2):
        pair = jnp.concatenate([pieces[index][...], pieces[index + 1][...]], axis=0)
        back_rows[index * piece : (index + 2) * piece, :] = matmul(pair, w_out[...]).astype(
            low_type
        )
    totals[:, latent_width:] = jnp.zeros((row_len, 2 * head_dim), jnp.float32)
    for head in range(width // head_dim):
        cols = slice(head * head_dim, (head + 1) * head_dim)
        for index in range(SIDE):
            first = index * block
            end = first + block
            rows = slice(first, end)
            query = query_in[rows, cols]
            back = jnp.concatenate(
                [
                    back_rows[block_at(where[CORES * index + side], piece), cols]
                    for side in range(CORES)
                ],
                axis=0,
            )
            keys = packed[:end, key_cols]
            scores = matmul_nt(query, keys) * scale
            allowed = visible(ids_q[rows, :], ids_k[:, :end], first, block, end)
            probs = jnp.where(allowed, jnp.exp(scores - lse[head, rows, :]), 0.0)
            probs_back = matmul_nt(back, packed[:end, value_cols])
            inner = jnp.sum(probs * probs_back, axis=-1, keepdims=True)
            score_back = (probs * (probs_back - inner)).astype(low_type)
            totals[:end, value_cols] += matmul_tn(probs.astype(low_type), back)
            totals[:end, key_cols] += matmul_tn(score_back, query) * scale
            query_grad = matmul(score_back, keys) * scale
            query_back[rows, cols] = rotate_back(
                query_grad, cosine[rows, :], sine[rows, :]
            ).astype(low_type)
    for index in range(SIDE):
        rows = slice(index * block, (index + 1) * block)
        totals[rows, :latent_width] = matmul_nt(query_back[rows, :], w_q_up[...])
    store_by_distance(where, totals, near_out, far_out, piece)
    weight_back[...] = matmul_tn(packed[:, :latent_width], query_back[...]).astype(low_type)


def attend_back(where, pieces, query_rows, packed, w_out, w_q_up, lse, cosine, sine, row_ids):
    row_len, packed_width = packed.shape
    latent_width, width = w_q_up.shape
    model_width = w_out.shape[0]
    return whole_call(
        attend_back_kernel,
        "attend_back",
        [where],
        [
            *pieces,
            query_rows,
            packed,
            w_out,
            w_q_up,
            lse,
            cosine,
            sine,
            row_ids[:, None],
            row_ids[None, :],
        ],
        [
            shaped((latent_width, width), low_type),
            shaped((row_len // 2, packed_width), low_type),
            shaped((row_len // 2, packed_width), low_type),
        ],
        [
            pltpu.VMEM((row_len, width), low_type),
            pltpu.VMEM((row_len, width), low_type),
            pltpu.VMEM((row_len, packed_width), jnp.float32),
        ],
        2 * width * row_len * (5 * row_len + model_width + 2 * latent_width),
        8 * row_len * width,
    )


def ffn_kernel(ready, numbers, still, held, targets, rest):
    w_gate = still[0]
    features, (w_up, grads, w_down) = held[0], held[SIDE:]
    gate_out, up_out, middle_out, features_back = targets
    gate_raw, up_raw = rest
    width = w_gate.shape[0]
    chunk = width // 2
    tile = features.shape[1] // 4

    def rows_of(part):
        return pl.ds(pl.multiple_of(part * chunk, chunk), chunk)

    def make_gate(part, carry):
        rows = rows_of(part)
        gate_raw[rows, :] = matmul_nt(w_gate[rows, :], features[...])
        return carry

    def make_up(part, carry):
        rows = rows_of(part)
        up_raw[rows, :] = matmul_nt(w_up[rows, :], features[...])
        return carry

    def make_backs(part, carry):
        rows = rows_of(part)
        middle_back = matmul_nt(w_down[rows, :], grads[...])
        gate, up = gate_raw[rows, :], up_raw[rows, :]
        sigmoid = jax.nn.sigmoid(gate)
        activated = gate * sigmoid
        middle_out[rows, :] = (activated * up).astype(low_type)
        gate_out[rows, :] = (
            middle_back * up * sigmoid * (1.0 + gate * (1.0 - sigmoid))
        ).astype(low_type)
        up_out[rows, :] = (middle_back * activated).astype(low_type)
        return carry

    def make_features(part, carry):
        area = pl.ds(pl.multiple_of(part * tile, tile), tile)
        features_back[:, area] = (
            matmul_tn(gate_out[...], w_gate[:, area]) + matmul_tn(up_out[...], w_up[:, area])
        ).astype(low_type)
        return carry

    ready(SIDE - 1)
    lax.fori_loop(0, 2, make_gate, 0)
    ready(SIDE)
    lax.fori_loop(0, 2, make_up, 0)
    ready(SIDE + 2)
    lax.fori_loop(0, 2, make_backs, 0)
    lax.fori_loop(0, 4, make_features, 0)


def ffn_half(owner, pieces, grads, w_gate, w_up, w_down, far):
    piece, model_width = pieces[0].shape
    width = w_gate.shape[0]
    rows = SIDE * piece

    def own_blocks(numbers, source, target):
        return [
            (
                source.at[block_at(numbers[0][SIDE * far + step], piece), :],
                target.at[step * piece : (step + 1) * piece, :],
            )
            for step in range(SIDE)
        ]

    return streamed_call(
        ffn_kernel,
        "ffn_far" if far else "ffn_near",
        [owner],
        [w_gate],
        [*pieces, w_up, grads, w_down],
        [shaped((width, rows), low_type)] * 3 + [shaped((rows, model_width), low_type)],
        [pltpu.VMEM((width, rows), jnp.float32)] * 2,
        10 * rows * model_width * width,
        6 * model_width * width + 6 * rows * model_width,
        {SIDE + 1: (rows, SIDE, own_blocks)},
        SIDE,
    )


def ffn_grads_kernel(owner, *refs):
    count = SIDE * CORES
    pieces, grads, halves, target = refs[:count], refs[count], refs[count + 1 : -1], refs[-1]
    width, half_rows = halves[0].shape
    piece = pieces[0].shape[0]
    places, share = target.shape[0], target.shape[2]
    block = places * share
    cols = pl.ds(pl.multiple_of(pl.program_id(0) * block, block), block)
    features = jnp.concatenate([source[:, cols] for source in pieces], axis=0)
    grads = jnp.concatenate(
        [grads[block_at(owner[index], piece), cols] for index in range(count)], axis=0
    )
    for index, right in enumerate((features, features, grads)):
        total = matmul(halves[index][...], right[:half_rows, :])
        total += matmul(halves[index + 3][...], right[half_rows:, :])
        total = total.astype(low_type)
        for place in range(places):
            target[place, index * width : (index + 1) * width, :] = total[
                :, place * share : (place + 1) * share
            ]


def ffn_grads(owner, pieces, grads, halves, dp_count):
    piece, model_width = pieces[0].shape
    row_len = grads.shape[0]
    width = halves[0].shape[0]
    block = model_width // 4
    share = model_width // dp_count
    return kernel_call(
        ffn_grads_kernel,
        "ffn_grads",
        (4,),
        1,
        [fixed((piece, model_width))] * len(pieces)
        + [fixed((row_len, model_width))]
        + [fixed(halves[0].shape)] * 6,
        pl.BlockSpec((block // share, 3 * width, share), lambda index, owner: (index, 0, 0)),
        pltpu.HBM((dp_count, 3 * width, share), low_type),
        [],
        6 * row_len * model_width * width,
        4 * row_len * model_width + 6 * model_width * width,
    )(owner, *map(in_hbm, pieces), in_hbm(grads), *halves)


def head_grads(pieces, halves, q_up_part, dp_count):
    piece, model_width = pieces[0].shape
    count = len(pieces)
    width = halves[0].shape[1]
    steps = 4
    block = model_width // steps
    each = dp_count // steps
    q_up_rows = q_up_part.shape[0] // dp_count
    out_rows = model_width // dp_count
    rows = piece * count

    def body(*refs):
        sources, (near, far, above, target) = refs[:count], refs[count:]
        cols = pl.ds(pl.multiple_of(pl.program_id(0) * block, block), block)
        left = jnp.concatenate([source[:, cols] for source in sources], axis=0)
        right = jnp.concatenate([near[...], far[...]], axis=0)
        total = matmul_tn(left, right)
        for index in range(each):
            first = index * q_up_rows
            target[index, :q_up_rows, :] = above[first : first + q_up_rows, :]
            first = index * out_rows
            target[index, q_up_rows:, :] = total[first : first + out_rows, :].astype(low_type)

    return kernel_call(
        body,
        "head_grads",
        (steps,),
        0,
        [fixed((piece, model_width))] * count
        + [fixed(source.shape) for source in halves]
        + [pl.BlockSpec((each * q_up_rows, width), lambda index: (index, 0))],
        pl.BlockSpec((each, q_up_rows + out_rows, width), lambda index: (index, 0, 0)),
        pltpu.HBM((dp_count, q_up_rows + out_rows, width), low_type),
        [],
        2 * rows * model_width * width,
        2 * rows * (model_width + width) + 4 * model_width * width,
    )(*map(in_hbm, pieces), *map(in_hbm, halves), q_up_part)


def shared_parts_kernel(count, owner, *refs):
    left, right, gains, target = refs[:count], refs[count:-2], refs[-2], refs[-1]
    left = jnp.concatenate([source[...] for source in left], axis=1)
    right = jnp.concatenate([source[...] for source in right], axis=0)
    total = matmul(left, right).astype(low_type)
    places, extra = gains.shape[0], gains.shape[1]
    rows = total.shape[0] // places
    tiles = total.shape[1] // LANES
    for place in range(places):
        for tile in range(tiles):
            target[place, tile * rows : (tile + 1) * rows, :] = total[
                place * rows : (place + 1) * rows, tile * LANES : (tile + 1) * LANES
            ]
        first = tiles * rows
        target[place, first : first + extra, :] = gains[place, :, :]


def shared_parts_of(owner, left, right, gains):
    count = len(right)
    width = left.shape[0] // count
    piece, cols = right[0].shape
    places = gains.shape[0]
    rows = width // places * (cols // LANES) + gains.shape[1]

    def body(owner, *refs):
        shared_parts_kernel(count, owner, *refs)

    return kernel_call(
        body,
        "shared_parts",
        (1,),
        1,
        [
            pl.BlockSpec((width, piece), lambda index, owner, place=place: (owner[place], 0))
            for place in range(count)
        ]
        + [fixed(source.shape) for source in right]
        + [fixed(gains.shape)],
        fixed((places, rows, LANES)),
        shaped((places, rows, LANES), low_type),
        [],
        2 * piece * count * width * cols,
        2 * piece * count * (width + cols) + 2 * width * cols,
    )(owner, *([in_hbm(left)] * count), *right, gains)


def shared_momenta_kernel(parts, q_down, key, value, *refs):
    grads, moms, gains_out, own, target = refs[:3], refs[3:6], refs[6], refs[7], refs[8]
    total = parts[0].astype(jnp.float32)
    for place in range(1, parts.shape[0]):
        total += parts[place].astype(jnp.float32)
    rows = q_down.shape[0]
    tiles = own.shape[1] // LANES
    first = 0
    for tile in range(tiles):
        own[:, tile * LANES : (tile + 1) * LANES] = total[tile * rows : (tile + 1) * rows, :]
    for old, grad_out, mom_out in zip((q_down, key, value), grads, moms):
        cols = slice(first, first + old.shape[1])
        grad = own[:, cols]
        new = decay_rate * old[...] + grad
        grad_out[...] = grad
        mom_out[...] = new
        own[:, cols] = new
        first += old.shape[1]
    head = tiles * rows
    extra = gains_out.shape[0]
    gains_out[...] = total[head : head + extra, :]
    for place in range(target.shape[0]):
        for tile in range(tiles):
            target[place, tile * rows : (tile + 1) * rows, :] = own[
                :, tile * LANES : (tile + 1) * LANES
            ].astype(low_type)


def shared_momenta(parts, old, extra):
    places, rows, _ = parts.shape
    shapes = [array.shape for array in old]
    width = sum(shape[1] for shape in shapes)
    return whole_call(
        shared_momenta_kernel,
        "shared_momenta",
        [],
        [parts, *old],
        [shaped(shape, jnp.float32) for shape in shapes + shapes]
        + [
            shaped((extra, LANES), jnp.float32),
            shaped((shapes[0][0], width), jnp.float32),
            shaped((places, rows - extra, LANES), low_type),
        ],
        [],
        places * rows * LANES,
        4 * places * rows * LANES,
    )


def panel_places(block):
    panel = min(block, LANES)
    count = -(-block // panel)
    return panel, count, upper_blocks(count)


def upper_blocks(count):
    return [(row, col) for row in range(count) for col in range(row, count)]


def momentum_kernel(spans, block, turned, *refs):
    count = len(spans)
    sums, moms = refs[0], refs[1 : 1 + count]
    grad_out, mom_out = refs[1 + count : 1 + 2 * count], refs[1 + 2 * count : 1 + 3 * count]
    gram_out = refs[-1]
    kind = gram_out.dtype
    panel, tiles, places = panel_places(block)
    place = 0
    for index, (row_at, rows) in enumerate(spans):
        grad = sums[row_at : row_at + rows, :].astype(jnp.float32)
        new = decay_rate * moms[index][...] + grad
        grad_out[index][...] = grad
        mom_out[index][...] = new
        low = new.astype(low_type)
        for first in range(0, low.shape[0 if turned else 1], block):
            if turned:
                part = low[first : first + block, :]
                if tiles * panel > block:
                    blank = jnp.zeros((tiles * panel - block, part.shape[1]), low_type)
                    part = jnp.concatenate([part, blank], axis=0)
                gram = matmul_nt(part, part).astype(kind)
            else:
                part = low[:, first : first + block]
                gram = matmul_tn(part, part).astype(kind)
            for row, col in places:
                gram_out[place * panel : (place + 1) * panel, :] = gram[
                    row * panel : (row + 1) * panel, col * panel : (col + 1) * panel
                ]
                place += 1


def momenta(sums, moms, block, turned, name):
    axis = 0 if turned else 1
    blocks = sum(mom.shape[axis] // block for mom in moms)
    panel, tiles, places = panel_places(block)
    spans, row_at = [], 0
    for mom in moms:
        spans.append((row_at, mom.shape[0]))
        row_at += mom.shape[0]

    def body(*refs):
        momentum_kernel(spans, block, turned, *refs)

    shapes = [mom.shape for mom in moms]
    panels = (blocks * len(places) * panel, panel)
    results = whole_call(
        body,
        name,
        [],
        [sums, *moms],
        [shaped(shape, jnp.float32) for shape in shapes + shapes]
        + [shaped(panels, low_type)],
        [],
        2 * block * sum(shape[0] * shape[1] for shape in shapes),
        16 * sum(shape[0] * shape[1] for shape in shapes),
    )
    count = len(moms)
    return results[:count], results[count : 2 * count], results[-1]


def trace_of(gram):
    rows = lax.broadcasted_iota(jnp.int32, gram.shape, 0)
    cols = lax.broadcasted_iota(jnp.int32, gram.shape, 1)
    diagonal = jnp.where(rows == cols, gram, 0.0)
    return jnp.sum(jnp.sum(diagonal, axis=0, keepdims=True), axis=1, keepdims=True)


def polish_small(grams, blocks, turned):
    def apply(values, right, turn):
        values = values.astype(low_type)
        return matmul(right, values) if turn else matmul(values, right)

    factors = [1.0 / (jnp.sqrt(trace_of(gram)) + 1e-07) for gram in grams]
    iterates = [block * factor for block, factor in zip(blocks, factors)]
    grams = [gram * (factor * factor) for gram, factor in zip(grams, factors)]
    for step_index in range(NS_STEPS):
        lows = [gram.astype(low_type) for gram in grams]
        if step_index + 1 == NS_STEPS:
            first = [apply(*args) for args in zip(iterates, lows, turned)]
            second = [apply(*args) for args in zip(first, lows, turned)]
            return [
                coef_first * iterate + coef_second * one + coef_third * two
                for iterate, one, two in zip(iterates, first, second)
            ]
        squares = [matmul(low, low) for low in lows]
        changes = [
            (coef_second * gram + coef_third * square).astype(low_type)
            for gram, square in zip(grams, squares)
        ]
        moves = [apply(*args) for args in zip(iterates, changes, turned)]
        iterates = [coef_first * iterate + move for iterate, move in zip(iterates, moves)]
        once = [matmul(low, change) for low, change in zip(lows, changes)]
        twice = [matmul(one.astype(low_type), change) for one, change in zip(once, changes)]
        grams = [
            (coef_first * coef_first) * gram + (2.0 * coef_first) * one + two
            for gram, one, two in zip(grams, once, twice)
        ]


def gram_from_panels(panels, first, block):
    panel, tiles, places = panel_places(block)
    parts = {}
    for index, (row, col) in enumerate(places):
        start = (first + index) * panel
        parts[row, col] = panels[start : start + panel, :].astype(jnp.float32)
        if row != col:
            parts[col, row] = parts[row, col].T
    return jnp.concatenate(
        [
            jnp.concatenate([parts[row, col] for col in range(tiles)], axis=1)
            for row in range(tiles)
        ],
        axis=0,
    )


def updates(rank, panels, groups, name):
    groups = [(None, *group) for group in groups]
    counts = [len(group[1]) for group in groups]
    total = sum(counts)
    moms = [mom for group in groups for mom in group[1]]
    weights = [weight for group in groups for weight in group[2]]
    flags = [group[4] for group in groups for _ in group[1]]
    shapes = [mom.shape for mom in moms]

    places = panels.shape[0]
    chunks, starts = [], []
    for _, group_moms, _, block, turned in groups:
        panel, _, tile_places = panel_places(block)
        count = sum(mom.shape[0 if turned else 1] // block for mom in group_moms)
        starts.append(sum(chunks))
        chunks.append(count * len(tile_places) * panel // places)

    def body(rank, *refs):
        parts, refs, flats = refs[0], refs[1 : 1 + 3 * total], refs[1 + 3 * total :]
        mom_refs, weight_refs, targets = refs[:total], refs[total : 2 * total], refs[2 * total :]
        for flat, chunk, at in zip(flats, chunks, starts):
            for place in range(places):
                flat[place * chunk : (place + 1) * chunk, :] = parts[place, at : at + chunk, :]
        grams, blocks, turns, targets_at = [], [], [], []
        index = 0
        for group, source in zip(groups, flats):
            block, turned = group[3], group[4]
            panel, tiles, tile_places = panel_places(block)
            first = 0
            for weight in group[2]:
                rate = muon_rate * math.sqrt(weight.shape[1 if turned else 0] / block)
                for start in range(0, shapes[index][0 if turned else 1], block):
                    grams.append(gram_from_panels(source, first, block))
                    first += len(tile_places)
                    part = slice(start, start + block)
                    area = (part, slice(None)) if turned else (slice(None), part)
                    values = mom_refs[index][area]
                    if turned and tiles * panel > block:
                        blank = jnp.zeros((tiles * panel - block, values.shape[1]), jnp.float32)
                        values = jnp.concatenate([values, blank], axis=0)
                    blocks.append(values)
                    turns.append(turned)
                    targets_at.append((index, area, rate, block))
                index += 1
        for ortho, turn, (index, area, rate, block) in zip(
            polish_small(grams, blocks, turns), turns, targets_at
        ):
            if turn:
                ortho = ortho[:block, :]
            targets[index][area] = weight_refs[index][area].astype(jnp.float32) - rate * ortho

    def own_block(shape, turned):
        if turned:
            return pl.BlockSpec(shape, lambda index, rank: (0, rank[0]))
        return pl.BlockSpec(shape, lambda index, rank: (rank[0], 0))

    results = kernel_call(
        body,
        name,
        (1,),
        1,
        [fixed(panels.shape)]
        + [fixed(shape) for shape in shapes]
        + [own_block(shape, flag) for shape, flag in zip(shapes, flags)],
        [fixed(shape) for shape in shapes],
        [shaped(shape, jnp.float32) for shape in shapes],
        [pltpu.VMEM((places * chunk, panels.shape[2]), low_type) for chunk in chunks],
        14 * panels.size * groups[-1][3],
        sum(12 * shape[0] * shape[1] for shape in shapes),
    )(rank, panels, *map(in_hbm, moms), *map(in_hbm, weights))
    split, place = [], 0
    for count in counts:
        split.append(results[place : place + count])
        place += count
    return split


def panel_sums_kernel(parts, target):
    total = parts[0].astype(jnp.float32)
    for place in range(1, parts.shape[0]):
        total += parts[place].astype(jnp.float32)
    total = total.astype(low_type)
    for place in range(target.shape[0]):
        target[place, :, :] = total


def panel_sums(parts):
    return whole_call(
        panel_sums_kernel,
        "panel_sums",
        [],
        [parts],
        [shaped(parts.shape, low_type)],
        [],
        parts.size,
        4 * parts.size,
    )[0]


def polish(gram, gram_low, change_low, once_low, iterate, size):
    block = min(size, 512)
    count = size // block
    for step_index in range(NS_STEPS):
        last = step_index + 1 == NS_STEPS
        if last:
            first_term = matmul(iterate.astype(low_type), gram_low[...])
            second_term = matmul(first_term.astype(low_type), gram_low[...])
            return coef_first * iterate + coef_second * first_term + coef_third * second_term

        def make_change(index, carry):
            rows = block_at(index, block)
            square = matmul(gram_low[rows, :], gram_low[...])
            change_low[rows, :] = (coef_second * gram[rows, :] + coef_third * square).astype(
                low_type
            )
            return carry

        def make_once(index, carry):
            rows = block_at(index, block)
            once = matmul(gram_low[rows, :], change_low[...])
            once_low[rows, :] = once.astype(low_type)
            gram[rows, :] = (coef_first * coef_first) * gram[rows, :] + (2.0 * coef_first) * once
            return carry

        def make_gram(index, carry):
            rows = block_at(index, block)
            total = gram[rows, :] + matmul(once_low[rows, :], change_low[...])
            gram[rows, :] = total
            gram_low[rows, :] = total.astype(low_type)
            return carry

        lax.fori_loop(0, count, make_change, 0)
        iterate = coef_first * iterate + matmul(iterate.astype(low_type), change_low[...])
        lax.fori_loop(0, count, make_once, 0)
        lax.fori_loop(0, count, make_gram, 0)


def gram_parts_kernel(where, *refs):
    parts, gains, near_out, far_out, blocks = refs
    narrow = blocks.shape[1]
    chunk = blocks.shape[0] // (SIDE * CORES)
    extra = gains.shape[0] // (SIDE * CORES)
    places = parts.shape[0]
    tiles = parts.shape[1] // extra
    rows = jnp.concatenate(
        [
            jnp.concatenate(
                [parts[place, tile * extra : (tile + 1) * extra, :] for place in range(places)],
                axis=0,
            )
            for tile in range(tiles)
        ],
        axis=1,
    )
    wide = rows.shape[1] // narrow
    places = upper_blocks(wide - 2) + [(wide - 2, wide - 2), (wide - 1, wide - 1)]
    for index, (left, right) in enumerate(places):
        blocks[index * narrow : (index + 1) * narrow, :] = matmul_tn(
            rows[:, left * narrow : (left + 1) * narrow],
            rows[:, right * narrow : (right + 1) * narrow],
        ).astype(low_type)
    core = where[SIDE * CORES]
    for step in range(SIDE):
        near = CORES * step + core
        far = CORES * step + 1 - core
        for target, source, place in ((near_out, near, 0), (far_out, far, SIDE)):
            start = pl.multiple_of((where[source] - place) * (chunk + extra), extra)
            target[pl.ds(start, chunk), :] = blocks[block_at(source, chunk), :]
            start = pl.multiple_of(start + chunk, extra)
            target[pl.ds(start, extra), :] = gains[block_at(source, extra), :]


def gram_parts(where, parts, gains, narrow):
    places = parts.shape[0]
    extra = gains.shape[0] // (SIDE * CORES)
    width = parts.shape[1] // extra * LANES
    wide = width // narrow - 2
    total = (wide * (wide + 1) // 2 + 2) * narrow
    out_rows = (total + gains.shape[0]) // CORES
    return whole_call(
        gram_parts_kernel,
        "gram_parts",
        [where],
        [parts, gains],
        [shaped((out_rows, narrow), low_type)] * 2,
        [pltpu.VMEM((total, narrow), low_type)],
        2 * places * extra * total * narrow,
        4 * total * narrow,
    )


def shared_kernel(rows_all, owner, *refs):
    pieces = refs[: SIDE * CORES]
    own, *refs = refs[SIDE * CORES :]
    weights, targets, refs = refs[:3], refs[3:6], refs[6:]
    blocks, gram, gram_low, change_low, once_low = refs
    chunk, narrow = pieces[0].shape
    wide = gram.shape[0]
    for index, source in enumerate(pieces):
        blocks[block_at(owner[index], chunk), :] = source[...]
    places = upper_blocks(wide // narrow)
    trace = jnp.zeros((1, 1), jnp.float32)
    for index, (left, right) in enumerate(places):
        if left == right:
            trace += trace_of(blocks[index * narrow : (index + 1) * narrow, :].astype(jnp.float32))
    factor = 1.0 / (jnp.sqrt(trace) + 1e-07)
    for index, (left, right) in enumerate(places):
        block = blocks[index * narrow : (index + 1) * narrow, :].astype(jnp.float32)
        block = block * (factor * factor)
        rows = slice(left * narrow, (left + 1) * narrow)
        cols = slice(right * narrow, (right + 1) * narrow)
        gram[rows, cols] = block
        gram_low[rows, cols] = block.astype(low_type)
        if left != right:
            turned = block.T
            gram[cols, rows] = turned
            gram_low[cols, rows] = turned.astype(low_type)
    grams, starts = [], []
    for index in range(2):
        first = (len(places) + index) * narrow
        grams.append(blocks[first : first + narrow, :].astype(jnp.float32))
        starts.append(own[:, wide + index * narrow : wide + (index + 1) * narrow])
    for index, ortho in enumerate(polish_small(grams, starts, [False, False])):
        rate = muon_rate * math.sqrt(rows_all / narrow)
        targets[1 + index][...] = weights[1 + index][...].astype(jnp.float32) - rate * ortho
    ortho = polish(gram, gram_low, change_low, once_low, own[:, :wide] * factor, wide)
    rate = muon_rate * math.sqrt(rows_all / wide)
    targets[0][...] = weights[0][...].astype(jnp.float32) - rate * ortho


def shared_updates(owner, pieces, own, weights, rows_all):
    chunk, narrow = pieces[0].shape
    wide = weights[0].shape[1]

    def body(owner, *refs):
        shared_kernel(rows_all, owner, *refs)

    return whole_call(
        body,
        "shared_updates",
        [owner],
        [*map(in_hbm, pieces), in_hbm(own), *map(in_hbm, weights)],
        [shaped(weight.shape, jnp.float32) for weight in weights],
        [pltpu.VMEM((SIDE * CORES * chunk, narrow), low_type), pltpu.VMEM((wide, wide), jnp.float32)]
        + [pltpu.VMEM((wide, wide), low_type)] * 3,
        20 * wide * wide * wide,
        8 * wide * wide,
    )


def own_rows(weight, count, rank):
    share_rows = weight.shape[0] // count
    return lax.dynamic_slice_in_dim(weight, rank * share_rows, share_rows, 0)


def on_device(
    tokens_in,
    cotangent,
    seg_starts,
    gains,
    w_q_down,
    w_key,
    w_value,
    w_q_up,
    w_out,
    w_gate,
    w_up,
    w_down,
    mom_gains,
    mom_q_down,
    mom_key,
    mom_value,
    mom_q_up,
    mom_out,
    mom_gate,
    mom_up,
    mom_down,
):
    heads_count = lax.axis_size("heads")
    heads_rank = lax.axis_index("heads")
    dp_count = lax.axis_size("dp")
    dp_rank = lax.axis_index("dp")
    all_rank = lax.axis_index(("dp", "heads"))
    all_count = dp_count * heads_count
    local_rows = tokens_in.shape[0]
    row_len = local_rows * heads_count
    model_width = tokens_in.shape[1]
    latent_width = w_q_down.shape[1]
    head_dim = w_key.shape[1]
    local_q = w_q_up.shape[1]
    share_rows = model_width // all_count
    share_gains = gains.shape[0] // all_count
    starts = seg_starts[0]
    whole_index = jnp.arange(row_len, dtype=jnp.int32)
    own_index = heads_rank * local_rows + jnp.arange(local_rows, dtype=jnp.int32)
    own_core = heads_rank % CORES
    own_step = heads_rank // CORES
    ranks = jnp.arange(heads_count, dtype=jnp.int32)
    where = SIDE * ((ranks % CORES) ^ own_core) + (ranks // CORES - own_step) % SIDE
    where = jnp.concatenate([where, own_core[None]]).astype(jnp.int32)
    owner = CORES * ((ranks % SIDE + own_step) % SIDE) + ((ranks // SIDE) ^ own_core)
    owner = owner.astype(jnp.int32)
    dp_place = dp_rank[None].astype(jnp.int32)
    gain_one = gains[:model_width]
    gain_latent = gains[model_width : model_width + latent_width]
    gain_two = gains[model_width + latent_width :]

    inputs = tokens_in.astype(jnp.float32)
    scale_one = rms_scale(inputs)
    normed_one = (inputs * scale_one * gain_one).astype(low_type)
    latent_raw = matmul(normed_one, w_q_down)
    scale_latent = rms_scale(latent_raw)
    latent_normed = (latent_raw * scale_latent * gain_latent).astype(low_type)
    own_pos = segment_info(starts, own_index)[1]
    own_cos, own_sin = rotary_tables(own_pos, head_dim)
    key_local = rotate(matmul(normed_one, w_key), own_cos, own_sin).astype(low_type)
    value_local = matmul(normed_one, w_value).astype(low_type)
    packed = lax.all_gather(
        jnp.concatenate([latent_normed, key_local, value_local], axis=1), "heads", axis=0, tiled=True
    )
    grad_rows = lax.all_gather(after(cotangent, packed), "heads", axis=0, tiled=True)
    normed_parts = lax.all_to_all(
        normed_one.T.reshape(dp_count, heads_count, share_rows, local_rows)
        .transpose(1, 0, 2, 3)
        .reshape(model_width, local_rows),
        "heads",
        split_axis=0,
        concat_axis=0,
        tiled=True,
    )
    shared_rows = [own_rows(weight, all_count, all_rank) for weight in (w_q_down, w_key, w_value)]
    packed, normed_parts = lax.optimization_barrier((packed, normed_parts))
    row_ids, row_pos = segment_info(starts, whole_index)
    row_cos, row_sin = rotary_tables(row_pos, head_dim)
    query_rows, attended_near, attended_far, lse = attend(
        where, packed, w_q_up, head_dim, row_cos, row_sin, row_ids
    )
    attn_mixed = ring_sums(
        ring_operands(
            chip_sums(
                matmul_nt(attended_far, w_out).astype(low_type),
                matmul_nt(attended_near, w_out).astype(low_type),
            )
        )
    )
    attn_mixed, shared_rows = lax.optimization_barrier((attn_mixed, shared_rows))
    hidden_one = inputs + attn_mixed
    scale_two = rms_scale(hidden_one)
    normed_two = (hidden_one * scale_two * gain_two).astype(low_type)

    gate_turned, up_turned, down_turned = w_gate.T, w_up.T, w_down.T
    pieces_two = gather_heads(normed_two)
    gate_near, up_near, middle_near, back_near = ffn_half(
        owner, pieces_two[:SIDE], grad_rows, gate_turned, up_turned, down_turned, 0
    )
    gate_far, up_far, middle_far, back_far = ffn_half(
        owner, pieces_two[SIDE:], grad_rows, gate_turned, up_turned, down_turned, 1
    )
    chip_two = ring_operands(chip_sums(back_far, back_near))
    normed_two_back = ring_sums(chip_two)
    ffn_part = ffn_grads(
        owner,
        pieces_two,
        grad_rows,
        (after(gate_near, *chip_two), up_near, middle_near, gate_far, up_far, middle_far),
        dp_count,
    )
    ffn_sums = lax.psum_scatter(ffn_part, "dp", scatter_dimension=0, tiled=True)[0]
    hidden_part, gain_two_grad = norm_back(hidden_one, scale_two, gain_two, normed_two_back)
    hidden_back = cotangent.astype(jnp.float32) + hidden_part

    hidden_low = after(hidden_back.astype(low_type), ffn_part)
    mixed_far = matmul_tn(after(middle_far, hidden_low), down_turned).astype(low_type)
    mixed_near = matmul_tn(after(middle_near, hidden_low), down_turned).astype(low_type)
    pieces_hidden, mixed_far, mixed_near = gather_heads(hidden_low, (mixed_far, mixed_near))
    q_up_part, sums_near, sums_far = attend_back(
        where, pieces_hidden, query_rows, packed, w_out, w_q_up, lse, row_cos, row_sin, row_ids
    )
    chip_back = ring_operands(chip_sums(sums_far, sums_near))
    packed_sums = ring_sums(chip_back)
    head_parts = head_grads(
        pieces_hidden, (after(attended_near, *chip_back), attended_far), q_up_part, dp_count
    )
    packed_sums = after(packed_sums, head_parts)
    head_sums = lax.psum_scatter(head_parts, "dp", scatter_dimension=0, tiled=True)[0]
    latent_back = packed_sums[:, :latent_width]
    key_sum = packed_sums[:, latent_width : latent_width + head_dim]
    value_sum = packed_sums[:, latent_width + head_dim :]
    latent_raw_grad, gain_latent_grad = norm_back(
        latent_raw, scale_latent, gain_latent, latent_back
    )
    latent_raw_back = latent_raw_grad.astype(low_type)
    key_pre_back = rotate_back(key_sum, own_cos, own_sin).astype(low_type)
    values_low = value_sum.astype(low_type)

    back_low = jnp.concatenate([latent_raw_back, key_pre_back, values_low], axis=1)
    latent_out = matmul_nt(latent_raw_back, w_q_down)
    pieces_back, latent_out, *chip_mixed = gather_heads(
        back_low, (latent_out, *ring_operands(chip_sums(mixed_far, mixed_near)))
    )
    normed_one_back = (
        latent_out
        + matmul_nt(key_pre_back, w_key)
        + matmul_nt(values_low, w_value)
    )
    input_part, gain_one_grad = norm_back(inputs, scale_one, gain_one, normed_one_back)
    input_grad = hidden_back + input_part
    gains_part = jnp.concatenate([gain_one_grad, gain_latent_grad, gain_two_grad])
    gains_part = gains_part.reshape(dp_count, heads_count, share_gains).astype(low_type)
    gains_part = jnp.pad(
        gains_part, ((0, 0), (0, share_rows - heads_count), (0, LANES - share_gains))
    )

    shared_part = shared_parts_of(owner, normed_parts, pieces_back, gains_part)
    *shared_grads, gains_dp, shared_mom, next_parts = shared_momenta(
        exchange_dp(shared_part), (mom_q_down, mom_key, mom_value), share_rows
    )
    q_down_grad, key_w_grad, value_w_grad, q_down_mom, key_w_mom, value_w_mom = shared_grads

    gains_rows = jnp.pad(
        gains_dp[:heads_count, None, :share_gains].astype(low_type),
        ((0, 0), (0, share_rows - 1), (0, head_dim - share_gains)),
    ).reshape(heads_count * share_rows, head_dim)
    ffn_grad, ffn_mom, ffn_gram = momenta(
        after(ffn_sums, shared_mom),
        (mom_gate.T, mom_up.T, mom_down.T),
        FF_BLOCK,
        True,
        "ffn_momenta",
    )
    parts_mom, ffn_gram = lax.optimization_barrier((exchange_dp(next_parts), ffn_gram))
    gram_near, gram_far = gram_parts(where, parts_mom, gains_rows, head_dim)
    chip_gram = ring_operands(chip_sums(gram_far, gram_near))
    first_gram = shift_heads(chip_gram[1], 1, 0)
    gram_sums = ring_sums(chip_gram, first_gram)
    head_grad, head_mom, head_gram = momenta(
        head_sums, (mom_q_up, mom_out), head_dim, False, "head_momenta"
    )
    gram_chunk = gram_sums.shape[0] - share_rows
    panels = jnp.concatenate(
        [
            after(panel, first_gram).reshape(dp_count, -1, panel.shape[1])
            for panel in (ffn_gram, head_gram)
        ],
        axis=1,
    )
    panels = exchange_dp(panels)
    pieces_gram = gather_heads(gram_sums[:gram_chunk].astype(low_type))
    panels = panel_sums(panels)
    pieces_gram, panels, chip_mixed = lax.optimization_barrier((pieces_gram, panels, chip_mixed))
    panels = exchange_dp(panels)
    layer_out = (hidden_one + ring_sums(chip_mixed)).astype(low_type)
    gains_grad = gram_sums[gram_chunk, :share_gains]
    gains_mom = decay_rate * mom_gains + gains_grad
    gains_new = own_rows(gains, all_count, all_rank) - gain_rate * gains_mom

    shared_new = shared_updates(
        owner,
        pieces_gram,
        shared_mom,
        shared_rows,
        model_width,
    )
    shared_new, panels, layer_out = lax.optimization_barrier((shared_new, panels, layer_out))
    ffn_new, (q_up_new, out_w_new) = updates(
        dp_place,
        panels,
        (
            (ffn_mom, (gate_turned, up_turned, down_turned), FF_BLOCK, True),
            (head_mom, (w_q_up, w_out), head_dim, False),
        ),
        "block_updates",
    )
    ffn_grad, ffn_mom, ffn_new = [
        [array.T for array in arrays] for arrays in (ffn_grad, ffn_mom, ffn_new)
    ]
    return (
        layer_out,
        input_grad,
        gains_grad,
        q_down_grad,
        key_w_grad,
        value_w_grad,
        *head_grad,
        *ffn_grad,
        gains_mom,
        q_down_mom,
        key_w_mom,
        value_w_mom,
        *head_mom,
        *ffn_mom,
        gains_new,
        *shared_new,
        q_up_new,
        out_w_new,
        *ffn_new,
    )


def solution(mesh):
    placed = (
        P(("dp", "heads"), None),
        P(("dp", "heads"), None),
        P("dp", None),
        P(),
        P(),
        P(),
        P(),
        P(None, "heads"),
        P(None, "heads"),
        P(None, "heads"),
        P(None, "heads"),
        P(None, "heads"),
        P(("dp", "heads")),
        P(("dp", "heads"), None),
        P(("dp", "heads"), None),
        P(("dp", "heads"), None),
        P("dp", "heads"),
        P("dp", "heads"),
        P("dp", "heads"),
        P("dp", "heads"),
        P("dp", "heads"),
    )
    return jax.shard_map(
        on_device,
        mesh=mesh,
        in_specs=placed,
        out_specs=(
            P(("dp", "heads"), None),
            P(("dp", "heads"), None),
            P(("dp", "heads")),
            P(("dp", "heads"), None),
            P(("dp", "heads"), None),
            P(("dp", "heads"), None),
            P("dp", "heads"),
            P("dp", "heads"),
            P("dp", "heads"),
            P("dp", "heads"),
            P("dp", "heads"),
            P(("dp", "heads")),
            P(("dp", "heads"), None),
            P(("dp", "heads"), None),
            P(("dp", "heads"), None),
            P("dp", "heads"),
            P("dp", "heads"),
            P("dp", "heads"),
            P("dp", "heads"),
            P("dp", "heads"),
            P(("dp", "heads")),
            P(("dp", "heads"), None),
            P(("dp", "heads"), None),
            P(("dp", "heads"), None),
            P("dp", "heads"),
            P("dp", "heads"),
            P("dp", "heads"),
            P("dp", "heads"),
            P("dp", "heads"),
        ),
        check_vma=False,
    )
```
